256 devices in a mesh: dp: 64 (over z, y, x_hi), tensor: 4 (over x_lo, core).
Axes of the slice: x: 4 (x_hi: 2, x_lo: 2; x = x_hi * 2 + x_lo), y: 4, z: 8, core: 2. Of those that a mesh axis runs over, the one named last changes fastest.
Arguments:
- target_queries: bfloat16 [32768, 8192], P('dp', 'tensor'), may hold values from -6 to 6
- target_keys: bfloat16 [32768, 1024], P('dp', 'tensor'), may hold values from -4 to 4
- target_values: bfloat16 [32768, 1024], P('dp', 'tensor'), may hold values from -6 to 6
- low_feature: bfloat16 [32768, 8192], P(('dp', 'tensor')), may hold values from -24 to 24
- mid_feature: bfloat16 [32768, 8192], P(('dp', 'tensor')), may hold values from -6 to 6
- merging_gain: float32 [3, 8192], replicated, may hold values from 0.25 to 4
- draft_gain: float32 [8192], replicated, may hold values from 0.5 to 2
- draft_weight: bfloat16 [8192, 512], P(('dp', 'tensor')), may hold values from -0.0625 to 0.0625
- cotangent: bfloat16 [3, 32768, 512], P(None, ('dp', 'tensor')), may hold values from -6 to 6
- doc_lengths: int32 [64, 8], P('dp'), may hold values from 1 to 256, 512 in all within a row
- step_offsets: int32 [3], replicated, may hold values from 1 to 32, as said below
Outputs:
- draft_values: bfloat16 [3, 32768, 512], P(None, ('dp', 'tensor'))
- weight_grad: float32 [8192, 512], P(('dp', 'tensor'))
- gain_grad: float32 [8192], P(('dp', 'tensor'))
The draws below stay inside these ranges and needn't reach their ends.
Inputs may be any that keep to these rules, and one draw needn't show every extreme that they name: `step_offsets`: each offset lies in 1 to 32; one of them equals 32.
All inputs are finite; a program needn't handle non-finite values.
Results may differ from the reference program's by a relative error of at most 0.0062.
Values may be sent and summed in bfloat16 or wider, within the bound.
No kernel may reach another device: no remote copies, remote signals or barrier semaphores. Data moves between devices by JAX's collectives and lax.ppermute only.
A program may use at most 128 MiB of HBM per device.

```python
import math
import jax
import jax.numpy as jnp
import numpy as np
from jax import lax

D = 8192
QH = 64
KVH = 8
HD = 128
DKV = 4
G = 512
NSEG = 8
STEPS = 3
OFFMAX = 32
MOSTSEG = 256
TOKENS = 32768
N_DP = 64


def shared_rows(key):
    base = jnp.clip(jax.random.normal(key, (TOKENS, KVH * HD), jnp.float32), -4.0, 4.0)
    return base


def draw_target_keys(key, part):
    base = shared_rows(key)
    result = base
    return result.astype(jnp.bfloat16)


def draw_target_queries(key, part):
    key = jax.random.fold_in(key, 12)
    own = jnp.clip(jax.random.normal(key, (TOKENS, QH * HD), jnp.float32), -6.0, 6.0)
    result = own
    return result.astype(jnp.bfloat16)


def draw_step_offsets(key, part):
    key = jax.random.fold_in(key, 13)
    picked = jax.random.randint(key, (STEPS,), 1, OFFMAX + 1)
    which = jax.random.randint(jax.random.fold_in(key, 5), (), 0, STEPS)
    return jnp.where(jnp.arange(STEPS, dtype=jnp.int32) == which, OFFMAX, picked).astype(jnp.int32)


def raised(drawn, stream_key, source, target, blocks, factor):
    def block_of(dim):
        return (jnp.arange(drawn.shape[dim]) // (drawn.shape[dim] // blocks)).reshape((-1,) + (1,) * (drawn.ndim - 1 - dim))

    first = jax.random.permutation(stream_key, blocks)[block_of(target)]
    far = (block_of(target) + blocks // 2) % blocks
    return jnp.where((block_of(source) == first) | (block_of(source) == far), factor * drawn, drawn)


def shard_levels(key, shape, pieces, low, high):
    gain = 1.0
    for axis_at, shards_of in pieces:
        heights = jax.random.uniform(jax.random.fold_in(jax.random.fold_in(key, 6), axis_at), (shards_of,), jnp.float32, low / len(pieces), high / len(pieces))
        gain = gain * jnp.repeat(jnp.exp(heights), shape[axis_at] // shards_of).reshape((-1,) + (1,) * (len(shape) - 1 - axis_at))
    return gain


def length_profile(amount, total, limit, slope):
    portions = [(1 << 20) // math.isqrt(rank ** slope) + 1 for rank in range(2, amount + 1)]
    rest, counts = total - limit - (amount - 1), [1] * (amount - 1)
    while rest > 0:
        free = [i for i in range(amount - 1) if counts[i] < limit]
        whole, left = sum([portions[i] for i in free]), rest
        for i in free:
            extra = min(limit - counts[i], max(1, left * portions[i] // whole), rest)
            counts[i] = counts[i] + extra
            rest = rest - extra
    return np.array([limit] + counts)


def uneven(own_key, count, total, limit, slope):
    if count == 2:
        one = jax.random.randint(own_key, (), max(1, total - limit), min(limit, total - 1) + 1)
        return jnp.stack([one, total - one])
    sizes = jnp.asarray(length_profile(count, total, limit, slope), jnp.int32)
    couples = (count - 1) // 2
    giver, taker = sizes[1:1 + 2 * couples:2], sizes[2:2 + 2 * couples:2]
    margin = jnp.minimum(giver - 1, limit - taker)
    passed = jax.random.randint(jax.random.fold_in(own_key, 1), (couples,), 0, 1 << 20) % (margin + 1)
    sizes = sizes.at[1:1 + 2 * couples:2].set(giver - passed).at[2:2 + 2 * couples:2].set(taker + passed)
    return sizes[jax.random.permutation(jax.random.fold_in(own_key, 2), count)]


def centred(rng, dims, deviation, bound, cuts=(), kind=jnp.bfloat16):
    entries = deviation * jax.random.normal(rng, dims, jnp.float32)
    if cuts:
        entries = entries * shard_levels(rng, dims, cuts, -0.22, 0.18)
    return jnp.clip(entries, -bound, bound).astype(kind)


def gaussian_with(key, shape, scale, most, cuts, heavy, kind=jnp.bfloat16):
    values = scale * jax.random.normal(key, shape, jnp.float32)
    if cuts:
        values = values * shard_levels(key, shape, cuts, -0.22, 0.18)
    return jnp.clip(raised(values, jax.random.fold_in(key, 3), *heavy), -most, most).astype(kind)


def setup_inputs(seed: int = 0) -> dict:
    splits = jax.random.split(jax.random.key(seed), 12)
    return {
        "target_queries": draw_target_queries(jax.random.fold_in(splits[11], 71), 0),
        "target_keys": draw_target_keys(jax.random.fold_in(splits[11], 71), 0),
        "target_values": centred(splits[2], (TOKENS, KVH * HD), 1.0, 6.0, ((0, 64), (1, 4))),
        "low_feature": gaussian_with(splits[3], (TOKENS, D), 1.0, 24.0, ((0, 256),), (0, 1, 256, 6.0)),
        "mid_feature": centred(splits[4], (TOKENS, D), 1.0, 6.0, ((0, 256),)),
        "merging_gain": jnp.clip(jnp.exp(jax.random.uniform(splits[5], (3, D), jnp.float32, math.log(0.25), math.log(4.0))), 0.25, 4.0),
        "draft_gain": jnp.clip(jnp.exp(jax.random.uniform(splits[6], (D,), jnp.float32, math.log(0.5), math.log(2.0))), 0.5, 2.0),
        "draft_weight": centred(splits[7], (D, DKV * HD), D ** -0.5, 0.0625, ((0, 256),)),
        "cotangent": centred(splits[8], (STEPS, TOKENS, DKV * HD), 1.0, 6.0, ((1, 256),)),
        "doc_lengths": jax.vmap(lambda own: uneven(own, NSEG, G, MOSTSEG, 1))(jax.random.split(splits[9], N_DP)).reshape((N_DP, NSEG)).astype(jnp.int32),
        "step_offsets": draw_step_offsets(jax.random.fold_in(splits[11], 71), 0),
    }


EPSILON = 1e-05

def row_norm(values):
    values = values.astype(jnp.float32)
    return values * lax.rsqrt(lax.optimization_barrier(jnp.mean(values * values, axis=-1, keepdims=True)) + EPSILON)

def pack_attend(operands):
    queries, keys_in, values_in, segment = operands
    group_size = QH // KVH
    query_four = queries.astype(jnp.float32).reshape(G, KVH, group_size, HD)
    key_three = keys_in.astype(jnp.float32).reshape(G, KVH, HD)
    value_three = values_in.astype(jnp.float32).reshape(G, KVH, HD)
    scores = jnp.einsum('qgrh,kgh->grqk', query_four, key_three) / jnp.sqrt(jnp.float32(HD))
    places = jnp.arange(G, dtype=jnp.int32)
    allowed = (places[None, :] <= places[:, None]) & (segment[None, :] == segment[:, None])
    scores = jnp.where(allowed, scores, -1e+30)
    highest = lax.optimization_barrier(jnp.max(scores, axis=-1, keepdims=True))
    expo = jnp.where(allowed, jnp.exp(scores - highest), 0.0)
    weights = (expo / lax.optimization_barrier(jnp.sum(expo, axis=-1, keepdims=True))).astype(jnp.bfloat16)
    mixed = jnp.einsum('grqk,kgh->qgrh', weights.astype(jnp.float32), value_three)
    return mixed.astype(jnp.bfloat16).reshape(G, QH * HD)

def reference(target_queries, target_keys, target_values, low_feature, mid_feature, merging_gain, draft_gain, draft_weight, cotangent, doc_lengths, step_offsets):
    packs = TOKENS // G
    ends = jnp.cumsum(doc_lengths, axis=1).astype(jnp.int32)
    places = jnp.arange(G, dtype=jnp.int32)
    segment = lax.optimization_barrier(jnp.sum((places[None, :, None] >= ends[:, None, :]).astype(jnp.int32), axis=-1))
    high = lax.map(pack_attend, (target_queries.reshape(packs, G, QH * HD), target_keys.reshape(packs, G, KVH * HD), target_values.reshape(packs, G, KVH * HD), segment))
    high = high.reshape(TOKENS, D)
    merged = (row_norm(low_feature) * merging_gain[0] + row_norm(mid_feature) * merging_gain[1] + row_norm(high) * merging_gain[2]).astype(jnp.bfloat16)
    flat_segment = segment.reshape(TOKENS)
    flat_place = jnp.tile(places, packs)
    outputs = []
    weight_grad = jnp.zeros((D, DKV * HD), jnp.float32)
    gain_grad = jnp.zeros((D,), jnp.float32)
    for step_index in range(STEPS):
        offset = step_offsets[step_index]
        source_segment = jnp.roll(flat_segment, offset)
        valid = (flat_place >= offset) & (source_segment == flat_segment)
        shifted = jnp.where(valid[:, None], jnp.roll(merged, offset, axis=0), jnp.zeros((), jnp.bfloat16))
        normed = row_norm(shifted)
        hidden = (normed * draft_gain).astype(jnp.bfloat16)
        outputs.append(jnp.dot(hidden, draft_weight, preferred_element_type=jnp.float32).astype(jnp.bfloat16))
        back = jnp.dot(cotangent[step_index], draft_weight.T, preferred_element_type=jnp.float32)
        gain_grad = gain_grad + lax.optimization_barrier(jnp.sum(back * normed, axis=0))
        weight_grad = weight_grad + jnp.dot(hidden.T, cotangent[step_index], preferred_element_type=jnp.float32)
    return (jnp.stack(outputs), weight_grad, gain_grad)
```

```python
import functools
import math

import jax
import jax.numpy as jnp
from jax import lax
from jax.experimental import pallas as pl
from jax.experimental.pallas import tpu as pltpu
from jax.sharding import PartitionSpec as P

HD = 128
STEPS = 3
OFFMAX = 32
EPSILON = 1e-05
VMEM_LIMIT = 48 * 1024 * 1024

VMEM = pl.BlockSpec(memory_space=pltpu.VMEM)
SMEM = pl.BlockSpec(memory_space=pltpu.SMEM)
F32 = jnp.float32
BF16 = jnp.bfloat16


def segment_start(places, lengths_ref):
    end = jnp.int32(0)
    start = jnp.zeros_like(places)
    for s in range(lengths_ref.shape[1]):
        end = end + lengths_ref[0, s]
        start = jnp.where(places >= end, end, start)
    return start


def column(row):
    n = row.shape[-1]
    eye = lax.broadcasted_iota(jnp.int32, (n, n), 0) == lax.broadcasted_iota(jnp.int32, (n, n), 1)
    return jnp.sum(jnp.where(eye, row, 0.0), axis=1, keepdims=True)


def lane_sums(values):
    return lax.dot_general(
        jnp.ones((8, values.shape[1]), F32), values, (((1,), (1,)), ((), ())),
        precision=lax.Precision.HIGHEST, preferred_element_type=F32)


def folded_square_sum(values):
    total = None
    for c in range(0, values.shape[1], 128):
        piece = values[:, c:c + 128]
        total = piece * piece if total is None else total + piece * piece
    return total


def features_kernel(tn, place_ref, low_ref, mid_ref, gain_ref, *outs):
    j = place_ref[0]
    width = low_ref.shape[1]
    piece = width // tn
    step = 1024

    def rms_scale(ref):
        total = None
        for c in range(0, width, step):
            part = folded_square_sum(ref[:, c:c + step].astype(F32))
            total = part if total is None else total + part
        return lax.rsqrt(jnp.sum(total, axis=1, keepdims=True) / width + EPSILON)

    low_scale = rms_scale(low_ref)
    mid_scale = rms_scale(mid_ref)
    for s, out in enumerate(outs):
        first = pl.multiple_of((j ^ s) * piece, piece)
        for c in range(0, piece, 512):
            at = pl.ds(first + c, 512)
            value = (low_ref[:, at].astype(F32) * low_scale * gain_ref[0:1, at]
                     + mid_ref[:, at].astype(F32) * mid_scale * gain_ref[1:2, at])
            out[:, c:c + 512] = value.astype(BF16)


def features(place, low, mid, gain, tn):
    rows, width = low.shape
    block = 32
    piece = width // tn
    return pl.pallas_call(
        functools.partial(features_kernel, tn),
        grid=(rows // block,),
        in_specs=[
            SMEM,
            pl.BlockSpec((block, width), lambda b: (b, 0)),
            pl.BlockSpec((block, width), lambda b: (b, 0)),
            pl.BlockSpec(gain.shape, lambda b: (0, 0)),
        ],
        out_specs=[pl.BlockSpec((block, piece), lambda b: (b, 0))] * tn,
        out_shape=[jax.ShapeDtypeStruct((rows, piece), BF16)] * tn,
        compiler_params=pltpu.CompilerParams(vmem_limit_bytes=VMEM_LIMIT),
        cost_estimate=pl.CostEstimate(flops=10 * rows * width, bytes_accessed=6 * rows * width, transcendentals=0),
        name="features",
    )(place, low, mid, gain)


def attend_kernel(window, lengths_ref, query_ref, key_ref, value_ref, high_ref, square_ref):
    block = query_ref.shape[0]
    pack = key_ref.shape[0]
    b = pl.program_id(0)
    first = pl.multiple_of(jnp.clip(b * block - (window - block), 0, pack - window), block)
    query_places = b * block + lax.broadcasted_iota(jnp.int32, (block, window), 0)
    key_places = first + lax.broadcasted_iota(jnp.int32, (block, window), 1)
    allowed = (key_places <= query_places) & (key_places >= segment_start(query_places, lengths_ref))
    bias = jnp.where(allowed, 0.0, -1e30).astype(F32)
    group = (query_ref.shape[1] // HD) // (key_ref.shape[1] // HD)
    squares = jnp.zeros((block, HD), F32)
    ones = jnp.ones((window, HD), BF16)
    scale = math.log2(math.e) / math.sqrt(HD)
    for g in range(key_ref.shape[1] // HD):
        key = key_ref[pl.ds(first, window), g * HD:(g + 1) * HD]
        value = jnp.concatenate([value_ref[pl.ds(first, window), g * HD:(g + 1) * HD], ones], axis=1)
        for r in range(group):
            at = slice((g * group + r) * HD, (g * group + r + 1) * HD)
            scores = lax.dot_general(query_ref[:, at], key, (((1,), (1,)), ((), ())), preferred_element_type=F32)
            scores = scores * scale + bias
            highest = jnp.max(scores, axis=1, keepdims=True)
            expo = jnp.exp2(scores - highest).astype(BF16)
            mixed = jnp.dot(expo, value, preferred_element_type=F32)
            out = (mixed[:, :HD] / mixed[:, HD:]).astype(BF16)
            high_ref[:, at] = out
            out = out.astype(F32)
            squares = squares + out * out
    square_ref[0] = lane_sums(squares)


def attend(lengths, queries, keys, values):
    pack, width = queries.shape
    block = 128
    window = min(pack, 256 + block)
    return pl.pallas_call(
        functools.partial(attend_kernel, window),
        grid=(pack // block,),
        in_specs=[
            SMEM,
            pl.BlockSpec((block, width), lambda b: (b, 0)),
            pl.BlockSpec(keys.shape, lambda b: (0, 0)),
            pl.BlockSpec(values.shape, lambda b: (0, 0)),
        ],
        out_specs=[
            pl.BlockSpec((block, width), lambda b: (b, 0)),
            pl.BlockSpec((1, 8, block), lambda b: (b, 0, 0)),
        ],
        out_shape=[
            jax.ShapeDtypeStruct((pack, width), BF16),
            jax.ShapeDtypeStruct((pack // block, 8, block), F32),
        ],
        compiler_params=pltpu.CompilerParams(vmem_limit_bytes=VMEM_LIMIT),
        cost_estimate=pl.CostEstimate(
            flops=4 * pack * window * width, bytes_accessed=4 * pack * width,
            transcendentals=pack * window * width // HD),
        name="attend",
    )(lengths, queries, keys, values)


def chosen(place_ref, lengths_ref, offset, rows, lead):
    target = place_ref[0] * rows + lax.broadcasted_iota(jnp.int32, (rows, rows + lead), 0)
    source = place_ref[0] * rows - lead + lax.broadcasted_iota(jnp.int32, (rows, rows + lead), 1)
    hit = (source == target - offset) & (source >= segment_start(target, lengths_ref))
    return jnp.where(hit, 1.0, 0.0).astype(BF16)


def fold_kernel(place_ref, lengths_ref, offsets_ref, cotangent_ref, out_ref):
    steps, rows, width = cotangent_ref.shape
    total = None
    for s in range(steps):
        pick = chosen(place_ref, lengths_ref, offsets_ref[s], rows, OFFMAX)
        part = lax.dot_general(pick, cotangent_ref[s], (((0,), (0,)), ((), ())), preferred_element_type=F32)
        total = part if total is None else total + part
    out_ref[...] = total.astype(BF16)


def fold(place, lengths, offsets, cotangent):
    steps, rows, width = cotangent.shape
    return pl.pallas_call(
        fold_kernel,
        in_specs=[SMEM, SMEM, SMEM, VMEM],
        out_specs=VMEM,
        out_shape=jax.ShapeDtypeStruct((rows + OFFMAX, width), BF16),
        compiler_params=pltpu.CompilerParams(vmem_limit_bytes=VMEM_LIMIT),
        cost_estimate=pl.CostEstimate(flops=2 * steps * rows * 160 * width, bytes_accessed=2 * steps * rows * width, transcendentals=0),
        name="fold",
    )(place, lengths, offsets, cotangent)


def merge_kernel(width, place_ref, square_ref, gain_ref, high_ref, *refs):
    tn = len(refs) - 2
    parts, out_ref, out_square_ref = refs[:tn], refs[tn], refs[tn + 1]
    j = place_ref[0]
    rows = parts[0].shape[0]
    for s in range(tn):
        b = j ^ s
        at = pl.ds(pl.multiple_of(b * rows, rows), rows)
        scale = lax.rsqrt(column(square_ref[pl.ds(b, 1), :]) / width + EPSILON)
        total = jnp.zeros((rows, 128), F32)
        for c in range(0, high_ref.shape[1], 128):
            cols = slice(c, c + 128)
            merged = (parts[s][:, cols].astype(F32)
                      + high_ref[at, cols].astype(F32) * scale * gain_ref[:, cols]).astype(BF16)
            out_ref[at, cols] = merged
            merged = merged.astype(F32)
            total = total + merged * merged
        out_square_ref[b] = lane_sums(total)


def merge(place, squares, gain, high, parts, width):
    pack, piece = high.shape
    return pl.pallas_call(
        functools.partial(merge_kernel, width),
        in_specs=[SMEM, VMEM, VMEM, VMEM] + [VMEM] * len(parts),
        out_specs=[VMEM, VMEM],
        out_shape=[
            jax.ShapeDtypeStruct((pack, piece), BF16),
            jax.ShapeDtypeStruct((len(parts), 8, pack // len(parts)), F32),
        ],
        compiler_params=pltpu.CompilerParams(vmem_limit_bytes=VMEM_LIMIT),
        cost_estimate=pl.CostEstimate(flops=8 * pack * piece, bytes_accessed=6 * pack * piece, transcendentals=0),
        name="merge",
    )(place, squares, gain, high, *parts)


def project(place, squares, gain, merged, weight, folds, width):
    pack, piece = merged.shape
    tn = len(folds)
    rows = pack // tn
    vw = weight.shape[1]

    def kernel(place_ref, square_ref, gain_ref, merged_ref, weight_ref, *refs):
        fold_refs = refs[:tn]
        grad_ref = refs[tn]
        value_refs = refs[tn + 1:2 * tn + 1]
        hidden_ref, fold_ref, total_ref = refs[2 * tn + 1:]
        j = place_ref[0]
        for b in range(tn):
            at = slice(b * rows, (b + 1) * rows)
            scale = lax.rsqrt(column(square_ref[b:b + 1, :]) / width + EPSILON)
            for c in range(0, piece, 128):
                cols = slice(c, c + 128)
                hidden_ref[at, cols] = (merged_ref[at, cols].astype(F32) * scale * gain_ref[:, cols]).astype(BF16)
        fold_ref[...] = jnp.zeros_like(fold_ref)
        for s in range(tn):
            at = pl.ds(pl.multiple_of((j ^ s) * rows, rows), rows + OFFMAX)
            fold_ref[at, :] = fold_ref[at, :] + fold_refs[s][...].astype(F32)
        folded = fold_ref[OFFMAX:, :].astype(BF16)
        total_ref[0:OFFMAX, :] = jnp.zeros((OFFMAX, vw), F32)
        for c in range(0, piece, 256):
            grad_ref[c:c + 256, :] = lax.dot_general(
                hidden_ref[:, c:c + 256], folded, (((0,), (0,)), ((), ())), preferred_element_type=F32)
        for c in range(0, pack, 256):
            total_ref[OFFMAX + c:OFFMAX + c + 256, :] = jnp.dot(
                hidden_ref[c:c + 256, :], weight_ref[...], preferred_element_type=F32)
        for s in range(tn):
            at = pl.ds(pl.multiple_of((j ^ s) * rows, rows), rows + OFFMAX)
            value_refs[s][...] = total_ref[at, :].astype(value_refs[s].dtype)

    return pl.pallas_call(
        kernel,
        in_specs=[SMEM] + [VMEM] * (4 + tn),
        out_specs=[VMEM] * (1 + tn),
        out_shape=[jax.ShapeDtypeStruct((piece, vw), F32)]
        + [jax.ShapeDtypeStruct((rows + OFFMAX, vw), F32 if s == 0 else BF16) for s in range(tn)],
        scratch_shapes=[
            pltpu.VMEM((pack, piece), BF16),
            pltpu.VMEM((pack + OFFMAX, vw), F32),
            pltpu.VMEM((pack + OFFMAX, vw), F32),
        ],
        compiler_params=pltpu.CompilerParams(vmem_limit_bytes=VMEM_LIMIT),
        cost_estimate=pl.CostEstimate(flops=4 * pack * piece * vw, bytes_accessed=12 * pack * piece, transcendentals=0),
        name="project",
    )(place, squares, gain, merged, weight, *folds)


def spread(place, lengths, offsets, parts):
    rows, vw = parts[0].shape[0] - OFFMAX, parts[0].shape[1]

    def kernel(place_ref, lengths_ref, offsets_ref, *refs):
        parts_refs, out_ref = refs[:-1], refs[-1]
        total = None
        for ref in parts_refs:
            part = ref[...].astype(F32)
            total = part if total is None else total + part
        total = total.astype(BF16)
        for s in range(STEPS):
            pick = chosen(place_ref, lengths_ref, offsets_ref[s], rows, OFFMAX)
            out_ref[s] = jnp.dot(pick, total, preferred_element_type=F32).astype(BF16)

    return pl.pallas_call(
        kernel,
        in_specs=[SMEM] * 3 + [VMEM] * len(parts),
        out_specs=VMEM,
        out_shape=jax.ShapeDtypeStruct((STEPS, rows, vw), BF16),
        compiler_params=pltpu.CompilerParams(vmem_limit_bytes=VMEM_LIMIT),
        cost_estimate=pl.CostEstimate(flops=2 * STEPS * rows * 160 * vw, bytes_accessed=8 * STEPS * rows * vw, transcendentals=0),
        name="spread",
    )(place, lengths, offsets, *parts)


def body(
    target_queries,
    target_keys,
    target_values,
    low_feature,
    mid_feature,
    merging_gain,
    draft_gain,
    draft_weight,
    cotangent,
    doc_lengths,
    step_offsets,
):
    n = lax.axis_size("dp")
    tn = lax.axis_size("tensor")
    j = lax.axis_index("tensor")
    flat = lax.axis_index("dp") * tn + j
    place = j.reshape(1).astype(jnp.int32)
    width = low_feature.shape[1]
    piece = width // tn
    pack = target_queries.shape[0]
    both = ("dp", "tensor")

    def swapped(values, s):
        return lax.ppermute(values, "tensor", [(a, a ^ s) for a in range(tn)])

    moved = lax.ppermute(draft_weight, both, [(r, (r % n) * tn + r // n) for r in range(n * tn)])
    weight = lax.all_gather(moved, "dp", axis=0, tiled=True)

    folded = fold(place, doc_lengths, step_offsets, cotangent)
    folds = [folded] + [swapped(folded, s) for s in range(1, tn)]
    sent = features(place, low_feature, mid_feature, merging_gain, tn)
    parts = [sent[0]] + [swapped(sent[s], s) for s in range(1, tn)]

    high, high_squares = attend(doc_lengths, target_queries, target_keys, target_values)

    def summed(squares):
        squares = squares[:, 0, :]
        total = squares
        for s in range(1, tn):
            total = total + swapped(squares, s)
        return total

    own_gain = lax.dynamic_slice(merging_gain, (2, j * piece), (1, piece))
    merged, squares = merge(place, summed(high_squares), own_gain, high, parts, width)
    own_gain = lax.dynamic_slice(draft_gain, (j * piece,), (piece,)).reshape(1, piece)
    grad, *values = project(place, summed(squares), own_gain, merged, weight, folds, width)
    values = [values[0]] + [swapped(values[s], s) for s in range(1, tn)]
    draft_values = spread(place, doc_lengths, step_offsets, values)

    grad = lax.psum_scatter(grad, "dp", scatter_dimension=0, tiled=True)
    weight_grad = lax.ppermute(grad, both, [((r % n) * tn + r // n, r) for r in range(n * tn)])
    rows = weight_grad.shape[0]
    gain = lax.dynamic_slice(draft_gain, (flat * rows,), (rows,))
    gain_grad = jnp.sum(weight_grad * draft_weight.astype(F32), axis=1) / gain
    return (draft_values, weight_grad, gain_grad)


def solution(mesh):
    placed = (
        P("dp", "tensor"),
        P("dp", "tensor"),
        P("dp", "tensor"),
        P(("dp", "tensor"), None),
        P(("dp", "tensor"), None),
        P(),
        P(),
        P(("dp", "tensor"), None),
        P(None, ("dp", "tensor"), None),
        P("dp", None),
        P(),
    )
    return jax.shard_map(
        body,
        mesh=mesh,
        in_specs=placed,
        out_specs=(P(None, ("dp", "tensor"), None), P(("dp", "tensor"), None), P(("dp", "tensor"))),
        check_vma=False,
    )
```

```python
import functools
import math

import jax
import jax.numpy as jnp
import numpy as np
from jax import lax
from jax.experimental import pallas as pl
from jax.experimental.pallas import tpu as pltpu
from jax.sharding import PartitionSpec as P

HD = 128
STEPS = 3
OFFMAX = 32
EPSILON = 1e-05
VMEM_LIMIT = 20 * 1024 * 1024

VMEM = pl.BlockSpec(memory_space=pltpu.VMEM)
SMEM = pl.BlockSpec(memory_space=pltpu.SMEM)
F32 = jnp.float32
BF16 = jnp.bfloat16


SIDES = {64: (8, 4, 2)}


def sides_of(n):
    return SIDES.get(n, (1, 1, n))


def groups_along(n, *sides):
    sizes = sides_of(n)
    where = np.moveaxis(np.arange(n).reshape(sizes), sides, range(-len(sides), 0))
    return where.reshape(-1, math.prod(sizes[side] for side in sides)).tolist()


def block_order(n, tn):
    nz, ny, nx = sides_of(n)
    order = np.arange(n).reshape(ny, nz, nx)
    if nz == 2 * tn and n == ny * nx * tn * 2:
        for y in range(ny):
            for z in range(nz):
                for x in range(nx):
                    order[y, z, x] = (((z // tn) * ny + y) * nx + x) * tn + z % tn
    return order


def place_weight(weight):
    n, tn = lax.axis_size("dp"), lax.axis_size("tensor")
    nz, ny, nx = sides_of(n)
    pairs = []
    for j in range(tn):
        for q in range(n):
            y, z, x = q // (nz * nx), q // nx % nz, q % nx
            pairs.append((j * n + q, ((z * ny + y) * nx + x) * tn + j))
    return lax.ppermute(weight, ("dp", "tensor"), pairs)


def gather_weight(weight, sides):
    groups = groups_along(lax.axis_size("dp"), *sides)
    if len(groups[0]) > 1:
        weight = lax.all_gather(weight, "dp", axis=0, tiled=True, axis_index_groups=groups)
    return weight


def reduce_grad(grad):
    n, tn = lax.axis_size("dp"), lax.axis_size("tensor")
    nz, ny, nx = sides_of(n)
    columns = grad.shape[1]
    for side in (1, 0):
        count = sides_of(n)[side]
        if count > 1:
            if grad.dtype != BF16:
                grad = grad.astype(BF16)
            grad = lax.all_to_all(grad, "dp", 0, 0, tiled=True, axis_index_groups=groups_along(n, side))
            grad = jnp.sum(grad.reshape(count, -1, columns).astype(F32), axis=0)
    grad = grad.astype(F32)
    rows = grad.shape[0] // nx
    order = block_order(n, tn)
    x = lax.axis_index("dp") % nx
    total = None
    for turn in range(nx):
        pairs = []
        for z in range(nz):
            for y in range(ny):
                for x0 in range(nx):
                    for j in range(tn):
                        block = j * n + int(order[y, z, (x0 + turn) % nx])
                        pairs.append((((z * ny + y) * nx + x0) * tn + j, block))
        part = lax.dynamic_slice(grad, ((x + turn) % nx * rows, 0), (rows, columns))
        part = lax.ppermute(part, ("dp", "tensor"), pairs)
        total = part if total is None else total + part
    return total


def segment_start(places, lengths_ref):
    end = jnp.int32(0)
    start = jnp.zeros_like(places)
    for s in range(lengths_ref.shape[1]):
        end = end + lengths_ref[0, s]
        start = jnp.where(places >= end, end, start)
    return start


def column(row):
    n = row.shape[-1]
    eye = lax.broadcasted_iota(jnp.int32, (n, n), 0) == lax.broadcasted_iota(jnp.int32, (n, n), 1)
    return jnp.sum(jnp.where(eye, row, 0.0), axis=1, keepdims=True)


def lane_sums(values):
    return lax.dot_general(
        jnp.ones((8, values.shape[1]), F32), values, (((1,), (1,)), ((), ())),
        precision=lax.Precision.HIGHEST, preferred_element_type=F32)


def folded_square_sum(values):
    total = None
    for c in range(0, values.shape[1], 128):
        piece = values[:, c:c + 128]
        total = piece * piece if total is None else total + piece * piece
    return total


def features_kernel(tn, place_ref, low_ref, mid_ref, gain_ref, *outs):
    j = place_ref[0]
    width = low_ref.shape[1]
    piece = width // tn
    step = 1024

    def rms_scale(ref):
        total = None
        for c in range(0, width, step):
            part = folded_square_sum(ref[:, c:c + step].astype(F32))
            total = part if total is None else total + part
        return lax.rsqrt(jnp.sum(total, axis=1, keepdims=True) / width + EPSILON)

    low_scale = rms_scale(low_ref)
    mid_scale = rms_scale(mid_ref)
    for s, out in enumerate(outs):
        first = pl.multiple_of((j ^ s) * piece, piece)
        for c in range(0, piece, 512):
            at = pl.ds(first + c, 512)
            value = (low_ref[:, at].astype(F32) * low_scale * gain_ref[0:1, at]
                     + mid_ref[:, at].astype(F32) * mid_scale * gain_ref[1:2, at])
            out[:, c:c + 512] = value.astype(BF16)


def features(place, low, mid, gain, tn):
    rows, width = low.shape
    block = 32
    piece = width // tn
    return pl.pallas_call(
        functools.partial(features_kernel, tn),
        grid=(rows // block,),
        in_specs=[
            SMEM,
            pl.BlockSpec((block, width), lambda b: (b, 0)),
            pl.BlockSpec((block, width), lambda b: (b, 0)),
            pl.BlockSpec(gain.shape, lambda b: (0, 0)),
        ],
        out_specs=[pl.BlockSpec((block, piece), lambda b: (b, 0))] * tn,
        out_shape=[jax.ShapeDtypeStruct((rows, piece), BF16)] * tn,
        compiler_params=pltpu.CompilerParams(vmem_limit_bytes=VMEM_LIMIT),
        cost_estimate=pl.CostEstimate(flops=10 * rows * width, bytes_accessed=6 * rows * width, transcendentals=0),
        name="features",
    )(place, low, mid, gain)


def attend_kernel(window, lengths_ref, query_ref, key_ref, value_ref, high_ref, square_ref):
    block = query_ref.shape[0]
    pack = key_ref.shape[0]
    b = pl.program_id(0)
    first = pl.multiple_of(jnp.clip(b * block - (window - block), 0, pack - window), block)
    query_places = b * block + lax.broadcasted_iota(jnp.int32, (block, window), 0)
    key_places = first + lax.broadcasted_iota(jnp.int32, (block, window), 1)
    allowed = (key_places <= query_places) & (key_places >= segment_start(query_places, lengths_ref))
    bias = jnp.where(allowed, 0.0, -1e30).astype(F32)
    group = (query_ref.shape[1] // HD) // (key_ref.shape[1] // HD)
    squares = jnp.zeros((block, HD), F32)
    ones = jnp.ones((window, HD), BF16)
    scale = math.log2(math.e) / math.sqrt(HD)
    for g in range(key_ref.shape[1] // HD):
        key = key_ref[pl.ds(first, window), g * HD:(g + 1) * HD]
        value = jnp.concatenate([value_ref[pl.ds(first, window), g * HD:(g + 1) * HD], ones], axis=1)
        for r in range(group):
            at = slice((g * group + r) * HD, (g * group + r + 1) * HD)
            scores = lax.dot_general(query_ref[:, at], key, (((1,), (1,)), ((), ())), preferred_element_type=F32)
            scores = scores * scale + bias
            highest = jnp.max(scores, axis=1, keepdims=True)
            expo = jnp.exp2(scores - highest).astype(BF16)
            mixed = jnp.dot(expo, value, preferred_element_type=F32)
            out = (mixed[:, :HD] / mixed[:, HD:]).astype(BF16)
            high_ref[:, at] = out
            out = out.astype(F32)
            squares = squares + out * out
    square_ref[...] = lane_sums(squares)


def attend(lengths, queries, keys, values):
    pack, width = queries.shape
    block = 128
    window = min(pack, 256 + block)
    return pl.pallas_call(
        functools.partial(attend_kernel, window),
        grid=(pack // block,),
        in_specs=[
            SMEM,
            pl.BlockSpec((block, width), lambda b: (b, 0)),
            pl.BlockSpec(keys.shape, lambda b: (0, 0)),
            pl.BlockSpec(values.shape, lambda b: (0, 0)),
        ],
        out_specs=[
            pl.BlockSpec((block, width), lambda b: (b, 0)),
            pl.BlockSpec((8, block), lambda b: (0, b)),
        ],
        out_shape=[
            jax.ShapeDtypeStruct((pack, width), BF16),
            jax.ShapeDtypeStruct((8, pack), F32),
        ],
        compiler_params=pltpu.CompilerParams(vmem_limit_bytes=VMEM_LIMIT),
        cost_estimate=pl.CostEstimate(
            flops=4 * pack * window * width, bytes_accessed=4 * pack * width,
            transcendentals=pack * window * width // HD),
        name="attend",
    )(lengths, queries, keys, values)


def chosen(place_ref, lengths_ref, offset, rows, lead):
    target = place_ref[0] * rows + lax.broadcasted_iota(jnp.int32, (rows, rows + lead), 0)
    source = place_ref[0] * rows - lead + lax.broadcasted_iota(jnp.int32, (rows, rows + lead), 1)
    hit = (source == target - offset) & (source >= segment_start(target, lengths_ref))
    return jnp.where(hit, 1.0, 0.0).astype(BF16)


def fold_kernel(place_ref, lengths_ref, offsets_ref, cotangent_ref, out_ref):
    steps, rows, width = cotangent_ref.shape
    total = None
    for s in range(steps):
        pick = chosen(place_ref, lengths_ref, offsets_ref[s], rows, OFFMAX)
        part = lax.dot_general(pick, cotangent_ref[s], (((0,), (0,)), ((), ())), preferred_element_type=F32)
        total = part if total is None else total + part
    out_ref[...] = total.astype(BF16)


def fold(place, lengths, offsets, cotangent):
    steps, rows, width = cotangent.shape
    return pl.pallas_call(
        fold_kernel,
        in_specs=[SMEM, SMEM, SMEM, VMEM],
        out_specs=VMEM,
        out_shape=jax.ShapeDtypeStruct((rows + OFFMAX, width), BF16),
        compiler_params=pltpu.CompilerParams(vmem_limit_bytes=VMEM_LIMIT),
        cost_estimate=pl.CostEstimate(flops=2 * steps * rows * 160 * width, bytes_accessed=2 * steps * rows * width, transcendentals=0),
        name="fold",
    )(place, lengths, offsets, cotangent)


def merge_kernel(width, tn, place_ref, gain_ref, high_ref, *refs):
    parts, square_refs, out_ref, out_square_ref = refs[:tn], refs[tn:2 * tn], refs[2 * tn], refs[2 * tn + 1]
    j = place_ref[0]
    rows = parts[0].shape[0]
    piece = high_ref.shape[1]
    squares = square_refs[0][...]
    for s in range(1, tn):
        squares = squares + square_refs[s][...]
    scales = lax.rsqrt(squares / width + EPSILON)
    for b in range(tn):
        out_square_ref[:, b * rows:(b + 1) * rows] = scales[:, b * rows:(b + 1) * rows]
    for s in range(tn):
        first = pl.multiple_of((j ^ s) * rows, rows)
        at = pl.ds(first, rows)
        scale = column(out_square_ref[0:1, at])
        total = jnp.zeros((rows, 128), F32)
        for c in range(0, piece, 128):
            cols = slice(c, c + 128)
            gain = gain_ref[2:3, pl.ds(pl.multiple_of(j * piece + c, 128), 128)]
            merged = (parts[s][:, cols].astype(F32) + high_ref[at, cols].astype(F32) * scale * gain).astype(BF16)
            out_ref[at, cols] = merged
            merged = merged.astype(F32)
            total = total + merged * merged
        out_square_ref[:, at] = lane_sums(total)


def merge(place, gain, high, parts, squares, width):
    pack, piece = high.shape
    tn = len(parts)
    return pl.pallas_call(
        functools.partial(merge_kernel, width, tn),
        in_specs=[SMEM] + [VMEM] * (2 + 2 * tn),
        out_specs=[VMEM, VMEM],
        out_shape=[
            jax.ShapeDtypeStruct((pack, piece), BF16),
            jax.ShapeDtypeStruct((8, pack), F32),
        ],
        compiler_params=pltpu.CompilerParams(vmem_limit_bytes=VMEM_LIMIT),
        cost_estimate=pl.CostEstimate(flops=8 * pack * piece, bytes_accessed=6 * pack * piece, transcendentals=0),
        name="merge",
    )(place, gain, high, *parts, *squares)


def grads(place, gain, merged, folds, squares, width, order):
    pack, piece = merged.shape
    tn = len(squares)
    rows = pack // tn
    vw = folds[0].shape[1]
    blocks = order.reshape(-1)
    size = piece // blocks.size

    def kernel(place_ref, gain_ref, merged_ref, *refs):
        fold_refs, square_refs, (grad_ref, hidden_ref, fold_ref) = refs[:tn], refs[tn:2 * tn], refs[2 * tn:]
        j = place_ref[0]
        squares = square_refs[0][...]
        for s in range(1, tn):
            squares = squares + square_refs[s][...]
        scales = lax.rsqrt(squares / width + EPSILON)
        for b in range(tn):
            at = slice(b * rows, (b + 1) * rows)
            scale = column(scales[0:1, at])
            for c in range(0, piece, 128):
                cols = slice(c, c + 128)
                gain = gain_ref[:, pl.ds(pl.multiple_of(j * piece + c, 128), 128)]
                hidden_ref[at, cols] = (merged_ref[at, cols].astype(F32) * scale * gain).astype(BF16)
        fold_ref[...] = jnp.zeros_like(fold_ref)
        for s in range(tn):
            at = pl.ds(pl.multiple_of((j ^ s) * rows, rows), rows + OFFMAX)
            fold_ref[at, :] = fold_ref[at, :] + fold_refs[s][...].astype(F32)
        folded = fold_ref[OFFMAX:, :].astype(BF16)
        chunk = max(256, size)
        for c in range(0, piece, chunk):
            part = lax.dot_general(
                hidden_ref[:, c:c + chunk], folded, (((0,), (0,)), ((), ())), preferred_element_type=F32).astype(BF16)
            for q in range(c // size, (c + chunk) // size):
                to = int(np.argmax(blocks == q)) * size
                grad_ref[to:to + size, :] = part[q * size - c:(q + 1) * size - c, :]

    return pl.pallas_call(
        kernel,
        in_specs=[SMEM] + [VMEM] * (2 + 2 * tn),
        out_specs=[VMEM] * 2,
        out_shape=[jax.ShapeDtypeStruct((piece, vw), BF16), jax.ShapeDtypeStruct((pack, piece), BF16)],
        scratch_shapes=[pltpu.VMEM((pack + OFFMAX, vw), F32)],
        compiler_params=pltpu.CompilerParams(vmem_limit_bytes=VMEM_LIMIT),
        cost_estimate=pl.CostEstimate(flops=2 * pack * piece * vw, bytes_accessed=8 * pack * piece, transcendentals=0),
        name="grads",
    )(place, gain, merged, *folds, *squares)


def project(place, hidden, weight, tn):
    pack, piece = hidden.shape
    rows = pack // tn
    vw = weight.shape[1]

    def kernel(place_ref, hidden_ref, weight_ref, *refs):
        value_refs, total_ref = refs[:tn], refs[tn]
        j = place_ref[0]
        total_ref[0:OFFMAX, :] = jnp.zeros((OFFMAX, vw), F32)
        for c in range(0, pack, 256):
            total_ref[OFFMAX + c:OFFMAX + c + 256, :] = jnp.dot(
                hidden_ref[c:c + 256, :], weight_ref[...], preferred_element_type=F32)
        for s in range(tn):
            at = pl.ds(pl.multiple_of((j ^ s) * rows, rows), rows + OFFMAX)
            value_refs[s][...] = total_ref[at, :].astype(value_refs[s].dtype)

    return pl.pallas_call(
        kernel,
        in_specs=[SMEM] + [VMEM] * 2,
        out_specs=[VMEM] * tn,
        out_shape=[jax.ShapeDtypeStruct((rows + OFFMAX, vw), F32 if s == 0 else BF16) for s in range(tn)],
        scratch_shapes=[pltpu.VMEM((pack + OFFMAX, vw), F32)],
        compiler_params=pltpu.CompilerParams(vmem_limit_bytes=VMEM_LIMIT),
        cost_estimate=pl.CostEstimate(flops=2 * pack * piece * vw, bytes_accessed=4 * pack * piece, transcendentals=0),
        name="project",
    )(place, hidden, weight)


def spread(place, lengths, offsets, parts):
    rows, vw = parts[0].shape[0] - OFFMAX, parts[0].shape[1]

    def kernel(place_ref, lengths_ref, offsets_ref, *refs):
        parts_refs, out_ref = refs[:-1], refs[-1]
        total = None
        for ref in parts_refs:
            part = ref[...].astype(F32)
            total = part if total is None else total + part
        total = total.astype(BF16)
        for s in range(STEPS):
            pick = chosen(place_ref, lengths_ref, offsets_ref[s], rows, OFFMAX)
            out_ref[s] = jnp.dot(pick, total, preferred_element_type=F32).astype(BF16)

    return pl.pallas_call(
        kernel,
        in_specs=[SMEM] * 3 + [VMEM] * len(parts),
        out_specs=VMEM,
        out_shape=jax.ShapeDtypeStruct((STEPS, rows, vw), BF16),
        compiler_params=pltpu.CompilerParams(vmem_limit_bytes=VMEM_LIMIT),
        cost_estimate=pl.CostEstimate(flops=2 * STEPS * rows * 160 * vw, bytes_accessed=8 * STEPS * rows * vw, transcendentals=0),
        name="spread",
    )(place, lengths, offsets, *parts)


def body(
    target_queries,
    target_keys,
    target_values,
    low_feature,
    mid_feature,
    merging_gain,
    draft_gain,
    draft_weight,
    cotangent,
    doc_lengths,
    step_offsets,
):
    n = lax.axis_size("dp")
    tn = lax.axis_size("tensor")
    j = lax.axis_index("tensor")
    flat = lax.axis_index("dp") * tn + j
    place = j.reshape(1).astype(jnp.int32)
    width = low_feature.shape[1]
    piece = width // tn
    pack = target_queries.shape[0]
    both = ("dp", "tensor")

    def swapped(values, s):
        return lax.ppermute(values, "tensor", [(a, a ^ s) for a in range(tn)])

    own_weight = place_weight(draft_weight)
    low_feature, _ = lax.optimization_barrier((low_feature, own_weight))
    sent = features(place, low_feature, mid_feature, merging_gain, tn)
    parts = [sent[0]] + [swapped(sent[s], s) for s in range(1, tn)]
    some_weight = gather_weight(own_weight, (0, 2))

    high, squares = attend(doc_lengths, target_queries, target_keys, target_values)
    squares = [squares] + [swapped(squares, s) for s in range(1, tn)]
    cotangent, _ = lax.optimization_barrier((cotangent, high))
    folded = fold(place, doc_lengths, step_offsets, cotangent)
    folds = [folded] + [swapped(folded, s) for s in range(1, tn)]
    gain, _ = lax.optimization_barrier((merging_gain, folds[1]))
    merged, squares = merge(place, gain, high, parts, squares, width)
    some_weight, _ = lax.optimization_barrier((some_weight, merged))
    weight = gather_weight(some_weight, (1,))
    squares = [squares] + [swapped(squares, s) for s in range(1, tn)]
    grad, hidden = grads(
        place, draft_gain.reshape(1, width), merged, folds, squares, width, block_order(n, tn))
    weight_grad = reduce_grad(grad)

    values = project(place, hidden, weight, tn)
    values = [values[0]] + [swapped(values[s], s) for s in range(1, tn)]
    draft_values = spread(place, doc_lengths, step_offsets, values)

    rows = weight_grad.shape[0]
    gain = lax.dynamic_slice(draft_gain, (flat * rows,), (rows,))
    gain_grad = jnp.sum(weight_grad * draft_weight.astype(F32), axis=1) / gain
    return (draft_values, weight_grad, gain_grad)


def solution(mesh):
    placed = (
        P("dp", "tensor"),
        P("dp", "tensor"),
        P("dp", "tensor"),
        P(("dp", "tensor"), None),
        P(("dp", "tensor"), None),
        P(),
        P(),
        P(("dp", "tensor"), None),
        P(None, ("dp", "tensor"), None),
        P("dp", None),
        P(),
    )
    return jax.shard_map(
        body,
        mesh=mesh,
        in_specs=placed,
        out_specs=(P(None, ("dp", "tensor"), None), P(("dp", "tensor"), None), P(("dp", "tensor"))),
        check_vma=False,
    )
```

```python
import functools
import math

import jax
import jax.numpy as jnp
import numpy as np
from jax import lax
from jax.experimental import pallas as pl
from jax.experimental.pallas import tpu as pltpu
from jax.sharding import PartitionSpec as P

HD = 128
STEPS = 3
OFFMAX = 32
EPSILON = 1e-05
VMEM_LIMIT = 20 * 1024 * 1024
FEATURES_LIMIT = 60 * 1024 * 1024

VMEM = pl.BlockSpec(memory_space=pltpu.VMEM)
SMEM = pl.BlockSpec(memory_space=pltpu.SMEM)
F32 = jnp.float32
BF16 = jnp.bfloat16


SIDES = {64: (8, 4, 2)}


def sides_of(n):
    return SIDES.get(n, (1, 1, n))


def groups_along(n, *sides):
    sizes = sides_of(n)
    where = np.moveaxis(np.arange(n).reshape(sizes), sides, range(-len(sides), 0))
    return where.reshape(-1, math.prod(sizes[side] for side in sides)).tolist()


def block_order(n, tn):
    nz, ny, nx = sides_of(n)
    order = np.arange(n).reshape(ny, nz, nx)
    if nz == 2 * tn and n == ny * nx * tn * 2:
        for y in range(ny):
            for z in range(nz):
                for x in range(nx):
                    order[y, z, x] = (((z // tn) * ny + y) * nx + x) * tn + z % tn
    return order


def moved(values, change):
    n = lax.axis_size("dp")
    nz, ny, nx = sides_of(n)
    pairs = []
    for source in range(n):
        z, y, x = change(source // (ny * nx), source // nx % ny, source % nx)
        pairs.append((source, (z * ny + y) * nx + x))
    return lax.ppermute(values, "dp", pairs)


def placed_weight(weight):
    n, tn = lax.axis_size("dp"), lax.axis_size("tensor")
    nz, ny, nx = sides_of(n)
    x = lax.axis_index("dp") % nx
    both = []
    for far in (0, nz // 2) if nz > 1 else (0,):
        parts = []
        for turn in range(nx):
            pairs = []
            for j in range(tn):
                for q in range(n):
                    y, z, x0 = q // (nz * nx), (q // nx % nz) ^ far, (q + turn) % nx
                    pairs.append((j * n + q, ((z * ny + y) * nx + x0) * tn + j))
            parts.append(lax.ppermute(weight, ("dp", "tensor"), pairs))
        both.append(parts)
    if nx == 1:
        return jnp.concatenate([parts[0] for parts in both])
    return jnp.where(
        x == 0,
        jnp.concatenate([part for parts in both for part in parts]),
        jnp.concatenate([part for parts in both for part in parts[::-1]]))


def weight_along_z(part):
    nz = sides_of(lax.axis_size("dp"))[0]
    return [part] + [moved(part, lambda z, y, x: (z ^ s, y, x)) for s in range(1, nz // 2)]


def weight_once(halves):
    if sides_of(lax.axis_size("dp"))[1] == 1:
        return [[half] for half in halves]
    return [[half, moved(half, lambda z, y, x: (z, y ^ first, x))] for half, (first, _) in zip(halves, EXCHANGES)]


def weight_twice(halves):
    if sides_of(lax.axis_size("dp"))[1] == 1:
        return halves
    out = []
    for half, (first, second) in zip(halves, EXCHANGES):
        got = dict(zip((0, first), half))
        for s in (0, first):
            got[s ^ second] = moved(got[s], lambda z, y, x: (z, y ^ second, x))
        out.append([got[s] for s in range(4)])
    return out


KEPT = ((0, 3), (0, 1))
SENT = ((1, 2), (3, 2))
EXCHANGES = ((1, 3), (3, 1))


def reduce_along_y(kept, sent):
    ny = sides_of(lax.axis_size("dp"))[1]
    halves = []
    for keep, send, (first, second) in zip(kept, sent, EXCHANGES):
        if ny > 1:
            got = moved(send, lambda z, y, x: (z, y ^ first, x))
            own = keep[0] + got[0].astype(F32)
            other = (keep[1] + got[1].astype(F32)).astype(BF16)
            halves.append((own, moved(other, lambda z, y, x: (z, y ^ second, x))))
        else:
            halves.append((keep[0], None))
    halves = [own if got is None else own + got.astype(F32) for own, got in halves]
    return jnp.concatenate(halves)


def reduce_grad(grad):
    n, tn = lax.axis_size("dp"), lax.axis_size("tensor")
    nz, ny, nx = sides_of(n)
    columns = grad.shape[-1]
    if nz > 1:
        grad = lax.all_to_all(grad.astype(BF16), "dp", 0, 0, tiled=True, axis_index_groups=groups_along(n, 0))
        grad = jnp.sum(grad.reshape(nz, -1, columns).astype(F32), axis=0)
    rows = grad.shape[0] // nx
    order = block_order(n, tn)
    x = lax.axis_index("dp") % nx
    total = None
    for turn in range(nx):
        pairs = []
        for z in range(nz):
            for y in range(ny):
                for x0 in range(nx):
                    for j in range(tn):
                        block = j * n + int(order[y, z, (x0 + turn) % nx])
                        pairs.append((((z * ny + y) * nx + x0) * tn + j, block))
        part = lax.dynamic_slice(grad, ((x + turn) % nx * rows, 0), (rows, columns))
        part = lax.ppermute(part, ("dp", "tensor"), pairs)
        total = part if total is None else total + part
    return total


def segment_start(places, lengths_ref):
    end = jnp.int32(0)
    start = jnp.zeros_like(places)
    for s in range(lengths_ref.shape[1]):
        end = end + lengths_ref[0, s]
        start = jnp.where(places >= end, end, start)
    return start


def column(row):
    n = row.shape[-1]
    eye = lax.broadcasted_iota(jnp.int32, (n, n), 0) == lax.broadcasted_iota(jnp.int32, (n, n), 1)
    return jnp.sum(jnp.where(eye, row, 0.0), axis=1, keepdims=True)


def lane_sums(values):
    return lax.dot_general(
        jnp.ones((8, values.shape[1]), F32), values, (((1,), (1,)), ((), ())),
        precision=lax.Precision.HIGHEST, preferred_element_type=F32)


def folded_square_sum(values):
    total = None
    for c in range(0, values.shape[1], 128):
        piece = values[:, c:c + 128]
        total = piece * piece if total is None else total + piece * piece
    return total


def features_kernel(tn, place_ref, low_ref, mid_ref, gain_ref, *outs):
    j = place_ref[0]
    width = low_ref.shape[1]
    piece = width // tn
    step = 1024

    def rms_scale(ref):
        total = None
        for c in range(0, width, step):
            part = folded_square_sum(ref[:, c:c + step].astype(F32))
            total = part if total is None else total + part
        return lax.rsqrt(jnp.sum(total, axis=1, keepdims=True) / width + EPSILON)

    low_scale = rms_scale(low_ref)
    mid_scale = rms_scale(mid_ref)
    for s, out in enumerate(outs):
        first = pl.multiple_of((j ^ s) * piece, piece)
        for c in range(0, piece, 512):
            at = pl.ds(first + c, 512)
            value = (low_ref[:, at].astype(F32) * low_scale * gain_ref[0:1, at]
                     + mid_ref[:, at].astype(F32) * mid_scale * gain_ref[1:2, at])
            out[:, c:c + 512] = value.astype(BF16)


def features(place, low, mid, gain, tn):
    rows, width = low.shape
    block = 32
    piece = width // tn
    return pl.pallas_call(
        functools.partial(features_kernel, tn),
        grid=(rows // block,),
        in_specs=[
            SMEM,
            pl.BlockSpec((block, width), lambda b: (b, 0)),
            pl.BlockSpec((block, width), lambda b: (b, 0)),
            pl.BlockSpec(gain.shape, lambda b: (0, 0)),
        ],
        out_specs=[pl.BlockSpec((block, piece), lambda b: (b, 0))] * tn,
        out_shape=[jax.ShapeDtypeStruct((rows, piece), BF16)] * tn,
        compiler_params=pltpu.CompilerParams(vmem_limit_bytes=FEATURES_LIMIT),
        cost_estimate=pl.CostEstimate(flops=10 * rows * width, bytes_accessed=6 * rows * width, transcendentals=0),
        name="features",
    )(place, low, mid, gain)


def attend_kernel(window, lengths_ref, query_ref, key_ref, value_ref, high_ref, square_ref):
    block = query_ref.shape[0]
    pack = key_ref.shape[0]
    b = pl.program_id(0)
    first = pl.multiple_of(jnp.clip(b * block - (window - block), 0, pack - window), block)
    query_places = b * block + lax.broadcasted_iota(jnp.int32, (block, window), 0)
    key_places = first + lax.broadcasted_iota(jnp.int32, (block, window), 1)
    allowed = (key_places <= query_places) & (key_places >= segment_start(query_places, lengths_ref))
    bias = jnp.where(allowed, 0.0, -1e30).astype(F32)
    group = (query_ref.shape[1] // HD) // (key_ref.shape[1] // HD)
    squares = jnp.zeros((block, HD), F32)
    ones = jnp.ones((window, HD), BF16)
    scale = math.log2(math.e) / math.sqrt(HD)
    for g in range(key_ref.shape[1] // HD):
        key = key_ref[pl.ds(first, window), g * HD:(g + 1) * HD]
        value = jnp.concatenate([value_ref[pl.ds(first, window), g * HD:(g + 1) * HD], ones], axis=1)
        for r in range(group):
            at = slice((g * group + r) * HD, (g * group + r + 1) * HD)
            scores = lax.dot_general(query_ref[:, at], key, (((1,), (1,)), ((), ())), preferred_element_type=F32)
            scores = scores * scale + bias
            highest = jnp.max(scores, axis=1, keepdims=True)
            expo = jnp.exp2(scores - highest).astype(BF16)
            mixed = jnp.dot(expo, value, preferred_element_type=F32)
            out = (mixed[:, :HD] / mixed[:, HD:]).astype(BF16)
            high_ref[:, at] = out
            out = out.astype(F32)
            squares = squares + out * out
    square_ref[...] = lane_sums(squares)


def attend(lengths, queries, keys, values):
    pack, width = queries.shape
    block = 128
    window = min(pack, 256 + block)
    return pl.pallas_call(
        functools.partial(attend_kernel, window),
        grid=(pack // block,),
        in_specs=[
            SMEM,
            pl.BlockSpec((block, width), lambda b: (b, 0)),
            pl.BlockSpec(keys.shape, lambda b: (0, 0)),
            pl.BlockSpec(values.shape, lambda b: (0, 0)),
        ],
        out_specs=[
            pl.BlockSpec((block, width), lambda b: (b, 0)),
            pl.BlockSpec((8, block), lambda b: (0, b)),
        ],
        out_shape=[
            jax.ShapeDtypeStruct((pack, width), BF16),
            jax.ShapeDtypeStruct((8, pack), F32),
        ],
        compiler_params=pltpu.CompilerParams(vmem_limit_bytes=VMEM_LIMIT),
        cost_estimate=pl.CostEstimate(
            flops=4 * pack * window * width, bytes_accessed=4 * pack * width,
            transcendentals=pack * window * width // HD),
        name="attend",
    )(lengths, queries, keys, values)


def chosen(place_ref, lengths_ref, offset, rows, lead):
    target = place_ref[0] * rows + lax.broadcasted_iota(jnp.int32, (rows, rows + lead), 0)
    source = place_ref[0] * rows - lead + lax.broadcasted_iota(jnp.int32, (rows, rows + lead), 1)
    hit = (source == target - offset) & (source >= segment_start(target, lengths_ref))
    return jnp.where(hit, 1.0, 0.0).astype(BF16)


def fold_kernel(place_ref, lengths_ref, offsets_ref, cotangent_ref, out_ref):
    steps, rows, width = cotangent_ref.shape
    total = None
    for s in range(steps):
        pick = chosen(place_ref, lengths_ref, offsets_ref[s], rows, OFFMAX)
        part = lax.dot_general(pick, cotangent_ref[s], (((0,), (0,)), ((), ())), preferred_element_type=F32)
        total = part if total is None else total + part
    out_ref[...] = total.astype(BF16)


def fold(place, lengths, offsets, cotangent):
    steps, rows, width = cotangent.shape
    return pl.pallas_call(
        fold_kernel,
        in_specs=[SMEM, SMEM, SMEM, VMEM],
        out_specs=VMEM,
        out_shape=jax.ShapeDtypeStruct((rows + OFFMAX, width), BF16),
        compiler_params=pltpu.CompilerParams(vmem_limit_bytes=VMEM_LIMIT),
        cost_estimate=pl.CostEstimate(flops=2 * steps * rows * 160 * width, bytes_accessed=2 * steps * rows * width, transcendentals=0),
        name="fold",
    )(place, lengths, offsets, cotangent)


def merge_kernel(width, tn, place_ref, gain_ref, high_ref, *refs):
    parts, square_refs, out_ref, out_square_ref = refs[:tn], refs[tn:2 * tn], refs[2 * tn], refs[2 * tn + 1]
    j = place_ref[0]
    rows = parts[0].shape[0]
    piece = high_ref.shape[1]
    squares = square_refs[0][...]
    for s in range(1, tn):
        squares = squares + square_refs[s][...]
    scales = lax.rsqrt(squares / width + EPSILON)
    for b in range(tn):
        out_square_ref[:, b * rows:(b + 1) * rows] = scales[:, b * rows:(b + 1) * rows]
    for s in range(tn):
        first = pl.multiple_of((j ^ s) * rows, rows)
        at = pl.ds(first, rows)
        scale = column(out_square_ref[0:1, at])
        total = jnp.zeros((rows, 128), F32)
        for c in range(0, piece, 128):
            cols = slice(c, c + 128)
            gain = gain_ref[2:3, pl.ds(pl.multiple_of(j * piece + c, 128), 128)]
            merged = (parts[s][:, cols].astype(F32) + high_ref[at, cols].astype(F32) * scale * gain).astype(BF16)
            out_ref[at, cols] = merged
            merged = merged.astype(F32)
            total = total + merged * merged
        out_square_ref[:, at] = lane_sums(total)


def merge(place, gain, high, parts, squares, width):
    pack, piece = high.shape
    tn = len(parts)
    return pl.pallas_call(
        functools.partial(merge_kernel, width, tn),
        in_specs=[SMEM] + [VMEM] * (2 + 2 * tn),
        out_specs=[VMEM, VMEM],
        out_shape=[
            jax.ShapeDtypeStruct((pack, piece), BF16),
            jax.ShapeDtypeStruct((8, pack), F32),
        ],
        compiler_params=pltpu.CompilerParams(vmem_limit_bytes=VMEM_LIMIT),
        cost_estimate=pl.CostEstimate(flops=8 * pack * piece, bytes_accessed=6 * pack * piece, transcendentals=0),
        name="merge",
    )(place, gain, high, *parts, *squares)


def grads(place, gain, merged, folds, squares, width, ny, tn):
    pack, piece = merged.shape
    rows = pack // tn
    vw = folds[0].shape[1]
    chunk = piece // (2 * ny)
    kept, sent = (KEPT, SENT) if ny > 1 else (((0,), (0,)), ((), ()))
    steps = [(h, s, True) for h in range(2) for s in kept[h]] + [(h, s, False) for h in range(2) for s in sent[h]]
    steps.sort(key=lambda step: step[2])
    size = chunk // (2 * tn) if ny > 1 else chunk

    def kernel(place_ref, gain_ref, merged_ref, *refs):
        fold_refs, square_refs, refs = refs[:tn], refs[tn:2 * tn], refs[2 * tn:]
        keep_refs, refs = refs[:2], refs[2:]
        send_refs, refs = refs[:2 if ny > 1 else 0], refs[2 if ny > 1 else 0:]
        hidden_ref, fold_ref = refs
        j, y = place_ref[0], place_ref[1]
        squares = square_refs[0][...]
        for s in range(1, tn):
            squares = squares + square_refs[s][...]
        scales = lax.rsqrt(squares / width + EPSILON)
        for b in range(tn):
            at = slice(b * rows, (b + 1) * rows)
            scale = column(scales[0:1, at])
            for c in range(0, piece, 128):
                cols = slice(c, c + 128)
                gain = gain_ref[:, pl.ds(pl.multiple_of(j * piece + c, 128), 128)]
                hidden_ref[at, cols] = (merged_ref[at, cols].astype(F32) * scale * gain).astype(BF16)
        fold_ref[...] = jnp.zeros_like(fold_ref)
        for s in range(tn):
            at = pl.ds(pl.multiple_of((j ^ s) * rows, rows), rows + OFFMAX)
            fold_ref[at, :] = fold_ref[at, :] + fold_refs[s][...].astype(F32)
        folded = fold_ref[OFFMAX:, :].astype(BF16)
        for h, s, keep in steps:
            at = pl.ds(pl.multiple_of(h * ny * chunk + (y ^ s) * chunk, chunk), chunk)
            part = lax.dot_general(
                hidden_ref[:, at], folded, (((0,), (0,)), ((), ())), preferred_element_type=F32)
            if size < chunk:
                part = jnp.concatenate(
                    [part[(x * tn + t) * size:(x * tn + t + 1) * size] for t in range(tn) for x in range(2)], axis=0)
            if keep:
                keep_refs[h][kept[h].index(s)] = part
            else:
                send_refs[h][sent[h].index(s)] = part.astype(BF16)

    out_shape = [jax.ShapeDtypeStruct((len(kept[h]), chunk, vw), F32) for h in range(2)]
    if ny > 1:
        out_shape += [jax.ShapeDtypeStruct((len(sent[h]), chunk, vw), BF16) for h in range(2)]
    out_shape += [jax.ShapeDtypeStruct((pack, piece), BF16)]
    out = pl.pallas_call(
        kernel,
        in_specs=[SMEM] + [VMEM] * (2 + 2 * tn),
        out_specs=[VMEM] * len(out_shape),
        out_shape=out_shape,
        scratch_shapes=[pltpu.VMEM((pack + OFFMAX, vw), F32)],
        compiler_params=pltpu.CompilerParams(vmem_limit_bytes=VMEM_LIMIT),
        cost_estimate=pl.CostEstimate(flops=2 * pack * piece * vw, bytes_accessed=8 * pack * piece, transcendentals=0),
        name="grads",
    )(place, gain, merged, *folds, *squares)
    return out[:2], out[2:-1] if ny > 1 else (None, None), out[-1]


def stacked(place, parts, nz):
    rows, vw = parts[0].shape
    half = rows // 2

    def kernel(place_ref, *refs):
        part_refs, out_refs = refs[:-2], refs[-2:]
        z = place_ref[2]
        if nz == 1:
            for h in range(2):
                out_refs[h][...] = part_refs[0][h * half:(h + 1) * half, :]
            return
        for h in range(2):
            @pl.when((z >= nz // 2) == (h == 1))
            def _(h=h):
                for s, ref in enumerate(part_refs):
                    at = pl.ds(pl.multiple_of(((z ^ s) & (nz // 2 - 1)) * half, half), half)
                    out_refs[h][at, :] = ref[0:half, :]
                    out_refs[1 - h][at, :] = ref[half:rows, :]

    return pl.pallas_call(
        kernel,
        in_specs=[SMEM] + [VMEM] * len(parts),
        out_specs=[VMEM] * 2,
        out_shape=[jax.ShapeDtypeStruct((half * len(parts), vw), BF16)] * 2,
        compiler_params=pltpu.CompilerParams(vmem_limit_bytes=VMEM_LIMIT),
        cost_estimate=pl.CostEstimate(flops=0, bytes_accessed=4 * len(parts) * rows * vw, transcendentals=0),
        name="stacked",
    )(place, *parts)


def project(place, hidden, weights, tn):
    pack, piece = hidden.shape
    rows = pack // tn
    part, vw = weights[0][0].shape
    count = len(weights[0])

    def kernel(place_ref, hidden_ref, *refs):
        weight_refs, value_refs, total_ref = refs[:2 * count], refs[2 * count:-1], refs[-1]
        j, y = place_ref[0], place_ref[1]
        total_ref[0:OFFMAX, :] = jnp.zeros((OFFMAX, vw), F32)
        block = 128
        for c in range(0, pack, block):
            total = None
            for h in range(2):
                for s in range(count):
                    at = pl.ds(pl.multiple_of((y ^ s) * 2 * part + h * part, part), part)
                    term = jnp.dot(
                        hidden_ref[c:c + block, at], weight_refs[h * count + s][...], preferred_element_type=F32)
                    total = term if total is None else total + term
            total_ref[OFFMAX + c:OFFMAX + c + block, :] = total
        for s in range(tn):
            at = pl.ds(pl.multiple_of((j ^ s) * rows, rows), rows + OFFMAX)
            value_refs[s][...] = total_ref[at, :].astype(value_refs[s].dtype)

    return pl.pallas_call(
        kernel,
        in_specs=[SMEM] + [VMEM] * (1 + 2 * count),
        out_specs=[VMEM] * tn,
        out_shape=[jax.ShapeDtypeStruct((rows + OFFMAX, vw), F32 if s == 0 else BF16) for s in range(tn)],
        scratch_shapes=[pltpu.VMEM((pack + OFFMAX, vw), F32)],
        compiler_params=pltpu.CompilerParams(vmem_limit_bytes=VMEM_LIMIT),
        cost_estimate=pl.CostEstimate(flops=2 * pack * piece * vw, bytes_accessed=4 * pack * piece, transcendentals=0),
        name="project",
    )(place, hidden, *weights[0], *weights[1])


def spread(place, lengths, offsets, parts):
    rows, vw = parts[0].shape[0] - OFFMAX, parts[0].shape[1]

    def kernel(place_ref, lengths_ref, offsets_ref, *refs):
        parts_refs, out_ref = refs[:-1], refs[-1]
        total = None
        for ref in parts_refs:
            part = ref[...].astype(F32)
            total = part if total is None else total + part
        total = total.astype(BF16)
        for s in range(STEPS):
            pick = chosen(place_ref, lengths_ref, offsets_ref[s], rows, OFFMAX)
            out_ref[s] = jnp.dot(pick, total, preferred_element_type=F32).astype(BF16)

    return pl.pallas_call(
        kernel,
        in_specs=[SMEM] * 3 + [VMEM] * len(parts),
        out_specs=VMEM,
        out_shape=jax.ShapeDtypeStruct((STEPS, rows, vw), BF16),
        compiler_params=pltpu.CompilerParams(vmem_limit_bytes=VMEM_LIMIT),
        cost_estimate=pl.CostEstimate(flops=2 * STEPS * rows * 160 * vw, bytes_accessed=8 * STEPS * rows * vw, transcendentals=0),
        name="spread",
    )(place, lengths, offsets, *parts)


def body(
    target_queries,
    target_keys,
    target_values,
    low_feature,
    mid_feature,
    merging_gain,
    draft_gain,
    draft_weight,
    cotangent,
    doc_lengths,
    step_offsets,
):
    n = lax.axis_size("dp")
    tn = lax.axis_size("tensor")
    j = lax.axis_index("tensor")
    i = lax.axis_index("dp")
    flat = i * tn + j
    nz, ny, nx = sides_of(n)
    place = jnp.stack([j, i // nx % ny, i // (ny * nx)]).astype(jnp.int32)
    width = low_feature.shape[1]
    piece = width // tn
    pack = target_queries.shape[0]
    both = ("dp", "tensor")

    def swapped(values, s):
        return lax.ppermute(values, "tensor", [(a, a ^ s) for a in range(tn)])

    own_weight = placed_weight(draft_weight)
    first_place, _ = lax.optimization_barrier((place, own_weight))
    sent = features(first_place, low_feature, mid_feature, merging_gain, tn)
    parts = [sent[0]] + [swapped(sent[s], s) for s in range(1, tn)]

    high, squares = attend(doc_lengths, target_queries, target_keys, target_values)
    own_weight, cotangent, _ = lax.optimization_barrier((own_weight, cotangent, high))
    halves = stacked(place, weight_along_z(own_weight), nz)
    folded = fold(place, doc_lengths, step_offsets, cotangent)
    folds = [folded] + [swapped(folded, s) for s in range(1, tn)]
    squares, _, _ = lax.optimization_barrier((squares, halves[0], folds[1]))
    squares = [squares] + [swapped(squares, s) for s in range(1, tn)]
    merged, squares = merge(place, merging_gain, high, parts, squares, width)
    squares = [squares] + [swapped(squares, s) for s in range(1, tn)]
    kept, cut, hidden = grads(place, draft_gain.reshape(1, width), merged, folds, squares, width, ny, tn)
    halves, hidden = lax.optimization_barrier((halves, hidden))
    halves = weight_once(halves)
    grad = reduce_along_y(kept, cut)
    halves, grad = lax.optimization_barrier((halves, grad))
    weights = weight_twice(halves)
    weight_grad = reduce_grad(grad)

    values = project(place, hidden, weights, tn)
    values = [values[0]] + [swapped(values[s], s) for s in range(1, tn)]
    draft_values = spread(place, doc_lengths, step_offsets, values)

    rows = weight_grad.shape[0]
    gain = lax.dynamic_slice(draft_gain, (flat * rows,), (rows,))
    gain_grad = jnp.sum(weight_grad * draft_weight.astype(F32), axis=1) / gain
    return (draft_values, weight_grad, gain_grad)


def solution(mesh):
    placed = (
        P("dp", "tensor"),
        P("dp", "tensor"),
        P("dp", "tensor"),
        P(("dp", "tensor"), None),
        P(("dp", "tensor"), None),
        P(),
        P(),
        P(("dp", "tensor"), None),
        P(None, ("dp", "tensor"), None),
        P("dp", None),
        P(),
    )
    return jax.shard_map(
        body,
        mesh=mesh,
        in_specs=placed,
        out_specs=(P(None, ("dp", "tensor"), None), P(("dp", "tensor"), None), P(("dp", "tensor"))),
        check_vma=False,
    )
```

```python
import functools
import math

import jax
import jax.numpy as jnp
import numpy as np
from jax import lax
from jax.experimental import pallas as pl
from jax.experimental.pallas import tpu as pltpu
from jax.sharding import PartitionSpec as P

HD = 128
STEPS = 3
OFFMAX = 32
EPSILON = 1e-05
VMEM_LIMIT = 20 * 1024 * 1024
FEATURES_LIMIT = 60 * 1024 * 1024

VMEM = pl.BlockSpec(memory_space=pltpu.VMEM)
SMEM = pl.BlockSpec(memory_space=pltpu.SMEM)
F32 = jnp.float32
BF16 = jnp.bfloat16


SIDES = {64: (8, 4, 2)}


def sides_of(n):
    return SIDES.get(n, (1, 1, n))


def groups_along(n, *sides):
    sizes = sides_of(n)
    where = np.moveaxis(np.arange(n).reshape(sizes), sides, range(-len(sides), 0))
    return where.reshape(-1, math.prod(sizes[side] for side in sides)).tolist()


def block_order(n, tn):
    nz, ny, nx = sides_of(n)
    order = np.arange(n).reshape(ny, nz, nx)
    if nz == 2 * tn and n == ny * nx * tn * 2:
        for y in range(ny):
            for z in range(nz):
                for x in range(nx):
                    order[y, z, x] = (((z // tn) * ny + y) * nx + x) * tn + z % tn
    return order


def moved(values, change):
    n = lax.axis_size("dp")
    nz, ny, nx = sides_of(n)
    pairs = []
    for source in range(n):
        z, y, x = change(source // (ny * nx), source // nx % ny, source % nx)
        pairs.append((source, (z * ny + y) * nx + x))
    return lax.ppermute(values, "dp", pairs)


def joined(own, got, own_first):
    return jnp.where(own_first, jnp.concatenate([own, got]), jnp.concatenate([got, own]))


def weight_of_chip(weight):
    tn, j = lax.axis_size("tensor"), lax.axis_index("tensor")
    return joined(weight, lax.ppermute(weight, "tensor", [(a, a ^ 1) for a in range(tn)]), j % 2 == 0)


def weight_of_place(weight):
    n, tn = lax.axis_size("dp"), lax.axis_size("tensor")
    nx = sides_of(n)[2]
    j, x = lax.axis_index("tensor"), lax.axis_index("dp") % nx
    weight = joined(weight, lax.ppermute(weight, "tensor", [(a, a ^ 2) for a in range(tn)]), j < 2)
    if nx > 1:
        weight = joined(weight, moved(weight, lambda z, y, x: (z, y, x ^ 1)), x == 0)
    return weight


def weight_along_z(weight):
    n, tn = lax.axis_size("dp"), lax.axis_size("tensor")
    nz, ny, nx = sides_of(n)
    if nz == 1:
        half = weight.shape[0] // (2 * tn)
        j = lax.axis_index("tensor")
        return [lax.dynamic_slice_in_dim(weight, (2 * j + h) * half, half) for h in range(2)]
    out = []
    for m in range(2):
        pairs = []
        for z in range(nz):
            for rest in range(ny * nx):
                for t in range(tn):
                    to = tn * ((z % 2) ^ m) + t
                    pairs.append(((z * ny * nx + rest) * tn + t, (to * ny * nx + rest) * tn + z // 2))
        out.append(lax.ppermute(weight, ("dp", "tensor"), pairs))
    return out


def weight_once(parts):
    nz, ny, _ = sides_of(lax.axis_size("dp"))
    if ny == 1:
        return [[part] for part in parts]
    half = nz // 2
    return [
        [part, moved(part, lambda z, y, x: (z, y ^ EXCHANGES[z // half ^ m][0], x))]
        for m, part in enumerate(parts)]


def weight_twice(parts):
    nz, ny, _ = sides_of(lax.axis_size("dp"))
    if ny == 1:
        return parts
    half = nz // 2
    return [
        part + [moved(chunk, lambda z, y, x: (z, y ^ EXCHANGES[z // half ^ m][1], x)) for chunk in part]
        for m, part in enumerate(parts)]


KEPT = ((0, 3), (0, 1))
SENT = ((1, 2), (3, 2))
EXCHANGES = ((1, 3), (3, 1))


def reduce_once(kept, sent):
    if sides_of(lax.axis_size("dp"))[1] == 1:
        return [(keep[0], None) for keep in kept]
    got = [moved(send, lambda z, y, x: (z, y ^ first, x)) for send, (first, _) in zip(sent, EXCHANGES)]
    got = lax.optimization_barrier(got)
    return [(keep[0] + part[0].astype(F32), (keep[1] + part[1].astype(F32)).astype(BF16)) for keep, part in zip(kept, got)]


def reduce_twice(halves):
    if sides_of(lax.axis_size("dp"))[1] == 1:
        return jnp.concatenate([own for own, _ in halves])
    got = [moved(other, lambda z, y, x: (z, y ^ second, x)) for (_, other), (_, second) in zip(halves, EXCHANGES)]
    return jnp.concatenate([own + part.astype(F32) for (own, _), part in zip(halves, got)])


def reduce_grad(grad):
    n, tn = lax.axis_size("dp"), lax.axis_size("tensor")
    nz, ny, nx = sides_of(n)
    columns = grad.shape[-1]
    if nz > 1:
        grad = lax.all_to_all(grad.astype(BF16), "dp", 0, 0, tiled=True, axis_index_groups=groups_along(n, 0))
        grad = jnp.sum(grad.reshape(nz, -1, columns).astype(F32), axis=0)
    rows = grad.shape[0] // nx
    order = block_order(n, tn)
    x = lax.axis_index("dp") % nx
    total = None
    for turn in range(nx):
        pairs = []
        for z in range(nz):
            for y in range(ny):
                for x0 in range(nx):
                    for j in range(tn):
                        block = j * n + int(order[y, z, (x0 + turn) % nx])
                        pairs.append((((z * ny + y) * nx + x0) * tn + j, block))
        part = lax.dynamic_slice(grad, ((x + turn) % nx * rows, 0), (rows, columns))
        part = lax.ppermute(part, ("dp", "tensor"), pairs)
        total = part if total is None else total + part
    return total


def segment_start(places, lengths_ref):
    end = jnp.int32(0)
    start = jnp.zeros_like(places)
    for s in range(lengths_ref.shape[1]):
        end = end + lengths_ref[0, s]
        start = jnp.where(places >= end, end, start)
    return start


def column(row):
    n = row.shape[-1]
    eye = lax.broadcasted_iota(jnp.int32, (n, n), 0) == lax.broadcasted_iota(jnp.int32, (n, n), 1)
    return jnp.sum(jnp.where(eye, row, 0.0), axis=1, keepdims=True)


def lane_sums(values):
    return lax.dot_general(
        jnp.ones((8, values.shape[1]), F32), values, (((1,), (1,)), ((), ())),
        precision=lax.Precision.HIGHEST, preferred_element_type=F32)


def folded_square_sum(values):
    total = None
    for c in range(0, values.shape[1], 128):
        piece = values[:, c:c + 128]
        total = piece * piece if total is None else total + piece * piece
    return total


def features_kernel(tn, place_ref, low_ref, mid_ref, gain_ref, *outs):
    j = place_ref[0]
    width = low_ref.shape[1]
    piece = width // tn
    step = 1024

    def rms_scale(ref):
        total = None
        for c in range(0, width, step):
            part = folded_square_sum(ref[:, c:c + step].astype(F32))
            total = part if total is None else total + part
        return lax.rsqrt(jnp.sum(total, axis=1, keepdims=True) / width + EPSILON)

    low_scale = rms_scale(low_ref)
    mid_scale = rms_scale(mid_ref)
    for s, out in enumerate(outs):
        first = pl.multiple_of((j ^ s) * piece, piece)
        for c in range(0, piece, 512):
            at = pl.ds(first + c, 512)
            value = (low_ref[:, at].astype(F32) * low_scale * gain_ref[0:1, at]
                     + mid_ref[:, at].astype(F32) * mid_scale * gain_ref[1:2, at])
            out[:, c:c + 512] = value.astype(BF16)


def features(place, low, mid, gain, tn):
    rows, width = low.shape
    block = 16
    piece = width // tn
    return pl.pallas_call(
        functools.partial(features_kernel, tn),
        grid=(rows // block,),
        in_specs=[
            SMEM,
            pl.BlockSpec((block, width), lambda b: (b, 0)),
            pl.BlockSpec((block, width), lambda b: (b, 0)),
            pl.BlockSpec(gain.shape, lambda b: (0, 0)),
        ],
        out_specs=[pl.BlockSpec((block, piece), lambda b: (b, 0))] * tn,
        out_shape=[jax.ShapeDtypeStruct((rows, piece), BF16)] * tn,
        compiler_params=pltpu.CompilerParams(vmem_limit_bytes=FEATURES_LIMIT),
        cost_estimate=pl.CostEstimate(flops=10 * rows * width, bytes_accessed=6 * rows * width, transcendentals=0),
        name="features",
    )(place, low, mid, gain)


def attend_kernel(window, lengths_ref, query_ref, key_ref, value_ref, high_ref, square_ref):
    block = query_ref.shape[0]
    pack = key_ref.shape[0]
    b = pl.program_id(0)
    first = pl.multiple_of(jnp.clip(b * block - (window - block), 0, pack - window), block)
    query_places = b * block + lax.broadcasted_iota(jnp.int32, (block, window), 0)
    key_places = first + lax.broadcasted_iota(jnp.int32, (block, window), 1)
    allowed = (key_places <= query_places) & (key_places >= segment_start(query_places, lengths_ref))
    bias = jnp.where(allowed, 0.0, -1e30).astype(F32)
    group = (query_ref.shape[1] // HD) // (key_ref.shape[1] // HD)
    squares = jnp.zeros((block, HD), F32)
    ones = jnp.ones((window, HD), BF16)
    scale = math.log2(math.e) / math.sqrt(HD)
    for g in range(key_ref.shape[1] // HD):
        key = key_ref[pl.ds(first, window), g * HD:(g + 1) * HD]
        value = jnp.concatenate([value_ref[pl.ds(first, window), g * HD:(g + 1) * HD], ones], axis=1)
        for r in range(group):
            at = slice((g * group + r) * HD, (g * group + r + 1) * HD)
            scores = lax.dot_general(query_ref[:, at], key, (((1,), (1,)), ((), ())), preferred_element_type=F32)
            scores = scores * scale + bias
            highest = jnp.max(scores, axis=1, keepdims=True)
            expo = jnp.exp2(scores - highest).astype(BF16)
            mixed = jnp.dot(expo, value, preferred_element_type=F32)
            out = (mixed[:, :HD] / mixed[:, HD:]).astype(BF16)
            high_ref[:, at] = out
            out = out.astype(F32)
            squares = squares + out * out
    square_ref[...] = lane_sums(squares)


def attend(lengths, queries, keys, values):
    pack, width = queries.shape
    block = 128
    window = min(pack, 256 + block)
    return pl.pallas_call(
        functools.partial(attend_kernel, window),
        grid=(pack // block,),
        in_specs=[
            SMEM,
            pl.BlockSpec((block, width), lambda b: (b, 0)),
            pl.BlockSpec(keys.shape, lambda b: (0, 0)),
            pl.BlockSpec(values.shape, lambda b: (0, 0)),
        ],
        out_specs=[
            pl.BlockSpec((block, width), lambda b: (b, 0)),
            pl.BlockSpec((8, block), lambda b: (0, b)),
        ],
        out_shape=[
            jax.ShapeDtypeStruct((pack, width), BF16),
            jax.ShapeDtypeStruct((8, pack), F32),
        ],
        compiler_params=pltpu.CompilerParams(vmem_limit_bytes=VMEM_LIMIT),
        cost_estimate=pl.CostEstimate(
            flops=4 * pack * window * width, bytes_accessed=4 * pack * width,
            transcendentals=pack * window * width // HD),
        name="attend",
    )(lengths, queries, keys, values)


def chosen(place_ref, lengths_ref, offset, rows, lead):
    target = place_ref[0] * rows + lax.broadcasted_iota(jnp.int32, (rows, rows + lead), 0)
    source = place_ref[0] * rows - lead + lax.broadcasted_iota(jnp.int32, (rows, rows + lead), 1)
    hit = (source == target - offset) & (source >= segment_start(target, lengths_ref))
    return jnp.where(hit, 1.0, 0.0).astype(BF16)


def fold_kernel(place_ref, lengths_ref, offsets_ref, cotangent_ref, out_ref):
    steps, rows, width = cotangent_ref.shape
    total = None
    for s in range(steps):
        pick = chosen(place_ref, lengths_ref, offsets_ref[s], rows, OFFMAX)
        part = lax.dot_general(pick, cotangent_ref[s], (((0,), (0,)), ((), ())), preferred_element_type=F32)
        total = part if total is None else total + part
    out_ref[...] = total.astype(BF16)


def fold(place, lengths, offsets, cotangent):
    steps, rows, width = cotangent.shape
    return pl.pallas_call(
        fold_kernel,
        in_specs=[SMEM, SMEM, SMEM, VMEM],
        out_specs=VMEM,
        out_shape=jax.ShapeDtypeStruct((rows + OFFMAX, width), BF16),
        compiler_params=pltpu.CompilerParams(vmem_limit_bytes=VMEM_LIMIT),
        cost_estimate=pl.CostEstimate(flops=2 * steps * rows * 160 * width, bytes_accessed=2 * steps * rows * width, transcendentals=0),
        name="fold",
    )(place, lengths, offsets, cotangent)


def merge_kernel(width, tn, place_ref, gain_ref, high_ref, *refs):
    parts, square_refs, out_ref, out_square_ref = refs[:tn], refs[tn:-2], refs[-2], refs[-1]
    j = place_ref[0]
    rows = parts[0].shape[0]
    piece = high_ref.shape[1]
    squares = square_refs[0][...]
    for ref in square_refs[1:]:
        squares = squares + ref[...]
    scales = lax.rsqrt(squares / width + EPSILON)
    for b in range(tn):
        out_square_ref[:, b * rows:(b + 1) * rows] = scales[:, b * rows:(b + 1) * rows]
    for s in range(tn):
        first = pl.multiple_of((j ^ s) * rows, rows)
        at = pl.ds(first, rows)
        scale = column(out_square_ref[0:1, at])
        total = jnp.zeros((rows, 128), F32)
        for c in range(0, piece, 128):
            cols = slice(c, c + 128)
            gain = gain_ref[2:3, pl.ds(pl.multiple_of(j * piece + c, 128), 128)]
            merged = (parts[s][:, cols].astype(F32) + high_ref[at, cols].astype(F32) * scale * gain).astype(BF16)
            out_ref[at, cols] = merged
            merged = merged.astype(F32)
            total = total + merged * merged
        out_square_ref[:, at] = lane_sums(total)


def merge(place, gain, high, parts, squares, width):
    pack, piece = high.shape
    tn = len(parts)
    return pl.pallas_call(
        functools.partial(merge_kernel, width, tn),
        in_specs=[SMEM] + [VMEM] * (2 + tn + len(squares)),
        out_specs=[VMEM, VMEM],
        out_shape=[
            jax.ShapeDtypeStruct((pack, piece), BF16),
            jax.ShapeDtypeStruct((8, pack), F32),
        ],
        compiler_params=pltpu.CompilerParams(vmem_limit_bytes=VMEM_LIMIT),
        cost_estimate=pl.CostEstimate(flops=8 * pack * piece, bytes_accessed=6 * pack * piece, transcendentals=0),
        name="merge",
    )(place, gain, high, *parts, *squares)


def grads(place, gain, merged, folds, squares, width, ny, tn):
    pack, piece = merged.shape
    rows = pack // tn
    vw = folds[0].shape[1]
    chunk = piece // (2 * ny)
    kept, sent = (KEPT, SENT) if ny > 1 else (((0,), (0,)), ((), ()))
    steps = [(h, s, True) for h in range(2) for s in kept[h]] + [(h, s, False) for h in range(2) for s in sent[h]]
    steps.sort(key=lambda step: step[2])
    size = chunk // (2 * tn) if ny > 1 else chunk

    def kernel(place_ref, gain_ref, merged_ref, *refs):
        fold_refs, square_refs, refs = refs[:tn], refs[tn:2 * tn], refs[2 * tn:]
        keep_refs, refs = refs[:2], refs[2:]
        send_refs, refs = refs[:2 if ny > 1 else 0], refs[2 if ny > 1 else 0:]
        hidden_ref, fold_ref = refs
        j, y = place_ref[0], place_ref[1]
        squares = square_refs[0][...]
        for s in range(1, tn):
            squares = squares + square_refs[s][...]
        scales = lax.rsqrt(squares / width + EPSILON)
        for b in range(tn):
            at = slice(b * rows, (b + 1) * rows)
            scale = column(scales[0:1, at])
            for c in range(0, piece, 128):
                cols = slice(c, c + 128)
                gain = gain_ref[:, pl.ds(pl.multiple_of(j * piece + c, 128), 128)]
                hidden_ref[at, cols] = (merged_ref[at, cols].astype(F32) * scale * gain).astype(BF16)
        fold_ref[...] = jnp.zeros_like(fold_ref)
        for s in range(tn):
            at = pl.ds(pl.multiple_of((j ^ s) * rows, rows), rows + OFFMAX)
            fold_ref[at, :] = fold_ref[at, :] + fold_refs[s][...].astype(F32)
        folded = fold_ref[OFFMAX:, :].astype(BF16)
        for h, s, keep in steps:
            at = pl.ds(pl.multiple_of(h * ny * chunk + (y ^ s) * chunk, chunk), chunk)
            part = lax.dot_general(
                hidden_ref[:, at], folded, (((0,), (0,)), ((), ())), preferred_element_type=F32)
            if size < chunk:
                part = jnp.concatenate(
                    [part[(x * tn + t) * size:(x * tn + t + 1) * size] for t in range(tn) for x in range(2)], axis=0)
            if keep:
                keep_refs[h][kept[h].index(s)] = part
            else:
                send_refs[h][sent[h].index(s)] = part.astype(BF16)

    out_shape = [jax.ShapeDtypeStruct((len(kept[h]), chunk, vw), F32) for h in range(2)]
    if ny > 1:
        out_shape += [jax.ShapeDtypeStruct((len(sent[h]), chunk, vw), BF16) for h in range(2)]
    out_shape += [jax.ShapeDtypeStruct((pack, piece), BF16)]
    out = pl.pallas_call(
        kernel,
        in_specs=[SMEM] + [VMEM] * (2 + 2 * tn),
        out_specs=[VMEM] * len(out_shape),
        out_shape=out_shape,
        scratch_shapes=[pltpu.VMEM((pack + OFFMAX, vw), F32)],
        compiler_params=pltpu.CompilerParams(vmem_limit_bytes=VMEM_LIMIT),
        cost_estimate=pl.CostEstimate(flops=2 * pack * piece * vw, bytes_accessed=8 * pack * piece, transcendentals=0),
        name="grads",
    )(place, gain, merged, *folds, *squares)
    return out[:2], out[2:-1] if ny > 1 else (None, None), out[-1]


def project(place, hidden, weights, tn):
    pack, piece = hidden.shape
    rows = pack // tn
    part, vw = weights[0][0].shape
    count = len(weights[0])

    def kernel(place_ref, hidden_ref, *refs):
        weight_refs, value_refs, total_ref = refs[:2 * count], refs[2 * count:-1], refs[-1]
        j, y, half = place_ref[0], place_ref[1], place_ref[2]
        total_ref[0:OFFMAX, :] = jnp.zeros((OFFMAX, vw), F32)
        block = 128
        for c in range(0, pack, block):
            total = None
            for m in range(2):
                h = half ^ m
                for s, at in enumerate((0, 1 + 2 * h, 3 - 2 * h, 2)[:count]):
                    at = pl.ds(pl.multiple_of(h * count * part + (y ^ at) * part, part), part)
                    term = jnp.dot(
                        hidden_ref[c:c + block, at], weight_refs[m * count + s][...], preferred_element_type=F32)
                    total = term if total is None else total + term
            total_ref[OFFMAX + c:OFFMAX + c + block, :] = total
        for s in range(tn):
            at = pl.ds(pl.multiple_of((j ^ s) * rows, rows), rows + OFFMAX)
            value_refs[s][...] = total_ref[at, :].astype(value_refs[s].dtype)

    return pl.pallas_call(
        kernel,
        in_specs=[SMEM] + [VMEM] * (1 + 2 * count),
        out_specs=[VMEM] * tn,
        out_shape=[jax.ShapeDtypeStruct((rows + OFFMAX, vw), F32 if s == 0 else BF16) for s in range(tn)],
        scratch_shapes=[pltpu.VMEM((pack + OFFMAX, vw), F32)],
        compiler_params=pltpu.CompilerParams(vmem_limit_bytes=VMEM_LIMIT),
        cost_estimate=pl.CostEstimate(flops=2 * pack * piece * vw, bytes_accessed=4 * pack * piece, transcendentals=0),
        name="project",
    )(place, hidden, *weights[0], *weights[1])


def spread(place, lengths, offsets, parts):
    rows, vw = parts[0].shape[0] - OFFMAX, parts[0].shape[1]

    def kernel(place_ref, lengths_ref, offsets_ref, *refs):
        parts_refs, out_ref = refs[:-1], refs[-1]
        total = None
        for ref in parts_refs:
            part = ref[...].astype(F32)
            total = part if total is None else total + part
        total = total.astype(BF16)
        for s in range(STEPS):
            pick = chosen(place_ref, lengths_ref, offsets_ref[s], rows, OFFMAX)
            out_ref[s] = jnp.dot(pick, total, preferred_element_type=F32).astype(BF16)

    return pl.pallas_call(
        kernel,
        in_specs=[SMEM] * 3 + [VMEM] * len(parts),
        out_specs=VMEM,
        out_shape=jax.ShapeDtypeStruct((STEPS, rows, vw), BF16),
        compiler_params=pltpu.CompilerParams(vmem_limit_bytes=VMEM_LIMIT),
        cost_estimate=pl.CostEstimate(flops=2 * STEPS * rows * 160 * vw, bytes_accessed=8 * STEPS * rows * vw, transcendentals=0),
        name="spread",
    )(place, lengths, offsets, *parts)


def body(
    target_queries,
    target_keys,
    target_values,
    low_feature,
    mid_feature,
    merging_gain,
    draft_gain,
    draft_weight,
    cotangent,
    doc_lengths,
    step_offsets,
):
    n = lax.axis_size("dp")
    tn = lax.axis_size("tensor")
    j = lax.axis_index("tensor")
    i = lax.axis_index("dp")
    flat = i * tn + j
    nz, ny, nx = sides_of(n)
    place = jnp.stack([j, i // nx % ny, i // (ny * nx) // max(1, nz // 2)]).astype(jnp.int32)
    width = low_feature.shape[1]
    piece = width // tn
    pack = target_queries.shape[0]
    both = ("dp", "tensor")

    def swapped(values, s):
        return lax.ppermute(values, "tensor", [(a, a ^ s) for a in range(tn)])

    sent = features(place, low_feature, mid_feature, merging_gain, tn)
    parts = [sent[0]] + [swapped(sent[s], s) for s in range(1, tn)]

    high, squares = attend(doc_lengths, target_queries, target_keys, target_values)
    own_weight, cotangent, high = lax.optimization_barrier((draft_weight, cotangent, high))
    squares = squares + swapped(squares, 1)
    own_weight = weight_of_chip(own_weight)
    squares, own_weight = lax.optimization_barrier((squares, own_weight))
    squares = [squares, swapped(squares, 2)]
    folded = fold(place, doc_lengths, step_offsets, cotangent)
    across, beside = swapped(folded, 2), swapped(folded, 1)
    merged, squares = merge(place, merging_gain, high, parts, squares, width)
    across, merged = lax.optimization_barrier((across, merged))
    folds = [folded, beside, across, swapped(across, 1)]
    squares = [squares] + [swapped(squares, s) for s in range(1, tn)]
    weights = weight_once(weight_along_z(weight_of_place(own_weight)))
    kept, cut, hidden = grads(place, draft_gain.reshape(1, width), merged, folds, squares, width, ny, tn)
    halves = reduce_once(kept, cut)
    weights, own = lax.optimization_barrier((weights, [half[0] for half in halves]))
    halves = [(mine, other) for mine, (_, other) in zip(own, halves)]
    weight_grad = reduce_grad(reduce_twice(halves))
    weights = weight_twice(weights)

    values = project(place, hidden, weights, tn)
    values = [values[0]] + [swapped(values[s], s) for s in range(1, tn)]
    draft_values = spread(place, doc_lengths, step_offsets, values)

    rows = weight_grad.shape[0]
    gain = lax.dynamic_slice(draft_gain, (flat * rows,), (rows,))
    gain_grad = jnp.sum(weight_grad * draft_weight.astype(F32), axis=1) / gain
    return (draft_values, weight_grad, gain_grad)


def solution(mesh):
    placed = (
        P("dp", "tensor"),
        P("dp", "tensor"),
        P("dp", "tensor"),
        P(("dp", "tensor"), None),
        P(("dp", "tensor"), None),
        P(),
        P(),
        P(("dp", "tensor"), None),
        P(None, ("dp", "tensor"), None),
        P("dp", None),
        P(),
    )
    return jax.shard_map(
        body,
        mesh=mesh,
        in_specs=placed,
        out_specs=(P(None, ("dp", "tensor"), None), P(("dp", "tensor"), None), P(("dp", "tensor"))),
        check_vma=False,
    )
```

```python
import functools
import math

import jax
import jax.numpy as jnp
import numpy as np
from jax import lax
from jax.experimental import pallas as pl
from jax.experimental.pallas import tpu as pltpu
from jax.sharding import PartitionSpec as P

HD = 128
STEPS = 3
OFFMAX = 32
EPSILON = 1e-05
VMEM_LIMIT = 20 * 1024 * 1024
FEATURES_LIMIT = 60 * 1024 * 1024

VMEM = pl.BlockSpec(memory_space=pltpu.VMEM)
SMEM = pl.BlockSpec(memory_space=pltpu.SMEM)
HBM = pl.BlockSpec(memory_space=pltpu.HBM)
F32 = jnp.float32
BF16 = jnp.bfloat16


SIDES = {64: (8, 4, 2)}


def sides_of(n):
    return SIDES.get(n, (1, 1, n))


def groups_along(n, *sides):
    sizes = sides_of(n)
    where = np.moveaxis(np.arange(n).reshape(sizes), sides, range(-len(sides), 0))
    return where.reshape(-1, math.prod(sizes[side] for side in sides)).tolist()


def block_order(n, tn):
    nz, ny, nx = sides_of(n)
    order = np.arange(n).reshape(ny, nz, nx)
    if nz == 2 * tn and n == ny * nx * tn * 2:
        for y in range(ny):
            for z in range(nz):
                for x in range(nx):
                    order[y, z, x] = (((z // tn) * ny + y) * nx + x) * tn + z % tn
    return order


def moved(values, change):
    n = lax.axis_size("dp")
    nz, ny, nx = sides_of(n)
    pairs = []
    for source in range(n):
        z, y, x = change(source // (ny * nx), source // nx % ny, source % nx)
        pairs.append((source, (z * ny + y) * nx + x))
    return lax.ppermute(values, "dp", pairs)


def joined(own, got, own_first):
    return jnp.where(own_first, jnp.concatenate([own, got]), jnp.concatenate([got, own]))


def weight_of_chip(weight):
    tn, j = lax.axis_size("tensor"), lax.axis_index("tensor")
    return joined(weight, lax.ppermute(weight, "tensor", [(a, a ^ 1) for a in range(tn)]), j % 2 == 0)


def weight_of_both(weight):
    nx = sides_of(lax.axis_size("dp"))[2]
    if nx == 1:
        return weight
    return joined(weight, moved(weight, lambda z, y, x: (z, y, x ^ 1)), lax.axis_index("dp") % nx == 0)


def weight_of_place(weight):
    tn, j = lax.axis_size("tensor"), lax.axis_index("tensor")
    rows, columns = weight.shape
    weight = weight.reshape(sides_of(lax.axis_size("dp"))[2], -1, columns)
    got = lax.ppermute(weight, "tensor", [(a, a ^ 2) for a in range(tn)])
    weight = jnp.where(j < 2, jnp.concatenate([weight, got], 1), jnp.concatenate([got, weight], 1))
    return weight.reshape(2 * rows, columns)


def weight_along_z(weight):
    n, tn = lax.axis_size("dp"), lax.axis_size("tensor")
    nz, ny, nx = sides_of(n)
    if nz == 1:
        half = weight.shape[0] // (2 * tn)
        j = lax.axis_index("tensor")
        return [lax.dynamic_slice_in_dim(weight, (2 * j + h) * half, half) for h in range(2)]
    out = []
    for m in range(2):
        pairs = []
        for z in range(nz):
            for rest in range(ny * nx):
                for t in range(tn):
                    to = tn * ((z % 2) ^ m) + t
                    pairs.append(((z * ny * nx + rest) * tn + t, (to * ny * nx + rest) * tn + z // 2))
        out.append(lax.ppermute(weight, ("dp", "tensor"), pairs))
    return out


def weight_once(parts):
    nz, ny, _ = sides_of(lax.axis_size("dp"))
    if ny == 1:
        return [[part] for part in parts]
    half = nz // 2
    return [
        [part, moved(part, lambda z, y, x: (z, y ^ EXCHANGES[z // half ^ m][0], x))]
        for m, part in enumerate(parts)]


def weight_twice(parts):
    nz, ny, _ = sides_of(lax.axis_size("dp"))
    if ny == 1:
        return parts
    half = nz // 2
    return [
        part + [moved(chunk, lambda z, y, x: (z, y ^ EXCHANGES[z // half ^ m][1], x)) for chunk in part]
        for m, part in enumerate(parts)]


KEPT = ((0, 3), (0, 1))
SENT = ((1, 2), (3, 2))
EXCHANGES = ((1, 3), (3, 1))


def reduce_once(kept, sent):
    if sides_of(lax.axis_size("dp"))[1] == 1:
        return [(keep[0], None) for keep in kept]
    got = [moved(send, lambda z, y, x: (z, y ^ first, x)) for send, (first, _) in zip(sent, EXCHANGES)]
    got = lax.optimization_barrier(got)
    return [(keep[0] + part[0].astype(F32), (keep[1] + part[1].astype(F32)).astype(BF16)) for keep, part in zip(kept, got)]


def reduce_twice(halves):
    if sides_of(lax.axis_size("dp"))[1] == 1:
        return jnp.concatenate([own for own, _ in halves])
    got = [moved(other, lambda z, y, x: (z, y ^ second, x)) for (_, other), (_, second) in zip(halves, EXCHANGES)]
    return jnp.concatenate([own + part.astype(F32) for (own, _), part in zip(halves, got)])


def reduce_along_z(grad):
    n = lax.axis_size("dp")
    nz = sides_of(n)[0]
    if nz == 1:
        return grad
    columns = grad.shape[-1]
    grad = lax.all_to_all(grad.astype(BF16), "dp", 0, 0, tiled=True, axis_index_groups=groups_along(n, 0))
    return jnp.sum(grad.reshape(nz, -1, columns).astype(F32), axis=0)


def reduce_to_owner(grad):
    n, tn = lax.axis_size("dp"), lax.axis_size("tensor")
    nz, ny, nx = sides_of(n)
    rows, columns = grad.shape[0] // nx, grad.shape[1]
    order = block_order(n, tn)
    x = lax.axis_index("dp") % nx
    total = None
    for turn in range(nx):
        pairs = []
        for z in range(nz):
            for y in range(ny):
                for x0 in range(nx):
                    for j in range(tn):
                        block = j * n + int(order[y, z, (x0 + turn) % nx])
                        pairs.append((((z * ny + y) * nx + x0) * tn + j, block))
        part = lax.dynamic_slice(grad, ((x + turn) % nx * rows, 0), (rows, columns))
        part = lax.ppermute(part, ("dp", "tensor"), pairs)
        total = part if total is None else total + part
    return total


def segment_start(places, lengths_ref):
    end = jnp.int32(0)
    start = jnp.zeros_like(places)
    for s in range(lengths_ref.shape[1]):
        end = end + lengths_ref[0, s]
        start = jnp.where(places >= end, end, start)
    return start


def column(row):
    n = row.shape[-1]
    eye = lax.broadcasted_iota(jnp.int32, (n, n), 0) == lax.broadcasted_iota(jnp.int32, (n, n), 1)
    return jnp.sum(jnp.where(eye, row, 0.0), axis=1, keepdims=True)


def lane_sums(values):
    return lax.dot_general(
        jnp.ones((8, values.shape[1]), F32), values, (((1,), (1,)), ((), ())),
        precision=lax.Precision.HIGHEST, preferred_element_type=F32)


def folded_square_sum(values):
    total = None
    for c in range(0, values.shape[1], 128):
        piece = values[:, c:c + 128]
        total = piece * piece if total is None else total + piece * piece
    return total


def features_kernel(tn, place_ref, low_ref, mid_ref, gain_ref, *outs):
    j = place_ref[0]
    width = low_ref.shape[1]
    piece = width // tn
    step = 1024

    def rms_scale(ref):
        total = None
        for c in range(0, width, step):
            part = folded_square_sum(ref[:, c:c + step].astype(F32))
            total = part if total is None else total + part
        return lax.rsqrt(jnp.sum(total, axis=1, keepdims=True) / width + EPSILON)

    low_scale = rms_scale(low_ref)
    mid_scale = rms_scale(mid_ref)
    for s, out in enumerate(outs):
        first = pl.multiple_of((j ^ s) * piece, piece)
        for c in range(0, piece, 512):
            at = pl.ds(first + c, 512)
            value = (low_ref[:, at].astype(F32) * low_scale * gain_ref[0:1, at]
                     + mid_ref[:, at].astype(F32) * mid_scale * gain_ref[1:2, at])
            out[:, c:c + 512] = value.astype(BF16)


def features(place, low, mid, gain, tn):
    rows, width = low.shape
    block = 16
    piece = width // tn
    return pl.pallas_call(
        functools.partial(features_kernel, tn),
        grid=(rows // block,),
        in_specs=[
            SMEM,
            pl.BlockSpec((block, width), lambda b: (b, 0)),
            pl.BlockSpec((block, width), lambda b: (b, 0)),
            pl.BlockSpec(gain.shape, lambda b: (0, 0)),
        ],
        out_specs=[pl.BlockSpec((block, piece), lambda b: (b, 0))] * tn,
        out_shape=[jax.ShapeDtypeStruct((rows, piece), BF16)] * tn,
        compiler_params=pltpu.CompilerParams(vmem_limit_bytes=FEATURES_LIMIT),
        cost_estimate=pl.CostEstimate(flops=10 * rows * width, bytes_accessed=6 * rows * width, transcendentals=0),
        name="features",
    )(place, low, mid, gain)


def attend_kernel(window, lengths_ref, query_ref, key_ref, value_ref, high_ref, square_ref):
    block = query_ref.shape[0]
    pack = key_ref.shape[0]
    b = pl.program_id(0)
    first = pl.multiple_of(jnp.clip(b * block - (window - block), 0, pack - window), block)
    query_places = b * block + lax.broadcasted_iota(jnp.int32, (block, window), 0)
    key_places = first + lax.broadcasted_iota(jnp.int32, (block, window), 1)
    allowed = (key_places <= query_places) & (key_places >= segment_start(query_places, lengths_ref))
    bias = jnp.where(allowed, 0.0, -1e30).astype(F32)
    group = (query_ref.shape[1] // HD) // (key_ref.shape[1] // HD)
    squares = jnp.zeros((block, HD), F32)
    ones = jnp.ones((window, HD), BF16)
    scale = math.log2(math.e) / math.sqrt(HD)
    for g in range(key_ref.shape[1] // HD):
        key = key_ref[pl.ds(first, window), g * HD:(g + 1) * HD]
        value = jnp.concatenate([value_ref[pl.ds(first, window), g * HD:(g + 1) * HD], ones], axis=1)
        for r in range(group):
            at = slice((g * group + r) * HD, (g * group + r + 1) * HD)
            scores = lax.dot_general(query_ref[:, at], key, (((1,), (1,)), ((), ())), preferred_element_type=F32)
            scores = scores * scale + bias
            highest = jnp.max(scores, axis=1, keepdims=True)
            expo = jnp.exp2(scores - highest).astype(BF16)
            mixed = jnp.dot(expo, value, preferred_element_type=F32)
            out = (mixed[:, :HD] / mixed[:, HD:]).astype(BF16)
            high_ref[:, at] = out
            out = out.astype(F32)
            squares = squares + out * out
    square_ref[...] = lane_sums(squares)


def attend(lengths, queries, keys, values):
    pack, width = queries.shape
    block = 128
    window = min(pack, 256 + block)
    return pl.pallas_call(
        functools.partial(attend_kernel, window),
        grid=(pack // block,),
        in_specs=[
            SMEM,
            pl.BlockSpec((block, width), lambda b: (b, 0)),
            pl.BlockSpec(keys.shape, lambda b: (0, 0)),
            pl.BlockSpec(values.shape, lambda b: (0, 0)),
        ],
        out_specs=[
            pl.BlockSpec((block, width), lambda b: (b, 0)),
            pl.BlockSpec((8, block), lambda b: (0, b)),
        ],
        out_shape=[
            jax.ShapeDtypeStruct((pack, width), BF16),
            jax.ShapeDtypeStruct((8, pack), F32),
        ],
        compiler_params=pltpu.CompilerParams(vmem_limit_bytes=VMEM_LIMIT),
        cost_estimate=pl.CostEstimate(
            flops=4 * pack * window * width, bytes_accessed=4 * pack * width,
            transcendentals=pack * window * width // HD),
        name="attend",
    )(lengths, queries, keys, values)


def chosen(place_ref, lengths_ref, offset, rows, lead):
    target = place_ref[0] * rows + lax.broadcasted_iota(jnp.int32, (rows, rows + lead), 0)
    source = place_ref[0] * rows - lead + lax.broadcasted_iota(jnp.int32, (rows, rows + lead), 1)
    hit = (source == target - offset) & (source >= segment_start(target, lengths_ref))
    return jnp.where(hit, 1.0, 0.0).astype(BF16)


def fold_kernel(place_ref, lengths_ref, offsets_ref, cotangent_ref, out_ref):
    steps, rows, width = cotangent_ref.shape
    total = None
    for s in range(steps):
        pick = chosen(place_ref, lengths_ref, offsets_ref[s], rows, OFFMAX)
        part = lax.dot_general(pick, cotangent_ref[s], (((0,), (0,)), ((), ())), preferred_element_type=F32)
        total = part if total is None else total + part
    out_ref[...] = total.astype(BF16)


def fold(place, lengths, offsets, cotangent):
    steps, rows, width = cotangent.shape
    return pl.pallas_call(
        fold_kernel,
        in_specs=[SMEM, SMEM, SMEM, VMEM],
        out_specs=VMEM,
        out_shape=jax.ShapeDtypeStruct((rows + OFFMAX, width), BF16),
        compiler_params=pltpu.CompilerParams(vmem_limit_bytes=VMEM_LIMIT),
        cost_estimate=pl.CostEstimate(flops=2 * steps * rows * 160 * width, bytes_accessed=2 * steps * rows * width, transcendentals=0),
        name="fold",
    )(place, lengths, offsets, cotangent)


def merge_kernel(width, tn, place_ref, gain_ref, high_ref, *refs):
    parts, square_refs, (far_ref, out_square_ref, out_ref, sems) = refs[:tn], refs[tn:-4], refs[-4:]
    copies = []
    j = place_ref[0]
    rows = parts[0].shape[0]
    piece = high_ref.shape[1]
    squares = square_refs[0][...]
    for ref in square_refs[1:]:
        squares = squares + ref[...]
    scales = lax.rsqrt(squares / width + EPSILON)
    for b in range(tn):
        out_square_ref[:, b * rows:(b + 1) * rows] = scales[:, b * rows:(b + 1) * rows]
    for s in range(tn):
        first = pl.multiple_of((j ^ s) * rows, rows)
        at = pl.ds(first, rows)
        scale = column(out_square_ref[0:1, at])
        total = jnp.zeros((rows, 128), F32)
        for c in range(0, piece, 128):
            cols = slice(c, c + 128)
            gain = gain_ref[2:3, pl.ds(pl.multiple_of(j * piece + c, 128), 128)]
            merged = (parts[s][:, cols].astype(F32) + high_ref[at, cols].astype(F32) * scale * gain).astype(BF16)
            out_ref[at, cols] = merged
            merged = merged.astype(F32)
            total = total + merged * merged
        copy = pltpu.make_async_copy(out_ref.at[at, :], far_ref.at[at, :], sems.at[s])
        copy.start()
        copies.append(copy)
        out_square_ref[:, at] = lane_sums(total)
    for copy in copies:
        copy.wait()


def merge(place, gain, high, parts, squares, width):
    pack, piece = high.shape
    tn = len(parts)
    return pl.pallas_call(
        functools.partial(merge_kernel, width, tn),
        in_specs=[SMEM] + [VMEM] * (2 + tn + len(squares)),
        out_specs=[HBM, VMEM],
        out_shape=[
            jax.ShapeDtypeStruct((pack, piece), BF16),
            jax.ShapeDtypeStruct((8, pack), F32),
        ],
        scratch_shapes=[pltpu.VMEM((pack, piece), BF16), pltpu.SemaphoreType.DMA((tn,))],
        compiler_params=pltpu.CompilerParams(vmem_limit_bytes=VMEM_LIMIT),
        cost_estimate=pl.CostEstimate(flops=8 * pack * piece, bytes_accessed=6 * pack * piece, transcendentals=0),
        name="merge",
    )(place, gain, high, *parts, *squares)


def grads(place, gain, merged, folds, squares, width, ny, tn):
    pack, piece = merged.shape
    rows = pack // tn
    vw = folds[0].shape[1]
    chunk = piece // (2 * ny)
    kept, sent = (KEPT, SENT) if ny > 1 else (((0,), (0,)), ((), ()))
    steps = [(h, s, True) for h in range(2) for s in kept[h]] + [(h, s, False) for h in range(2) for s in sent[h]]
    steps.sort(key=lambda step: step[2])
    size = chunk // (2 * tn) if ny > 1 else chunk

    def kernel(place_ref, gain_ref, merged_ref, *refs):
        fold_refs, square_refs, refs = refs[:tn], refs[tn:2 * tn], refs[2 * tn:]
        keep_refs, refs = refs[:2], refs[2:]
        send_refs, refs = refs[:2 if ny > 1 else 0], refs[2 if ny > 1 else 0:]
        hidden_ref, fold_ref, near_ref, near_folds, near_cut, sems = refs
        coming = [
            pltpu.make_async_copy(
                merged_ref.at[b * rows:(b + 1) * rows, :], near_ref.at[b * rows:(b + 1) * rows, :], sems.at[b])
            for b in range(tn)]
        folds_coming = [
            pltpu.make_async_copy(fold_refs[s], near_folds.at[s], sems.at[tn + s]) for s in range(tn)]
        for copy in coming + folds_coming:
            copy.start()
        j, y = place_ref[0], place_ref[1]
        squares = square_refs[0][...]
        for s in range(1, tn):
            squares = squares + square_refs[s][...]
        scales = lax.rsqrt(squares / width + EPSILON)
        for b in range(tn):
            at = slice(b * rows, (b + 1) * rows)
            scale = column(scales[0:1, at])
            coming[b].wait()
            for c in range(0, piece, 128):
                cols = slice(c, c + 128)
                gain = gain_ref[:, pl.ds(pl.multiple_of(j * piece + c, 128), 128)]
                hidden_ref[at, cols] = (near_ref[at, cols].astype(F32) * scale * gain).astype(BF16)
        fold_ref[...] = jnp.zeros_like(fold_ref)
        for s in range(tn):
            at = pl.ds(pl.multiple_of((j ^ s) * rows, rows), rows + OFFMAX)
            folds_coming[s].wait()
            fold_ref[at, :] = fold_ref[at, :] + near_folds[s].astype(F32)
        folded = fold_ref[OFFMAX:, :].astype(BF16)
        going = []
        for h, s, keep in steps:
            at = pl.ds(pl.multiple_of(h * ny * chunk + (y ^ s) * chunk, chunk), chunk)
            part = lax.dot_general(
                hidden_ref[:, at], folded, (((0,), (0,)), ((), ())), preferred_element_type=F32)
            if size < chunk:
                part = jnp.concatenate(
                    [part[(x * tn + t) * size:(x * tn + t + 1) * size] for t in range(tn) for x in range(2)], axis=0)
            if keep:
                keep_refs[h][kept[h].index(s)] = part
            else:
                k = sent[h].index(s)
                near_cut[h, k] = part.astype(BF16)
                copy = pltpu.make_async_copy(near_cut.at[h, k], send_refs[h].at[k], sems.at[2 * tn + 2 * h + k])
                copy.start()
                going.append(copy)
        for copy in going:
            copy.wait()

    out_shape = [jax.ShapeDtypeStruct((len(kept[h]), chunk, vw), F32) for h in range(2)]
    if ny > 1:
        out_shape += [jax.ShapeDtypeStruct((len(sent[h]), chunk, vw), BF16) for h in range(2)]
    out_shape += [jax.ShapeDtypeStruct((pack, piece), BF16)]
    out = pl.pallas_call(
        kernel,
        in_specs=[SMEM, VMEM, HBM] + [HBM] * tn + [VMEM] * tn,
        out_specs=[VMEM] * 2 + ([HBM] * 2 if ny > 1 else []) + [VMEM],
        out_shape=out_shape,
        scratch_shapes=[
            pltpu.VMEM((pack + OFFMAX, vw), F32),
            pltpu.VMEM((pack, piece), BF16),
            pltpu.VMEM((tn, rows + OFFMAX, vw), BF16),
            pltpu.VMEM((2, 2, chunk if ny > 1 else 16, vw), BF16),
            pltpu.SemaphoreType.DMA((2 * tn + 4,)),
        ],
        compiler_params=pltpu.CompilerParams(vmem_limit_bytes=VMEM_LIMIT),
        cost_estimate=pl.CostEstimate(flops=2 * pack * piece * vw, bytes_accessed=8 * pack * piece, transcendentals=0),
        name="grads",
    )(place, gain, merged, *folds, *squares)
    return out[:2], out[2:-1] if ny > 1 else (None, None), out[-1]


def project(place, hidden, weights, tn):
    pack, piece = hidden.shape
    rows = pack // tn
    part, vw = weights[0][0].shape
    count = len(weights[0])

    def kernel(place_ref, hidden_ref, *refs):
        weight_refs, value_refs, total_ref = refs[:2 * count], refs[2 * count:-1], refs[-1]
        j, y, half = place_ref[0], place_ref[1], place_ref[2]
        total_ref[0:OFFMAX, :] = jnp.zeros((OFFMAX, vw), F32)
        block = 128
        for c in range(0, pack, block):
            total = None
            for m in range(2):
                h = half ^ m
                for s, at in enumerate((0, 1 + 2 * h, 3 - 2 * h, 2)[:count]):
                    at = pl.ds(pl.multiple_of(h * count * part + (y ^ at) * part, part), part)
                    term = jnp.dot(
                        hidden_ref[c:c + block, at], weight_refs[m * count + s][...], preferred_element_type=F32)
                    total = term if total is None else total + term
            total_ref[OFFMAX + c:OFFMAX + c + block, :] = total
        for s in range(tn):
            at = pl.ds(pl.multiple_of((j ^ s) * rows, rows), rows + OFFMAX)
            value_refs[s][...] = total_ref[at, :].astype(value_refs[s].dtype)

    return pl.pallas_call(
        kernel,
        in_specs=[SMEM] + [VMEM] * (1 + 2 * count),
        out_specs=[VMEM] * tn,
        out_shape=[jax.ShapeDtypeStruct((rows + OFFMAX, vw), F32 if s == 0 else BF16) for s in range(tn)],
        scratch_shapes=[pltpu.VMEM((pack + OFFMAX, vw), F32)],
        compiler_params=pltpu.CompilerParams(vmem_limit_bytes=VMEM_LIMIT),
        cost_estimate=pl.CostEstimate(flops=2 * pack * piece * vw, bytes_accessed=4 * pack * piece, transcendentals=0),
        name="project",
    )(place, hidden, *weights[0], *weights[1])


def spread(place, lengths, offsets, parts):
    rows, vw = parts[0].shape[0] - OFFMAX, parts[0].shape[1]

    def kernel(place_ref, lengths_ref, offsets_ref, *refs):
        parts_refs, out_ref = refs[:-1], refs[-1]
        total = None
        for ref in parts_refs:
            part = ref[...].astype(F32)
            total = part if total is None else total + part
        total = total.astype(BF16)
        for s in range(STEPS):
            pick = chosen(place_ref, lengths_ref, offsets_ref[s], rows, OFFMAX)
            out_ref[s] = jnp.dot(pick, total, preferred_element_type=F32).astype(BF16)

    return pl.pallas_call(
        kernel,
        in_specs=[SMEM] * 3 + [VMEM] * len(parts),
        out_specs=VMEM,
        out_shape=jax.ShapeDtypeStruct((STEPS, rows, vw), BF16),
        compiler_params=pltpu.CompilerParams(vmem_limit_bytes=VMEM_LIMIT),
        cost_estimate=pl.CostEstimate(flops=2 * STEPS * rows * 160 * vw, bytes_accessed=8 * STEPS * rows * vw, transcendentals=0),
        name="spread",
    )(place, lengths, offsets, *parts)


def body(
    target_queries,
    target_keys,
    target_values,
    low_feature,
    mid_feature,
    merging_gain,
    draft_gain,
    draft_weight,
    cotangent,
    doc_lengths,
    step_offsets,
):
    n = lax.axis_size("dp")
    tn = lax.axis_size("tensor")
    j = lax.axis_index("tensor")
    i = lax.axis_index("dp")
    flat = i * tn + j
    nz, ny, nx = sides_of(n)
    place = jnp.stack([j, i // nx % ny, i // (ny * nx) // max(1, nz // 2)]).astype(jnp.int32)
    width = low_feature.shape[1]
    piece = width // tn
    pack = target_queries.shape[0]
    both = ("dp", "tensor")

    def swapped(values, s):
        return lax.ppermute(values, "tensor", [(a, a ^ s) for a in range(tn)])

    sent = features(place, low_feature, mid_feature, merging_gain, tn)
    parts = [sent[0]] + [swapped(sent[s], s) for s in range(1, tn)]

    high, squares = attend(doc_lengths, target_queries, target_keys, target_values)
    own_weight, cotangent, high = lax.optimization_barrier((draft_weight, cotangent, high))
    squares = squares + swapped(squares, 1)
    own_weight = weight_of_chip(own_weight)
    folded = fold(place, doc_lengths, step_offsets, cotangent)
    across, beside = swapped(folded, 2), swapped(folded, 1)
    squares, own_weight, beside, parts[1] = lax.optimization_barrier((squares, own_weight, beside, parts[1]))
    squares = [squares, swapped(squares, 2)]
    merged, squares = merge(place, merging_gain, high, parts, squares, width)
    own_weight = weight_of_both(own_weight)
    across, own_weight, merged, squares = lax.optimization_barrier((across, own_weight, merged, squares))
    folds = [folded, beside, across, swapped(across, 1)]
    own_weight = weight_of_place(own_weight)
    squares = [squares] + [swapped(squares, s) for s in range(1, tn)]
    weights = weight_once(weight_along_z(own_weight))
    kept, cut, hidden = grads(place, draft_gain.reshape(1, width), merged, folds, squares, width, ny, tn)
    halves = reduce_once(kept, cut)
    weights, own = lax.optimization_barrier((weights, [half[0] for half in halves]))
    halves = [(mine, other) for mine, (_, other) in zip(own, halves)]
    weights = weight_twice(weights)
    grad = reduce_along_z(reduce_twice(halves))
    hidden, grad = lax.optimization_barrier((hidden, grad))
    weight_grad = reduce_to_owner(grad)
    values = project(place, hidden, weights, tn)
    values = [values[0]] + [swapped(values[s], s) for s in range(1, tn)]
    draft_values = spread(place, doc_lengths, step_offsets, values)

    rows = weight_grad.shape[0]
    gain = lax.dynamic_slice(draft_gain, (flat * rows,), (rows,))
    gain_grad = jnp.sum(weight_grad * draft_weight.astype(F32), axis=1) / gain
    return (draft_values, weight_grad, gain_grad)


def solution(mesh):
    placed = (
        P("dp", "tensor"),
        P("dp", "tensor"),
        P("dp", "tensor"),
        P(("dp", "tensor"), None),
        P(("dp", "tensor"), None),
        P(),
        P(),
        P(("dp", "tensor"), None),
        P(None, ("dp", "tensor"), None),
        P("dp", None),
        P(),
    )
    return jax.shard_map(
        body,
        mesh=mesh,
        in_specs=placed,
        out_specs=(P(None, ("dp", "tensor"), None), P(("dp", "tensor"), None), P(("dp", "tensor"))),
        check_vma=False,
    )
```

```python
import functools
import math

import jax
import jax.numpy as jnp
import numpy as np
from jax import lax
from jax.experimental import pallas as pl
from jax.experimental.pallas import tpu as pltpu
from jax.sharding import PartitionSpec as P

HD = 128
STEPS = 3
OFFMAX = 32
EPSILON = 1e-05
VMEM_LIMIT = 20 * 1024 * 1024
FEATURES_LIMIT = 60 * 1024 * 1024

VMEM = pl.BlockSpec(memory_space=pltpu.VMEM)
SMEM = pl.BlockSpec(memory_space=pltpu.SMEM)
HBM = pl.BlockSpec(memory_space=pltpu.HBM)
F32 = jnp.float32
BF16 = jnp.bfloat16


SIDES = {64: (8, 4, 2)}


def sides_of(n):
    return SIDES.get(n, (1, 1, n))


def groups_along(n, *sides):
    sizes = sides_of(n)
    where = np.moveaxis(np.arange(n).reshape(sizes), sides, range(-len(sides), 0))
    return where.reshape(-1, math.prod(sizes[side] for side in sides)).tolist()


def block_order(n, tn):
    nz, ny, nx = sides_of(n)
    order = np.arange(n).reshape(ny, nz, nx)
    if nz == 2 * tn and n == ny * nx * tn * 2:
        for y in range(ny):
            for z in range(nz):
                for x in range(nx):
                    order[y, z, x] = (((z // tn) * ny + y) * nx + x) * tn + z % tn
    return order


def moved(values, change):
    n = lax.axis_size("dp")
    nz, ny, nx = sides_of(n)
    pairs = []
    for source in range(n):
        z, y, x = change(source // (ny * nx), source // nx % ny, source % nx)
        pairs.append((source, (z * ny + y) * nx + x))
    return lax.ppermute(values, "dp", pairs)


def weight_to_place(weight):
    n, tn = lax.axis_size("dp"), lax.axis_size("tensor")
    nz, ny, nx = sides_of(n)
    parts = []
    for turn in range(nx):
        pairs = []
        for j in range(tn):
            for q in range(n):
                y, z, x = q // (nz * nx), q // nx % nz, q % nx ^ turn
                pairs.append((j * n + q, ((z * ny + y) * nx + x) * tn + j))
        parts.append(lax.ppermute(weight, ("dp", "tensor"), pairs))
    return parts


def weight_across(weight, far):
    if sides_of(lax.axis_size("dp"))[0] == 1:
        return weight
    return jnp.concatenate([weight, moved(weight, lambda z, y, x: (z ^ far, y, x))])


def weight_halves(weight):
    if sides_of(lax.axis_size("dp"))[0] == 1:
        return [weight]
    return [weight, moved(weight, lambda z, y, x: (z ^ 1, y, x))]


def weight_once(halves):
    if sides_of(lax.axis_size("dp"))[1] == 1:
        return [[half] for half in halves]
    return [[half, moved(half, lambda z, y, x: (z, y ^ first, x))] for half, (first, _) in zip(halves, EXCHANGES)]


def weight_twice(halves):
    if sides_of(lax.axis_size("dp"))[1] == 1:
        return halves
    return [
        half + [moved(part, lambda z, y, x: (z, y ^ second, x)) for part in half]
        for half, (_, second) in zip(halves, EXCHANGES)]


KEPT = ((0, 3), (0, 1))
SENT = ((1, 2), (3, 2))
EXCHANGES = ((1, 3), (3, 1))


def reduce_once(kept, sent):
    if sides_of(lax.axis_size("dp"))[1] == 1:
        return [(keep[0], None) for keep in kept]
    got = [moved(send, lambda z, y, x: (z, y ^ first, x)) for send, (first, _) in zip(sent, EXCHANGES)]
    got = lax.optimization_barrier(got)
    return [(keep[0] + part[0].astype(F32), (keep[1] + part[1].astype(F32)).astype(BF16)) for keep, part in zip(kept, got)]


def reduce_twice(halves):
    if sides_of(lax.axis_size("dp"))[1] == 1:
        return jnp.concatenate([own for own, _ in halves])
    got = [moved(other, lambda z, y, x: (z, y ^ second, x)) for (_, other), (_, second) in zip(halves, EXCHANGES)]
    return jnp.concatenate([own + part.astype(F32) for (own, _), part in zip(halves, got)])


def reduce_along_z(grad):
    n = lax.axis_size("dp")
    nz = sides_of(n)[0]
    if nz == 1:
        return grad
    columns = grad.shape[-1]
    grad = lax.all_to_all(grad.astype(BF16), "dp", 0, 0, tiled=True, axis_index_groups=groups_along(n, 0))
    return jnp.sum(grad.reshape(nz, -1, columns).astype(F32), axis=0)


def reduce_to_owner(grad):
    n, tn = lax.axis_size("dp"), lax.axis_size("tensor")
    nz, ny, nx = sides_of(n)
    rows, columns = grad.shape[0] // nx, grad.shape[1]
    order = block_order(n, tn)
    x = lax.axis_index("dp") % nx
    total = None
    for turn in range(nx):
        pairs = []
        for z in range(nz):
            for y in range(ny):
                for x0 in range(nx):
                    for j in range(tn):
                        block = j * n + int(order[y, z, (x0 + turn) % nx])
                        pairs.append((((z * ny + y) * nx + x0) * tn + j, block))
        part = lax.dynamic_slice(grad, ((x + turn) % nx * rows, 0), (rows, columns))
        part = lax.ppermute(part, ("dp", "tensor"), pairs)
        total = part if total is None else total + part
    return total


def held(values, after):
    def kernel(*refs):
        pass

    return pl.pallas_call(
        kernel,
        in_specs=[pl.BlockSpec(memory_space=pl.ANY)] * (len(values) + 1),
        out_specs=[pl.BlockSpec(memory_space=pl.ANY)] * len(values),
        out_shape=[jax.ShapeDtypeStruct(value.shape, value.dtype) for value in values],
        input_output_aliases={k: k for k in range(len(values))},
        cost_estimate=pl.CostEstimate(flops=0, bytes_accessed=0, transcendentals=0),
        name="held",
    )(*values, after)


def segment_start(places, lengths_ref):
    end = jnp.int32(0)
    start = jnp.zeros_like(places)
    for s in range(lengths_ref.shape[1]):
        end = end + lengths_ref[0, s]
        start = jnp.where(places >= end, end, start)
    return start


def column(row):
    n = row.shape[-1]
    eye = lax.broadcasted_iota(jnp.int32, (n, n), 0) == lax.broadcasted_iota(jnp.int32, (n, n), 1)
    return jnp.sum(jnp.where(eye, row, 0.0), axis=1, keepdims=True)


def lane_sums(values):
    return lax.dot_general(
        jnp.ones((8, values.shape[1]), F32), values, (((1,), (1,)), ((), ())),
        precision=lax.Precision.HIGHEST, preferred_element_type=F32)


def folded_square_sum(values):
    total = None
    for c in range(0, values.shape[1], 128):
        piece = values[:, c:c + 128]
        total = piece * piece if total is None else total + piece * piece
    return total


def features_kernel(tn, place_ref, low_ref, mid_ref, gain_ref, *outs):
    j = place_ref[0]
    width = low_ref.shape[1]
    piece = width // tn
    step = 1024

    def rms_scale(ref):
        total = None
        for c in range(0, width, step):
            part = folded_square_sum(ref[:, c:c + step].astype(F32))
            total = part if total is None else total + part
        return lax.rsqrt(jnp.sum(total, axis=1, keepdims=True) / width + EPSILON)

    low_scale = rms_scale(low_ref)
    mid_scale = rms_scale(mid_ref)
    for s, out in enumerate(outs):
        first = pl.multiple_of((j ^ s) * piece, piece)
        for c in range(0, piece, 512):
            at = pl.ds(first + c, 512)
            value = (low_ref[:, at].astype(F32) * low_scale * gain_ref[0:1, at]
                     + mid_ref[:, at].astype(F32) * mid_scale * gain_ref[1:2, at])
            out[:, c:c + 512] = value.astype(BF16)


def features(place, low, mid, gain, tn):
    rows, width = low.shape
    block = 16
    piece = width // tn
    return pl.pallas_call(
        functools.partial(features_kernel, tn),
        grid=(rows // block,),
        in_specs=[
            SMEM,
            pl.BlockSpec((block, width), lambda b: (b, 0)),
            pl.BlockSpec((block, width), lambda b: (b, 0)),
            pl.BlockSpec(gain.shape, lambda b: (0, 0)),
        ],
        out_specs=[pl.BlockSpec((block, piece), lambda b: (b, 0))] * tn,
        out_shape=[jax.ShapeDtypeStruct((rows, piece), BF16)] * tn,
        compiler_params=pltpu.CompilerParams(vmem_limit_bytes=FEATURES_LIMIT),
        cost_estimate=pl.CostEstimate(flops=10 * rows * width, bytes_accessed=6 * rows * width, transcendentals=0),
        name="features",
    )(place, low, mid, gain)


def attend_kernel(window, lengths_ref, query_ref, key_ref, value_ref, high_ref, square_ref):
    block = query_ref.shape[0]
    pack = key_ref.shape[0]
    b = pl.program_id(0)
    first = pl.multiple_of(jnp.clip(b * block - (window - block), 0, pack - window), block)
    query_places = b * block + lax.broadcasted_iota(jnp.int32, (block, window), 0)
    key_places = first + lax.broadcasted_iota(jnp.int32, (block, window), 1)
    allowed = (key_places <= query_places) & (key_places >= segment_start(query_places, lengths_ref))
    bias = jnp.where(allowed, 0.0, -1e30).astype(F32)
    group = (query_ref.shape[1] // HD) // (key_ref.shape[1] // HD)
    squares = jnp.zeros((block, HD), F32)
    ones = jnp.ones((window, HD), BF16)
    scale = math.log2(math.e) / math.sqrt(HD)
    for g in range(key_ref.shape[1] // HD):
        key = key_ref[pl.ds(first, window), g * HD:(g + 1) * HD]
        value = jnp.concatenate([value_ref[pl.ds(first, window), g * HD:(g + 1) * HD], ones], axis=1)
        for r in range(group):
            at = slice((g * group + r) * HD, (g * group + r + 1) * HD)
            scores = lax.dot_general(query_ref[:, at], key, (((1,), (1,)), ((), ())), preferred_element_type=F32)
            scores = scores * scale + bias
            highest = jnp.max(scores, axis=1, keepdims=True)
            expo = jnp.exp2(scores - highest).astype(BF16)
            mixed = jnp.dot(expo, value, preferred_element_type=F32)
            out = (mixed[:, :HD] / mixed[:, HD:]).astype(BF16)
            high_ref[:, at] = out
            out = out.astype(F32)
            squares = squares + out * out
    square_ref[...] = lane_sums(squares)


def attend(lengths, queries, keys, values):
    pack, width = queries.shape
    block = 128
    window = min(pack, 256 + block)
    return pl.pallas_call(
        functools.partial(attend_kernel, window),
        grid=(pack // block,),
        in_specs=[
            SMEM,
            pl.BlockSpec((block, width), lambda b: (b, 0)),
            pl.BlockSpec(keys.shape, lambda b: (0, 0)),
            pl.BlockSpec(values.shape, lambda b: (0, 0)),
        ],
        out_specs=[
            pl.BlockSpec((block, width), lambda b: (b, 0)),
            pl.BlockSpec((8, block), lambda b: (0, b)),
        ],
        out_shape=[
            jax.ShapeDtypeStruct((pack, width), BF16),
            jax.ShapeDtypeStruct((8, pack), F32),
        ],
        compiler_params=pltpu.CompilerParams(vmem_limit_bytes=VMEM_LIMIT),
        cost_estimate=pl.CostEstimate(
            flops=4 * pack * window * width, bytes_accessed=4 * pack * width,
            transcendentals=pack * window * width // HD),
        name="attend",
    )(lengths, queries, keys, values)


def chosen(place_ref, lengths_ref, offset, rows, lead):
    target = place_ref[0] * rows + lax.broadcasted_iota(jnp.int32, (rows, rows + lead), 0)
    source = place_ref[0] * rows - lead + lax.broadcasted_iota(jnp.int32, (rows, rows + lead), 1)
    hit = (source == target - offset) & (source >= segment_start(target, lengths_ref))
    return jnp.where(hit, 1.0, 0.0).astype(BF16)


def fold_kernel(place_ref, lengths_ref, offsets_ref, cotangent_ref, out_ref):
    steps, rows, width = cotangent_ref.shape
    total = None
    for s in range(steps):
        pick = chosen(place_ref, lengths_ref, offsets_ref[s], rows, OFFMAX)
        part = lax.dot_general(pick, cotangent_ref[s], (((0,), (0,)), ((), ())), preferred_element_type=F32)
        total = part if total is None else total + part
    out_ref[...] = total.astype(BF16)


def fold(place, lengths, offsets, cotangent):
    steps, rows, width = cotangent.shape
    return pl.pallas_call(
        fold_kernel,
        in_specs=[SMEM, SMEM, SMEM, VMEM],
        out_specs=VMEM,
        out_shape=jax.ShapeDtypeStruct((rows + OFFMAX, width), BF16),
        compiler_params=pltpu.CompilerParams(vmem_limit_bytes=VMEM_LIMIT),
        cost_estimate=pl.CostEstimate(flops=2 * steps * rows * 160 * width, bytes_accessed=2 * steps * rows * width, transcendentals=0),
        name="fold",
    )(place, lengths, offsets, cotangent)


def merge_kernel(width, tn, place_ref, gain_ref, high_ref, *refs):
    parts, square_refs, (far_ref, out_square_ref, out_ref, sems) = refs[:tn], refs[tn:-4], refs[-4:]
    copies = []
    j = place_ref[0]
    rows = parts[0].shape[0]
    piece = high_ref.shape[1]
    squares = square_refs[0][...]
    for ref in square_refs[1:]:
        squares = squares + ref[...]
    scales = lax.rsqrt(squares / width + EPSILON)
    for b in range(tn):
        out_square_ref[:, b * rows:(b + 1) * rows] = scales[:, b * rows:(b + 1) * rows]
    for s in range(tn):
        first = pl.multiple_of((j ^ s) * rows, rows)
        at = pl.ds(first, rows)
        scale = column(out_square_ref[0:1, at])
        total = jnp.zeros((rows, 128), F32)
        for c in range(0, piece, 128):
            cols = slice(c, c + 128)
            gain = gain_ref[2:3, pl.ds(pl.multiple_of(j * piece + c, 128), 128)]
            merged = (parts[s][:, cols].astype(F32) + high_ref[at, cols].astype(F32) * scale * gain).astype(BF16)
            out_ref[at, cols] = merged
            merged = merged.astype(F32)
            total = total + merged * merged
        copy = pltpu.make_async_copy(out_ref.at[at, :], far_ref.at[at, :], sems.at[s])
        copy.start()
        copies.append(copy)
        out_square_ref[:, at] = lane_sums(total)
    for copy in copies:
        copy.wait()


def merge(place, gain, high, parts, squares, width):
    pack, piece = high.shape
    tn = len(parts)
    return pl.pallas_call(
        functools.partial(merge_kernel, width, tn),
        in_specs=[SMEM] + [VMEM] * (2 + tn + len(squares)),
        out_specs=[HBM, VMEM],
        out_shape=[
            jax.ShapeDtypeStruct((pack, piece), BF16),
            jax.ShapeDtypeStruct((8, pack), F32),
        ],
        scratch_shapes=[pltpu.VMEM((pack, piece), BF16), pltpu.SemaphoreType.DMA((tn,))],
        compiler_params=pltpu.CompilerParams(vmem_limit_bytes=VMEM_LIMIT),
        cost_estimate=pl.CostEstimate(flops=8 * pack * piece, bytes_accessed=6 * pack * piece, transcendentals=0),
        name="merge",
    )(place, gain, high, *parts, *squares)


def grads(place, gain, merged, folds, squares, width, ny, tn):
    pack, piece = merged.shape
    rows = pack // tn
    vw = folds[0].shape[1]
    chunk = piece // (2 * ny)
    kept, sent = (KEPT, SENT) if ny > 1 else (((0,), (0,)), ((), ()))
    steps = [(h, s, True) for h in range(2) for s in kept[h]] + [(h, s, False) for h in range(2) for s in sent[h]]
    steps.sort(key=lambda step: step[2])
    size = chunk // (2 * tn) if ny > 1 else chunk

    def kernel(place_ref, gain_ref, merged_ref, *refs):
        fold_refs, square_refs, refs = refs[:tn], refs[tn:2 * tn], refs[2 * tn:]
        keep_refs, refs = refs[:2], refs[2:]
        send_refs, refs = refs[:2 if ny > 1 else 0], refs[2 if ny > 1 else 0:]
        hidden_ref, fold_ref, near_ref, near_folds, near_cut, sems = refs
        coming = [
            pltpu.make_async_copy(
                merged_ref.at[b * rows:(b + 1) * rows, :], near_ref.at[b * rows:(b + 1) * rows, :], sems.at[b])
            for b in range(tn)]
        folds_coming = [
            pltpu.make_async_copy(fold_refs[s], near_folds.at[s], sems.at[tn + s]) for s in range(tn)]
        for copy in coming + folds_coming:
            copy.start()
        j, y = place_ref[0], place_ref[1]
        squares = square_refs[0][...]
        for s in range(1, tn):
            squares = squares + square_refs[s][...]
        scales = lax.rsqrt(squares / width + EPSILON)
        for b in range(tn):
            at = slice(b * rows, (b + 1) * rows)
            scale = column(scales[0:1, at])
            coming[b].wait()
            for c in range(0, piece, 128):
                cols = slice(c, c + 128)
                gain = gain_ref[:, pl.ds(pl.multiple_of(j * piece + c, 128), 128)]
                hidden_ref[at, cols] = (near_ref[at, cols].astype(F32) * scale * gain).astype(BF16)
        fold_ref[...] = jnp.zeros_like(fold_ref)
        for s in range(tn):
            at = pl.ds(pl.multiple_of((j ^ s) * rows, rows), rows + OFFMAX)
            folds_coming[s].wait()
            fold_ref[at, :] = fold_ref[at, :] + near_folds[s].astype(F32)
        folded = fold_ref[OFFMAX:, :].astype(BF16)
        going = []
        for h, s, keep in steps:
            at = pl.ds(pl.multiple_of(h * ny * chunk + (y ^ s) * chunk, chunk), chunk)
            part = lax.dot_general(
                hidden_ref[:, at], folded, (((0,), (0,)), ((), ())), preferred_element_type=F32)
            if size < chunk:
                part = jnp.concatenate(
                    [part[(x * tn + t) * size:(x * tn + t + 1) * size] for t in range(tn) for x in range(2)], axis=0)
            if keep:
                keep_refs[h][kept[h].index(s)] = part
            else:
                k = sent[h].index(s)
                near_cut[h, k] = part.astype(BF16)
                copy = pltpu.make_async_copy(near_cut.at[h, k], send_refs[h].at[k], sems.at[2 * tn + 2 * h + k])
                copy.start()
                going.append(copy)
        for copy in going:
            copy.wait()

    out_shape = [jax.ShapeDtypeStruct((len(kept[h]), chunk, vw), F32) for h in range(2)]
    if ny > 1:
        out_shape += [jax.ShapeDtypeStruct((len(sent[h]), chunk, vw), BF16) for h in range(2)]
    out_shape += [jax.ShapeDtypeStruct((pack, piece), BF16)]
    out = pl.pallas_call(
        kernel,
        in_specs=[SMEM, VMEM, HBM] + [HBM] * tn + [VMEM] * tn,
        out_specs=[VMEM] * 2 + ([HBM] * 2 if ny > 1 else []) + [VMEM],
        out_shape=out_shape,
        scratch_shapes=[
            pltpu.VMEM((pack + OFFMAX, vw), F32),
            pltpu.VMEM((pack, piece), BF16),
            pltpu.VMEM((tn, rows + OFFMAX, vw), BF16),
            pltpu.VMEM((2, 2, chunk if ny > 1 else 16, vw), BF16),
            pltpu.SemaphoreType.DMA((2 * tn + 4,)),
        ],
        compiler_params=pltpu.CompilerParams(vmem_limit_bytes=VMEM_LIMIT),
        cost_estimate=pl.CostEstimate(flops=2 * pack * piece * vw, bytes_accessed=8 * pack * piece, transcendentals=0),
        name="grads",
    )(place, gain, merged, *folds, *squares)
    return out[:2], out[2:-1] if ny > 1 else (None, None), out[-1]


def project(place, hidden, weights, tn, nz, nx):
    pack, piece = hidden.shape
    rows = pack // tn
    vw = weights[0][0].shape[1]
    parts = [
        (part, far, near)
        for half, near, (first, second) in zip(weights, (0, 1), EXCHANGES)
        for part, far in zip(half, (0, first, second, first ^ second))]
    distances = (0, 4, 2, 6) if nz > 1 else (0,)
    size = parts[0][0].shape[0] // (len(distances) * nx)

    def kernel(place_ref, hidden_ref, *refs):
        weight_refs, value_refs, weight_ref, total_ref = refs[:len(parts)], refs[len(parts):-2], refs[-2], refs[-1]
        j, y, z, x = place_ref[0], place_ref[1], place_ref[2], place_ref[3]
        for ref, (_, far, near) in zip(weight_refs, parts):
            for k, distance in enumerate(distances):
                for m in range(nx):
                    block = ((y ^ far) * nz + (z ^ distance ^ near)) * nx + (x ^ m)
                    at = pl.ds(pl.multiple_of(block * size, size), size)
                    weight_ref[at, :] = ref[(k * nx + m) * size:(k * nx + m + 1) * size, :]
        total_ref[0:OFFMAX, :] = jnp.zeros((OFFMAX, vw), F32)
        for c in range(0, pack, 256):
            total_ref[OFFMAX + c:OFFMAX + c + 256, :] = jnp.dot(
                hidden_ref[c:c + 256, :], weight_ref[...], preferred_element_type=F32)
        for s in range(tn):
            at = pl.ds(pl.multiple_of((j ^ s) * rows, rows), rows + OFFMAX)
            value_refs[s][...] = total_ref[at, :].astype(value_refs[s].dtype)

    return pl.pallas_call(
        kernel,
        in_specs=[SMEM] + [VMEM] * (1 + len(parts)),
        out_specs=[VMEM] * tn,
        out_shape=[jax.ShapeDtypeStruct((rows + OFFMAX, vw), F32 if s == 0 else BF16) for s in range(tn)],
        scratch_shapes=[pltpu.VMEM((piece, vw), BF16), pltpu.VMEM((pack + OFFMAX, vw), F32)],
        compiler_params=pltpu.CompilerParams(vmem_limit_bytes=VMEM_LIMIT),
        cost_estimate=pl.CostEstimate(flops=2 * pack * piece * vw, bytes_accessed=4 * pack * piece, transcendentals=0),
        name="project",
    )(place, hidden, *[part for part, _, _ in parts])


def spread(place, lengths, offsets, parts):
    rows, vw = parts[0].shape[0] - OFFMAX, parts[0].shape[1]

    def kernel(place_ref, lengths_ref, offsets_ref, *refs):
        parts_refs, out_ref = refs[:-1], refs[-1]
        total = None
        for ref in parts_refs:
            part = ref[...].astype(F32)
            total = part if total is None else total + part
        total = total.astype(BF16)
        for s in range(STEPS):
            pick = chosen(place_ref, lengths_ref, offsets_ref[s], rows, OFFMAX)
            out_ref[s] = jnp.dot(pick, total, preferred_element_type=F32).astype(BF16)

    return pl.pallas_call(
        kernel,
        in_specs=[SMEM] * 3 + [VMEM] * len(parts),
        out_specs=VMEM,
        out_shape=jax.ShapeDtypeStruct((STEPS, rows, vw), BF16),
        compiler_params=pltpu.CompilerParams(vmem_limit_bytes=VMEM_LIMIT),
        cost_estimate=pl.CostEstimate(flops=2 * STEPS * rows * 160 * vw, bytes_accessed=8 * STEPS * rows * vw, transcendentals=0),
        name="spread",
    )(place, lengths, offsets, *parts)


def body(
    target_queries,
    target_keys,
    target_values,
    low_feature,
    mid_feature,
    merging_gain,
    draft_gain,
    draft_weight,
    cotangent,
    doc_lengths,
    step_offsets,
):
    n = lax.axis_size("dp")
    tn = lax.axis_size("tensor")
    j = lax.axis_index("tensor")
    i = lax.axis_index("dp")
    flat = i * tn + j
    nz, ny, nx = sides_of(n)
    place = jnp.stack([j, i // nx % ny, i // (ny * nx), i % nx]).astype(jnp.int32)
    width = low_feature.shape[1]
    piece = width // tn
    pack = target_queries.shape[0]
    both = ("dp", "tensor")

    def swapped(values, s):
        return lax.ppermute(values, "tensor", [(a, a ^ s) for a in range(tn)])

    folded = fold(place, doc_lengths, step_offsets, cotangent)
    across = swapped(folded, 2)
    low_feature, folded = lax.optimization_barrier((low_feature, folded))
    sent = features(place, low_feature, mid_feature, merging_gain, tn)
    across, sent = lax.optimization_barrier((across, sent))
    parts = [sent[0]] + [swapped(sent[s], s) for s in range(1, tn)]

    high, squares = attend(doc_lengths, target_queries, target_keys, target_values)
    own_weight, high, folded, across = lax.optimization_barrier((draft_weight, high, folded, across))
    squares = squares + swapped(squares, 1)
    folds = [folded, swapped(folded, 1), across, swapped(across, 1)]
    squares, folds, parts[1] = lax.optimization_barrier((squares, folds, parts[1]))
    squares = [squares, swapped(squares, 2)]
    weights = weight_to_place(own_weight)
    merged, squares = merge(place, merging_gain, high, parts, squares, width)
    weights, merged, squares = lax.optimization_barrier((weights, merged, squares))
    weights = weight_across(jnp.concatenate(weights), nz // 2)
    squares = [squares] + [swapped(squares, s) for s in range(1, tn)]
    kept, cut, hidden = grads(place, draft_gain.reshape(1, width), merged, folds, squares, width, ny, tn)
    weights, hidden = lax.optimization_barrier((weights, hidden))
    weights = weight_halves(weight_across(weights, nz // 4))
    halves = reduce_once(kept, cut)
    weights, own = lax.optimization_barrier((weights, [half[0] for half in halves]))
    halves = [(mine, other) for mine, (_, other) in zip(own, halves)]
    weights = weight_once(weights)
    grad = reduce_twice(halves)
    if ny > 1:
        flat_weights = held([part for half in weights for part in half], grad)
        weights = [list(flat_weights[:2]), list(flat_weights[2:])]
    weights = weight_twice(weights)
    grad = reduce_along_z(grad)
    hidden, grad = lax.optimization_barrier((hidden, grad))
    weight_grad = reduce_to_owner(grad)
    values = project(place, hidden, weights, tn, nz, nx)
    values = [values[0]] + [swapped(values[s], s) for s in range(1, tn)]
    draft_values = spread(place, doc_lengths, step_offsets, values)

    rows = weight_grad.shape[0]
    gain = lax.dynamic_slice(draft_gain, (flat * rows,), (rows,))
    gain_grad = jnp.sum(weight_grad * draft_weight.astype(F32), axis=1) / gain
    return (draft_values, weight_grad, gain_grad)


def solution(mesh):
    placed = (
        P("dp", "tensor"),
        P("dp", "tensor"),
        P("dp", "tensor"),
        P(("dp", "tensor"), None),
        P(("dp", "tensor"), None),
        P(),
        P(),
        P(("dp", "tensor"), None),
        P(None, ("dp", "tensor"), None),
        P("dp", None),
        P(),
    )
    return jax.shard_map(
        body,
        mesh=mesh,
        in_specs=placed,
        out_specs=(P(None, ("dp", "tensor"), None), P(("dp", "tensor"), None), P(("dp", "tensor"))),
        check_vma=False,
    )
```

```python
import functools
import math

import jax
import jax.numpy as jnp
import numpy as np
from jax import lax
from jax.experimental import pallas as pl
from jax.experimental.pallas import tpu as pltpu
from jax.sharding import PartitionSpec as P

HD = 128
STEPS = 3
OFFMAX = 32
EPSILON = 1e-05
VMEM_LIMIT = 20 * 1024 * 1024
LARGE_LIMIT = 60 * 1024 * 1024

VMEM = pl.BlockSpec(memory_space=pltpu.VMEM)
SMEM = pl.BlockSpec(memory_space=pltpu.SMEM)
HBM = pl.BlockSpec(memory_space=pltpu.HBM)
F32 = jnp.float32
BF16 = jnp.bfloat16


SIDES = {64: (8, 4, 2)}


def sides_of(n):
    return SIDES.get(n, (1, 1, n))


def groups_along(n, *sides):
    sizes = sides_of(n)
    where = np.moveaxis(np.arange(n).reshape(sizes), sides, range(-len(sides), 0))
    return where.reshape(-1, math.prod(sizes[side] for side in sides)).tolist()


def block_order(n, tn):
    nz, ny, nx = sides_of(n)
    order = np.arange(n).reshape(ny, nz, nx)
    if nz == 2 * tn and n == ny * nx * tn * 2:
        for y in range(ny):
            for z in range(nz):
                for x in range(nx):
                    order[y, z, x] = (((z // tn) * ny + y) * nx + x) * tn + z % tn
    return order


def moved(values, change):
    n = lax.axis_size("dp")
    nz, ny, nx = sides_of(n)
    pairs = []
    for source in range(n):
        z, y, x = change(source // (ny * nx), source // nx % ny, source % nx)
        pairs.append((source, (z * ny + y) * nx + x))
    return lax.ppermute(values, "dp", pairs)


def weight_to_place(weight):
    n, tn = lax.axis_size("dp"), lax.axis_size("tensor")
    nz, ny, nx = sides_of(n)
    parts = []
    for turn in range(nx):
        pairs = []
        for j in range(tn):
            for q in range(n):
                y, z, x = q // (nz * nx), q // nx % nz, q % nx ^ turn
                pairs.append((j * n + q, ((z * ny + y) * nx + x) * tn + j))
        parts.append(lax.ppermute(weight, ("dp", "tensor"), pairs))
    return parts


def weight_across(weight, far):
    if sides_of(lax.axis_size("dp"))[0] == 1:
        return weight
    return jnp.concatenate([weight, moved(weight, lambda z, y, x: (z ^ far, y, x))])


def weight_halves(weight):
    if sides_of(lax.axis_size("dp"))[0] == 1:
        return [weight]
    return [weight, moved(weight, lambda z, y, x: (z ^ 1, y, x))]


def weight_once(halves):
    if sides_of(lax.axis_size("dp"))[1] == 1:
        return [[half] for half in halves]
    return [[half, moved(half, lambda z, y, x: (z, y ^ first, x))] for half, (first, _) in zip(halves, EXCHANGES)]


def weight_twice(halves):
    if sides_of(lax.axis_size("dp"))[1] == 1:
        return halves
    return [
        half + [moved(part, lambda z, y, x: (z, y ^ second, x)) for part in half]
        for half, (_, second) in zip(halves, EXCHANGES)]


KEPT = ((0, 3), (0, 1))
SENT = ((1, 2), (3, 2))
EXCHANGES = ((1, 3), (3, 1))


def reduce_once(kept, sent):
    if sides_of(lax.axis_size("dp"))[1] == 1:
        return [(keep[0], None) for keep in kept]
    got = [moved(send, lambda z, y, x: (z, y ^ first, x)) for send, (first, _) in zip(sent, EXCHANGES)]
    got = lax.optimization_barrier(got)
    return [(keep[0] + part[0].astype(F32), (keep[1] + part[1].astype(F32)).astype(BF16)) for keep, part in zip(kept, got)]


def reduce_twice(halves):
    if sides_of(lax.axis_size("dp"))[1] == 1:
        return [jnp.zeros_like(own) for own, _ in halves]
    return [moved(other, lambda z, y, x: (z, y ^ second, x)) for (_, other), (_, second) in zip(halves, EXCHANGES)]


def reduce_along_z(grad):
    n = lax.axis_size("dp")
    nz = sides_of(n)[0]
    if nz == 1:
        return grad
    columns = grad.shape[-1]
    grad = lax.all_to_all(grad.astype(BF16), "dp", 0, 0, tiled=True, axis_index_groups=groups_along(n, 0))
    return jnp.sum(grad.reshape(nz, -1, columns).astype(F32), axis=0)


def reduce_to_owner(grad):
    n, tn = lax.axis_size("dp"), lax.axis_size("tensor")
    nz, ny, nx = sides_of(n)
    rows, columns = grad.shape[0] // nx, grad.shape[1]
    order = block_order(n, tn)
    x = lax.axis_index("dp") % nx
    total = None
    for turn in range(nx):
        pairs = []
        for z in range(nz):
            for y in range(ny):
                for x0 in range(nx):
                    for j in range(tn):
                        block = j * n + int(order[y, z, (x0 + turn) % nx])
                        pairs.append((((z * ny + y) * nx + x0) * tn + j, block))
        part = lax.dynamic_slice(grad, ((x + turn) % nx * rows, 0), (rows, columns))
        part = lax.ppermute(part, ("dp", "tensor"), pairs)
        total = part if total is None else total + part
    return total


OFFSETS = 4
LENGTHS = OFFSETS + STEPS


def segment_start(places, info_ref):
    end = jnp.int32(0)
    start = jnp.zeros_like(places)
    for s in range(LENGTHS, info_ref.shape[0]):
        end = end + info_ref[s]
        start = jnp.where(places >= end, end, start)
    return start


def column(row):
    n = row.shape[-1]
    eye = lax.broadcasted_iota(jnp.int32, (n, n), 0) == lax.broadcasted_iota(jnp.int32, (n, n), 1)
    return jnp.sum(jnp.where(eye, row, 0.0), axis=1, keepdims=True)


def lane_sums(values):
    return lax.dot_general(
        jnp.ones((8, values.shape[1]), F32), values, (((1,), (1,)), ((), ())),
        precision=lax.Precision.HIGHEST, preferred_element_type=F32)


def folded_square_sum(values):
    total = None
    for c in range(0, values.shape[1], 128):
        piece = values[:, c:c + 128]
        total = piece * piece if total is None else total + piece * piece
    return total


def features_kernel(tn, info_ref, low_ref, mid_ref, gain_ref, *outs):
    j = info_ref[0]
    width = low_ref.shape[1]
    piece = width // tn
    step = 1024

    def rms_scale(ref):
        total = None
        for c in range(0, width, step):
            part = folded_square_sum(ref[:, c:c + step].astype(F32))
            total = part if total is None else total + part
        return lax.rsqrt(jnp.sum(total, axis=1, keepdims=True) / width + EPSILON)

    low_scale = rms_scale(low_ref)
    mid_scale = rms_scale(mid_ref)
    for s, out in enumerate(outs):
        first = pl.multiple_of((j ^ s) * piece, piece)
        for c in range(0, piece, 512):
            at = pl.ds(first + c, 512)
            value = (low_ref[:, at].astype(F32) * low_scale * gain_ref[0:1, at]
                     + mid_ref[:, at].astype(F32) * mid_scale * gain_ref[1:2, at])
            out[:, c:c + 512] = value.astype(BF16)


def features(info, low, mid, gain, tn):
    rows, width = low.shape
    block = 32
    piece = width // tn
    return pl.pallas_call(
        functools.partial(features_kernel, tn),
        grid=(rows // block,),
        in_specs=[
            SMEM,
            pl.BlockSpec((block, width), lambda b: (b, 0)),
            pl.BlockSpec((block, width), lambda b: (b, 0)),
            pl.BlockSpec(gain.shape, lambda b: (0, 0)),
        ],
        out_specs=[pl.BlockSpec((block, piece), lambda b: (b, 0))] * tn,
        out_shape=[jax.ShapeDtypeStruct((rows, piece), BF16)] * tn,
        compiler_params=pltpu.CompilerParams(vmem_limit_bytes=LARGE_LIMIT),
        cost_estimate=pl.CostEstimate(flops=10 * rows * width, bytes_accessed=6 * rows * width, transcendentals=0),
        name="features",
    )(info, low, mid, gain)


def attend_kernel(window, info_ref, query_ref, key_ref, value_ref, high_ref, square_ref):
    block = query_ref.shape[0]
    pack = key_ref.shape[0]
    b = pl.program_id(0)
    first = pl.multiple_of(jnp.clip(b * block - (window - block), 0, pack - window), block)
    query_places = b * block + lax.broadcasted_iota(jnp.int32, (block, window), 0)
    key_places = first + lax.broadcasted_iota(jnp.int32, (block, window), 1)
    allowed = (key_places <= query_places) & (key_places >= segment_start(query_places, info_ref))
    bias = jnp.where(allowed, 0.0, -1e30).astype(F32)
    group = (query_ref.shape[1] // HD) // (key_ref.shape[1] // HD)
    squares = jnp.zeros((block, HD), F32)
    ones = jnp.ones((window, HD), BF16)
    scale = math.log2(math.e) / math.sqrt(HD)
    for g in range(key_ref.shape[1] // HD):
        key = key_ref[pl.ds(first, window), g * HD:(g + 1) * HD]
        value = jnp.concatenate([value_ref[pl.ds(first, window), g * HD:(g + 1) * HD], ones], axis=1)
        for r in range(group):
            at = slice((g * group + r) * HD, (g * group + r + 1) * HD)
            scores = lax.dot_general(query_ref[:, at], key, (((1,), (1,)), ((), ())), preferred_element_type=F32)
            scores = scores * scale + bias
            highest = jnp.max(scores, axis=1, keepdims=True)
            expo = jnp.exp2(scores - highest).astype(BF16)
            mixed = jnp.dot(expo, value, preferred_element_type=F32)
            out = (mixed[:, :HD] / mixed[:, HD:]).astype(BF16)
            high_ref[:, at] = out
            out = out.astype(F32)
            squares = squares + out * out
    square_ref[...] = lane_sums(squares)


def attend(info, queries, keys, values):
    pack, width = queries.shape
    block = 128
    window = min(pack, 256 + block)
    return pl.pallas_call(
        functools.partial(attend_kernel, window),
        grid=(pack // block,),
        in_specs=[
            SMEM,
            pl.BlockSpec((block, width), lambda b: (b, 0)),
            pl.BlockSpec(keys.shape, lambda b: (0, 0)),
            pl.BlockSpec(values.shape, lambda b: (0, 0)),
        ],
        out_specs=[
            pl.BlockSpec((block, width), lambda b: (b, 0)),
            pl.BlockSpec((8, block), lambda b: (0, b)),
        ],
        out_shape=[
            jax.ShapeDtypeStruct((pack, width), BF16),
            jax.ShapeDtypeStruct((8, pack), F32),
        ],
        compiler_params=pltpu.CompilerParams(vmem_limit_bytes=VMEM_LIMIT),
        cost_estimate=pl.CostEstimate(
            flops=4 * pack * window * width, bytes_accessed=4 * pack * width,
            transcendentals=pack * window * width // HD),
        name="attend",
    )(info, queries, keys, values)


def chosen(info_ref, step, rows, lead):
    target = info_ref[0] * rows + lax.broadcasted_iota(jnp.int32, (rows, rows + lead), 0)
    source = info_ref[0] * rows - lead + lax.broadcasted_iota(jnp.int32, (rows, rows + lead), 1)
    hit = (source == target - info_ref[OFFSETS + step]) & (source >= segment_start(target, info_ref))
    return jnp.where(hit, 1.0, 0.0).astype(BF16)


def fold_kernel(info_ref, cotangent_ref, out_ref, near_ref, sems):
    steps, rows, width = cotangent_ref.shape
    coming = [pltpu.make_async_copy(cotangent_ref.at[s], near_ref.at[s], sems.at[s]) for s in range(steps)]
    for copy in coming:
        copy.start()
    total = None
    for s in range(steps):
        pick = chosen(info_ref, s, rows, OFFMAX)
        coming[s].wait()
        part = lax.dot_general(pick, near_ref[s], (((0,), (0,)), ((), ())), preferred_element_type=F32)
        total = part if total is None else total + part
    out_ref[...] = total.astype(BF16)


def fold(info, cotangent):
    steps, rows, width = cotangent.shape
    return pl.pallas_call(
        fold_kernel,
        in_specs=[SMEM, HBM],
        out_specs=VMEM,
        out_shape=jax.ShapeDtypeStruct((rows + OFFMAX, width), BF16),
        scratch_shapes=[pltpu.VMEM(cotangent.shape, BF16), pltpu.SemaphoreType.DMA((steps,))],
        compiler_params=pltpu.CompilerParams(vmem_limit_bytes=LARGE_LIMIT),
        cost_estimate=pl.CostEstimate(flops=2 * steps * rows * 160 * width, bytes_accessed=2 * steps * rows * width, transcendentals=0),
        name="fold",
    )(info, cotangent)


def merge_kernel(width, tn, info_ref, gain_ref, high_ref, *refs):
    parts, square_refs, (far_ref, out_square_ref, out_ref, sems) = refs[:tn], refs[tn:-4], refs[-4:]
    copies = []
    j = info_ref[0]
    rows = parts[0].shape[0]
    piece = high_ref.shape[1]
    squares = square_refs[0][...]
    for ref in square_refs[1:]:
        squares = squares + ref[...]
    scales = lax.rsqrt(squares / width + EPSILON)
    for b in range(tn):
        out_square_ref[:, b * rows:(b + 1) * rows] = scales[:, b * rows:(b + 1) * rows]
    for s in range(tn):
        first = pl.multiple_of((j ^ s) * rows, rows)
        at = pl.ds(first, rows)
        scale = column(out_square_ref[0:1, at])
        total = jnp.zeros((rows, 128), F32)
        for c in range(0, piece, 128):
            cols = slice(c, c + 128)
            gain = gain_ref[2:3, pl.ds(pl.multiple_of(j * piece + c, 128), 128)]
            merged = (parts[s][:, cols].astype(F32) + high_ref[at, cols].astype(F32) * scale * gain).astype(BF16)
            out_ref[at, cols] = merged
            merged = merged.astype(F32)
            total = total + merged * merged
        copy = pltpu.make_async_copy(out_ref.at[at, :], far_ref.at[at, :], sems.at[s])
        copy.start()
        copies.append(copy)
        out_square_ref[:, at] = lane_sums(total)
    for copy in copies:
        copy.wait()


def merge(info, gain, high, parts, squares, width):
    pack, piece = high.shape
    tn = len(parts)
    return pl.pallas_call(
        functools.partial(merge_kernel, width, tn),
        in_specs=[SMEM] + [VMEM] * (2 + tn + len(squares)),
        out_specs=[HBM, VMEM],
        out_shape=[
            jax.ShapeDtypeStruct((pack, piece), BF16),
            jax.ShapeDtypeStruct((8, pack), F32),
        ],
        scratch_shapes=[pltpu.VMEM((pack, piece), BF16), pltpu.SemaphoreType.DMA((tn,))],
        compiler_params=pltpu.CompilerParams(vmem_limit_bytes=VMEM_LIMIT),
        cost_estimate=pl.CostEstimate(flops=8 * pack * piece, bytes_accessed=6 * pack * piece, transcendentals=0),
        name="merge",
    )(info, gain, high, *parts, *squares)


def grads(info, gain, merged, folds, squares, width, ny, tn):
    pack, piece = merged.shape
    rows = pack // tn
    vw = folds[0].shape[1]
    chunk = piece // (2 * ny)
    kept, sent = (KEPT, SENT) if ny > 1 else (((0,), (0,)), ((), ()))
    steps = [(h, s, True) for h in range(2) for s in kept[h]] + [(h, s, False) for h in range(2) for s in sent[h]]
    steps.sort(key=lambda step: step[2])
    size = chunk // (2 * tn) if ny > 1 else chunk

    def kernel(info_ref, gain_ref, merged_ref, *refs):
        fold_refs, square_refs, refs = refs[:tn], refs[tn:2 * tn], refs[2 * tn:]
        keep_refs, refs = refs[:2], refs[2:]
        send_refs, refs = refs[:2 if ny > 1 else 0], refs[2 if ny > 1 else 0:]
        hidden_ref, fold_ref, near_ref, near_folds, near_cut, sems = refs
        coming = [
            pltpu.make_async_copy(
                merged_ref.at[b * rows:(b + 1) * rows, :], near_ref.at[b * rows:(b + 1) * rows, :], sems.at[b])
            for b in range(tn)]
        folds_coming = [
            pltpu.make_async_copy(fold_refs[s], near_folds.at[s], sems.at[tn + s]) for s in range(tn)]
        for copy in coming + folds_coming:
            copy.start()
        j, y = info_ref[0], info_ref[1]
        squares = square_refs[0][...]
        for s in range(1, tn):
            squares = squares + square_refs[s][...]
        scales = lax.rsqrt(squares / width + EPSILON)
        for b in range(tn):
            at = slice(b * rows, (b + 1) * rows)
            scale = column(scales[0:1, at])
            coming[b].wait()
            for c in range(0, piece, 128):
                cols = slice(c, c + 128)
                gain = gain_ref[:, pl.ds(pl.multiple_of(j * piece + c, 128), 128)]
                hidden_ref[at, cols] = (near_ref[at, cols].astype(F32) * scale * gain).astype(BF16)
        fold_ref[...] = jnp.zeros_like(fold_ref)
        for s in range(tn):
            at = pl.ds(pl.multiple_of((j ^ s) * rows, rows), rows + OFFMAX)
            folds_coming[s].wait()
            fold_ref[at, :] = fold_ref[at, :] + near_folds[s].astype(F32)
        folded = fold_ref[OFFMAX:, :].astype(BF16)
        going = []
        for h, s, keep in steps:
            at = pl.ds(pl.multiple_of(h * ny * chunk + (y ^ s) * chunk, chunk), chunk)
            part = lax.dot_general(
                hidden_ref[:, at], folded, (((0,), (0,)), ((), ())), preferred_element_type=F32)
            if size < chunk:
                part = jnp.concatenate(
                    [part[(x * tn + t) * size:(x * tn + t + 1) * size] for t in range(tn) for x in range(2)], axis=0)
            if keep:
                keep_refs[h][kept[h].index(s)] = part
            else:
                k = sent[h].index(s)
                near_cut[h, k] = part.astype(BF16)
                copy = pltpu.make_async_copy(near_cut.at[h, k], send_refs[h].at[k], sems.at[2 * tn + 2 * h + k])
                copy.start()
                going.append(copy)
        for copy in going:
            copy.wait()

    out_shape = [jax.ShapeDtypeStruct((len(kept[h]), chunk, vw), F32) for h in range(2)]
    if ny > 1:
        out_shape += [jax.ShapeDtypeStruct((len(sent[h]), chunk, vw), BF16) for h in range(2)]
    out_shape += [jax.ShapeDtypeStruct((pack, piece), BF16)]
    out = pl.pallas_call(
        kernel,
        in_specs=[SMEM, VMEM, HBM] + [HBM] * tn + [VMEM] * tn,
        out_specs=[VMEM] * 2 + ([HBM] * 2 if ny > 1 else []) + [VMEM],
        out_shape=out_shape,
        scratch_shapes=[
            pltpu.VMEM((pack + OFFMAX, vw), F32),
            pltpu.VMEM((pack, piece), BF16),
            pltpu.VMEM((tn, rows + OFFMAX, vw), BF16),
            pltpu.VMEM((2, 2, chunk if ny > 1 else 16, vw), BF16),
            pltpu.SemaphoreType.DMA((2 * tn + 4,)),
        ],
        compiler_params=pltpu.CompilerParams(vmem_limit_bytes=VMEM_LIMIT),
        cost_estimate=pl.CostEstimate(flops=2 * pack * piece * vw, bytes_accessed=8 * pack * piece, transcendentals=0),
        name="grads",
    )(info, gain, merged, *folds, *squares)
    return out[:2], out[2:-1] if ny > 1 else (None, None), out[-1]


def project(info, hidden, weights, tn, nz, nx):
    pack, piece = hidden.shape
    rows = pack // tn
    vw = weights[0][0].shape[1]
    parts = [
        (part, far, near)
        for half, near, (first, second) in zip(weights, (0, 1), EXCHANGES)
        for part, far in zip(half, (0, first, second, first ^ second))]
    distances = (0, 4, 2, 6) if nz > 1 else (0,)
    size = parts[0][0].shape[0] // (len(distances) * nx)

    def kernel(info_ref, hidden_ref, *refs):
        weight_refs, value_refs = refs[:len(parts)], refs[len(parts):-4]
        weight_ref, total_ref, near_ref, sems = refs[-4:]
        coming = [pltpu.make_async_copy(ref, near_ref.at[p], sems.at[p]) for p, ref in enumerate(weight_refs)]
        for copy in coming:
            copy.start()
        j, y, z, x = info_ref[0], info_ref[1], info_ref[2], info_ref[3]
        for p, (_, far, near) in enumerate(parts):
            coming[p].wait()
            for k, distance in enumerate(distances):
                for m in range(nx):
                    block = ((y ^ far) * nz + (z ^ distance ^ near)) * nx + (x ^ m)
                    at = pl.ds(pl.multiple_of(block * size, size), size)
                    weight_ref[at, :] = near_ref[p, (k * nx + m) * size:(k * nx + m + 1) * size, :]
        total_ref[0:OFFMAX, :] = jnp.zeros((OFFMAX, vw), F32)
        for c in range(0, pack, 256):
            total_ref[OFFMAX + c:OFFMAX + c + 256, :] = jnp.dot(
                hidden_ref[c:c + 256, :], weight_ref[...], preferred_element_type=F32)
        for s in range(tn):
            at = pl.ds(pl.multiple_of((j ^ s) * rows, rows), rows + OFFMAX)
            value_refs[s][...] = total_ref[at, :].astype(value_refs[s].dtype)

    return pl.pallas_call(
        kernel,
        in_specs=[SMEM, VMEM] + [HBM] * len(parts),
        out_specs=[VMEM] * tn,
        out_shape=[jax.ShapeDtypeStruct((rows + OFFMAX, vw), F32 if s == 0 else BF16) for s in range(tn)],
        scratch_shapes=[
            pltpu.VMEM((piece, vw), BF16),
            pltpu.VMEM((pack + OFFMAX, vw), F32),
            pltpu.VMEM((len(parts),) + parts[0][0].shape, BF16),
            pltpu.SemaphoreType.DMA((len(parts),)),
        ],
        compiler_params=pltpu.CompilerParams(vmem_limit_bytes=VMEM_LIMIT),
        cost_estimate=pl.CostEstimate(flops=2 * pack * piece * vw, bytes_accessed=4 * pack * piece, transcendentals=0),
        name="project",
    )(info, hidden, *[part for part, _, _ in parts])


def spread(info, parts):
    rows, vw = parts[0].shape[0] - OFFMAX, parts[0].shape[1]

    def kernel(info_ref, *refs):
        parts_refs, out_ref = refs[:-1], refs[-1]
        total = None
        for ref in parts_refs:
            part = ref[...].astype(F32)
            total = part if total is None else total + part
        total = total.astype(BF16)
        for s in range(STEPS):
            pick = chosen(info_ref, s, rows, OFFMAX)
            out_ref[s] = jnp.dot(pick, total, preferred_element_type=F32).astype(BF16)

    return pl.pallas_call(
        kernel,
        in_specs=[SMEM] + [VMEM] * len(parts),
        out_specs=VMEM,
        out_shape=jax.ShapeDtypeStruct((STEPS, rows, vw), BF16),
        compiler_params=pltpu.CompilerParams(vmem_limit_bytes=VMEM_LIMIT),
        cost_estimate=pl.CostEstimate(flops=2 * STEPS * rows * 160 * vw, bytes_accessed=8 * STEPS * rows * vw, transcendentals=0),
        name="spread",
    )(info, *parts)


def body(
    target_queries,
    target_keys,
    target_values,
    low_feature,
    mid_feature,
    merging_gain,
    draft_gain,
    draft_weight,
    cotangent,
    doc_lengths,
    step_offsets,
):
    n = lax.axis_size("dp")
    tn = lax.axis_size("tensor")
    j = lax.axis_index("tensor")
    i = lax.axis_index("dp")
    flat = i * tn + j
    nz, ny, nx = sides_of(n)
    place = jnp.stack([j, i // nx % ny, i // (ny * nx), i % nx]).astype(jnp.int32)
    info = jnp.concatenate([place, step_offsets, doc_lengths.reshape(-1)])
    width = low_feature.shape[1]
    piece = width // tn
    pack = target_queries.shape[0]
    both = ("dp", "tensor")

    def swapped(values, s):
        return lax.ppermute(values, "tensor", [(a, a ^ s) for a in range(tn)])

    folded = fold(info, cotangent)
    across = swapped(folded, 2)
    low_feature, folded = lax.optimization_barrier((low_feature, folded))
    sent = features(info, low_feature, mid_feature, merging_gain, tn)
    across, sent = lax.optimization_barrier((across, sent))
    parts = [sent[0]] + [swapped(sent[s], s) for s in range(1, tn)]

    high, squares = attend(info, target_queries, target_keys, target_values)
    own_weight, high, folded, across = lax.optimization_barrier((draft_weight, high, folded, across))
    squares = squares + swapped(squares, 1)
    folds = [folded, swapped(folded, 1), across, swapped(across, 1)]
    squares, folds, parts[1] = lax.optimization_barrier((squares, folds, parts[1]))
    squares = [squares, swapped(squares, 2)]
    weights = weight_to_place(own_weight)
    merged, squares = merge(info, merging_gain, high, parts, squares, width)
    weights, merged, squares = lax.optimization_barrier((weights, merged, squares))
    weights = weight_across(jnp.concatenate(weights), nz // 2)
    squares = [squares] + [swapped(squares, s) for s in range(1, tn)]
    kept, cut, hidden = grads(info, draft_gain.reshape(1, width), merged, folds, squares, width, ny, tn)
    weights, hidden = lax.optimization_barrier((weights, hidden))
    weights = weight_halves(weight_across(weights, nz // 4))
    halves = reduce_once(kept, cut)
    weights, own = lax.optimization_barrier((weights, [half[0] for half in halves]))
    got = reduce_twice(halves)
    weights = weight_once(weights)
    grad = [mine + part.astype(F32) for mine, part in zip(own, got)]
    if ny > 1:
        grad = [half.astype(BF16) for half in grad]
    weights, grad = lax.optimization_barrier((weights, grad))
    grad = jnp.concatenate(grad)
    weights = weight_twice(weights)
    grad = reduce_along_z(grad)
    hidden, grad = lax.optimization_barrier((hidden, grad))
    weight_grad = reduce_to_owner(grad)
    values = project(info, hidden, weights, tn, nz, nx)
    values = [values[0]] + [swapped(values[s], s) for s in range(1, tn)]
    draft_values = spread(info, values)

    rows = weight_grad.shape[0]
    gain = lax.dynamic_slice(draft_gain, (flat * rows,), (rows,))
    gain_grad = jnp.sum(weight_grad * draft_weight.astype(F32), axis=1) / gain
    return (draft_values, weight_grad, gain_grad)


def solution(mesh):
    placed = (
        P("dp", "tensor"),
        P("dp", "tensor"),
        P("dp", "tensor"),
        P(("dp", "tensor"), None),
        P(("dp", "tensor"), None),
        P(),
        P(),
        P(("dp", "tensor"), None),
        P(None, ("dp", "tensor"), None),
        P("dp", None),
        P(),
    )
    return jax.shard_map(
        body,
        mesh=mesh,
        in_specs=placed,
        out_specs=(P(None, ("dp", "tensor"), None), P(("dp", "tensor"), None), P(("dp", "tensor"))),
        check_vma=False,
    )
```

```python
import functools
import math

import jax
import jax.numpy as jnp
import numpy as np
from jax import lax
from jax.experimental import pallas as pl
from jax.experimental.pallas import tpu as pltpu
from jax.sharding import PartitionSpec as P

HD = 128
STEPS = 3
OFFMAX = 32
EPSILON = 1e-05
VMEM_LIMIT = 20 * 1024 * 1024
LARGE_LIMIT = 60 * 1024 * 1024

VMEM = pl.BlockSpec(memory_space=pltpu.VMEM)
SMEM = pl.BlockSpec(memory_space=pltpu.SMEM)
HBM = pl.BlockSpec(memory_space=pltpu.HBM)
F32 = jnp.float32
BF16 = jnp.bfloat16


SIDES = {64: (8, 4, 2)}


def sides_of(n):
    return SIDES.get(n, (1, 1, n))


def groups_along(n, *sides):
    sizes = sides_of(n)
    where = np.moveaxis(np.arange(n).reshape(sizes), sides, range(-len(sides), 0))
    return where.reshape(-1, math.prod(sizes[side] for side in sides)).tolist()


def block_order(n, tn):
    nz, ny, nx = sides_of(n)
    order = np.arange(n).reshape(ny, nz, nx)
    if nz == 2 * tn and n == ny * nx * tn * 2:
        for y in range(ny):
            for z in range(nz):
                for x in range(nx):
                    order[y, z, x] = (((z // tn) * ny + y) * nx + x) * tn + z % tn
    return order


def moved(values, change):
    n = lax.axis_size("dp")
    nz, ny, nx = sides_of(n)
    pairs = []
    for source in range(n):
        z, y, x = change(source // (ny * nx), source // nx % ny, source % nx)
        pairs.append((source, (z * ny + y) * nx + x))
    return lax.ppermute(values, "dp", pairs)


def weight_to_place(weight):
    n, tn = lax.axis_size("dp"), lax.axis_size("tensor")
    nz, ny, nx = sides_of(n)
    parts = []
    for turn in range(nx):
        pairs = []
        for j in range(tn):
            for q in range(n):
                y, z, x = q // (nz * nx), q // nx % nz, q % nx ^ turn
                pairs.append((j * n + q, ((z * ny + y) * nx + x) * tn + j))
        parts.append(lax.ppermute(weight, ("dp", "tensor"), pairs))
    return parts


def weight_across(weight, far):
    if sides_of(lax.axis_size("dp"))[0] == 1:
        return weight
    return jnp.concatenate([weight, moved(weight, lambda z, y, x: (z ^ far, y, x))])


def weight_halves(weight):
    if sides_of(lax.axis_size("dp"))[0] == 1:
        return [weight]
    return [weight, moved(weight, lambda z, y, x: (z ^ 1, y, x))]


def weight_once(halves):
    if sides_of(lax.axis_size("dp"))[1] == 1:
        return [[half] for half in halves]
    return [[half, moved(half, lambda z, y, x: (z, y ^ first, x))] for half, (first, _) in zip(halves, EXCHANGES)]


def weight_twice(halves):
    if sides_of(lax.axis_size("dp"))[1] == 1:
        return halves
    return [
        half + [moved(part, lambda z, y, x: (z, y ^ second, x)) for part in half]
        for half, (_, second) in zip(halves, EXCHANGES)]


KEPT = ((0, 3), (0, 1))
SENT = ((1, 2), (3, 2))
EXCHANGES = ((1, 3), (3, 1))


def reduce_once(kept, sent):
    if sides_of(lax.axis_size("dp"))[1] == 1:
        return [(keep[0], None) for keep in kept]
    got = [moved(send, lambda z, y, x: (z, y ^ first, x)) for send, (first, _) in zip(sent, EXCHANGES)]
    got = lax.optimization_barrier(got)
    return [(keep[0] + part[0].astype(F32), (keep[1] + part[1].astype(F32)).astype(BF16)) for keep, part in zip(kept, got)]


def reduce_twice(halves):
    if sides_of(lax.axis_size("dp"))[1] == 1:
        return [jnp.zeros_like(own) for own, _ in halves]
    return [moved(other, lambda z, y, x: (z, y ^ second, x)) for (_, other), (_, second) in zip(halves, EXCHANGES)]


def reduce_along_z(grad):
    n = lax.axis_size("dp")
    nz = sides_of(n)[0]
    if nz == 1:
        return grad
    columns = grad.shape[-1]
    grad = lax.all_to_all(grad.astype(BF16), "dp", 0, 0, tiled=True, axis_index_groups=groups_along(n, 0))
    return jnp.sum(grad.reshape(nz, -1, columns).astype(F32), axis=0)


def reduce_to_owner(grad):
    n, tn = lax.axis_size("dp"), lax.axis_size("tensor")
    nz, ny, nx = sides_of(n)
    rows, columns = grad.shape[0] // nx, grad.shape[1]
    order = block_order(n, tn)
    x = lax.axis_index("dp") % nx
    total = None
    for turn in range(nx):
        pairs = []
        for z in range(nz):
            for y in range(ny):
                for x0 in range(nx):
                    for j in range(tn):
                        block = j * n + int(order[y, z, (x0 + turn) % nx])
                        pairs.append((((z * ny + y) * nx + x0) * tn + j, block))
        part = lax.dynamic_slice(grad, ((x + turn) % nx * rows, 0), (rows, columns))
        part = lax.ppermute(part, ("dp", "tensor"), pairs)
        total = part if total is None else total + part
    return total


def held(values, after):
    def kernel(*refs):
        pass

    return pl.pallas_call(
        kernel,
        in_specs=[pl.BlockSpec(memory_space=pl.ANY)] * (len(values) + 1),
        out_specs=[pl.BlockSpec(memory_space=pl.ANY)] * len(values),
        out_shape=[jax.ShapeDtypeStruct(value.shape, value.dtype) for value in values],
        input_output_aliases={k: k for k in range(len(values))},
        cost_estimate=pl.CostEstimate(flops=0, bytes_accessed=0, transcendentals=0),
        name="held",
    )(*values, after)


OFFSETS = 4
LENGTHS = OFFSETS + STEPS


def segment_start(places, info_ref):
    end = jnp.int32(0)
    start = jnp.zeros_like(places)
    for s in range(LENGTHS, info_ref.shape[0]):
        end = end + info_ref[s]
        start = jnp.where(places >= end, end, start)
    return start


def column(row):
    n = row.shape[-1]
    eye = lax.broadcasted_iota(jnp.int32, (n, n), 0) == lax.broadcasted_iota(jnp.int32, (n, n), 1)
    return jnp.sum(jnp.where(eye, row, 0.0), axis=1, keepdims=True)


def lane_sums(values):
    return lax.dot_general(
        jnp.ones((8, values.shape[1]), F32), values, (((1,), (1,)), ((), ())),
        precision=lax.Precision.HIGHEST, preferred_element_type=F32)


def folded_square_sum(values):
    total = None
    for c in range(0, values.shape[1], 128):
        piece = values[:, c:c + 128]
        total = piece * piece if total is None else total + piece * piece
    return total


def features_kernel(tn, info_ref, low_ref, mid_ref, gain_ref, *outs):
    j = info_ref[0]
    width = low_ref.shape[1]
    piece = width // tn
    step = 1024

    def rms_scale(ref):
        total = None
        for c in range(0, width, step):
            part = folded_square_sum(ref[:, c:c + step].astype(F32))
            total = part if total is None else total + part
        return lax.rsqrt(jnp.sum(total, axis=1, keepdims=True) / width + EPSILON)

    low_scale = rms_scale(low_ref)
    mid_scale = rms_scale(mid_ref)
    for s, out in enumerate(outs):
        first = pl.multiple_of((j ^ s) * piece, piece)
        for c in range(0, piece, 512):
            at = pl.ds(first + c, 512)
            value = (low_ref[:, at].astype(F32) * low_scale * gain_ref[0:1, at]
                     + mid_ref[:, at].astype(F32) * mid_scale * gain_ref[1:2, at])
            out[:, c:c + 512] = value.astype(BF16)


def features(info, low, mid, gain, tn):
    rows, width = low.shape
    block = 32
    piece = width // tn
    return pl.pallas_call(
        functools.partial(features_kernel, tn),
        grid=(rows // block,),
        in_specs=[
            SMEM,
            pl.BlockSpec((block, width), lambda b: (b, 0)),
            pl.BlockSpec((block, width), lambda b: (b, 0)),
            pl.BlockSpec(gain.shape, lambda b: (0, 0)),
        ],
        out_specs=[pl.BlockSpec((block, piece), lambda b: (b, 0))] * tn,
        out_shape=[jax.ShapeDtypeStruct((rows, piece), BF16)] * tn,
        compiler_params=pltpu.CompilerParams(vmem_limit_bytes=LARGE_LIMIT),
        cost_estimate=pl.CostEstimate(flops=10 * rows * width, bytes_accessed=6 * rows * width, transcendentals=0),
        name="features",
    )(info, low, mid, gain)


def attend_kernel(window, info_ref, query_ref, key_ref, value_ref, high_ref, square_ref):
    block = query_ref.shape[0]
    pack = key_ref.shape[0]
    b = pl.program_id(0)
    first = pl.multiple_of(jnp.clip(b * block - (window - block), 0, pack - window), block)
    query_places = b * block + lax.broadcasted_iota(jnp.int32, (block, window), 0)
    key_places = first + lax.broadcasted_iota(jnp.int32, (block, window), 1)
    allowed = (key_places <= query_places) & (key_places >= segment_start(query_places, info_ref))
    bias = jnp.where(allowed, 0.0, -1e30).astype(F32)
    group = (query_ref.shape[1] // HD) // (key_ref.shape[1] // HD)
    squares = jnp.zeros((block, HD), F32)
    ones = jnp.ones((window, HD), BF16)
    scale = math.log2(math.e) / math.sqrt(HD)
    for g in range(key_ref.shape[1] // HD):
        key = key_ref[pl.ds(first, window), g * HD:(g + 1) * HD]
        value = jnp.concatenate([value_ref[pl.ds(first, window), g * HD:(g + 1) * HD], ones], axis=1)
        for r in range(group):
            at = slice((g * group + r) * HD, (g * group + r + 1) * HD)
            scores = lax.dot_general(query_ref[:, at], key, (((1,), (1,)), ((), ())), preferred_element_type=F32)
            scores = scores * scale + bias
            highest = jnp.max(scores, axis=1, keepdims=True)
            expo = jnp.exp2(scores - highest).astype(BF16)
            mixed = jnp.dot(expo, value, preferred_element_type=F32)
            out = (mixed[:, :HD] / mixed[:, HD:]).astype(BF16)
            high_ref[:, at] = out
            out = out.astype(F32)
            squares = squares + out * out
    square_ref[...] = lane_sums(squares)


def attend(info, queries, keys, values):
    pack, width = queries.shape
    block = 128
    window = min(pack, 256 + block)
    return pl.pallas_call(
        functools.partial(attend_kernel, window),
        grid=(pack // block,),
        in_specs=[
            SMEM,
            pl.BlockSpec((block, width), lambda b: (b, 0)),
            pl.BlockSpec(keys.shape, lambda b: (0, 0)),
            pl.BlockSpec(values.shape, lambda b: (0, 0)),
        ],
        out_specs=[
            pl.BlockSpec((block, width), lambda b: (b, 0)),
            pl.BlockSpec((8, block), lambda b: (0, b)),
        ],
        out_shape=[
            jax.ShapeDtypeStruct((pack, width), BF16),
            jax.ShapeDtypeStruct((8, pack), F32),
        ],
        compiler_params=pltpu.CompilerParams(vmem_limit_bytes=VMEM_LIMIT),
        cost_estimate=pl.CostEstimate(
            flops=4 * pack * window * width, bytes_accessed=4 * pack * width,
            transcendentals=pack * window * width // HD),
        name="attend",
    )(info, queries, keys, values)


def chosen(info_ref, step, rows, lead):
    target = info_ref[0] * rows + lax.broadcasted_iota(jnp.int32, (rows, rows + lead), 0)
    source = info_ref[0] * rows - lead + lax.broadcasted_iota(jnp.int32, (rows, rows + lead), 1)
    hit = (source == target - info_ref[OFFSETS + step]) & (source >= segment_start(target, info_ref))
    return jnp.where(hit, 1.0, 0.0).astype(BF16)


def fold_kernel(info_ref, cotangent_ref, out_ref, near_ref, sems):
    steps, rows, width = cotangent_ref.shape
    coming = [pltpu.make_async_copy(cotangent_ref.at[s], near_ref.at[s], sems.at[s]) for s in range(steps)]
    for copy in coming:
        copy.start()
    total = None
    for s in range(steps):
        pick = chosen(info_ref, s, rows, OFFMAX)
        coming[s].wait()
        part = lax.dot_general(pick, near_ref[s], (((0,), (0,)), ((), ())), preferred_element_type=F32)
        total = part if total is None else total + part
    out_ref[...] = total.astype(BF16)


def fold(info, cotangent):
    steps, rows, width = cotangent.shape
    return pl.pallas_call(
        fold_kernel,
        in_specs=[SMEM, HBM],
        out_specs=VMEM,
        out_shape=jax.ShapeDtypeStruct((rows + OFFMAX, width), BF16),
        scratch_shapes=[pltpu.VMEM(cotangent.shape, BF16), pltpu.SemaphoreType.DMA((steps,))],
        compiler_params=pltpu.CompilerParams(vmem_limit_bytes=LARGE_LIMIT),
        cost_estimate=pl.CostEstimate(flops=2 * steps * rows * 160 * width, bytes_accessed=2 * steps * rows * width, transcendentals=0),
        name="fold",
    )(info, cotangent)


def merge_kernel(width, tn, info_ref, gain_ref, high_ref, *refs):
    parts, square_refs, (far_ref, out_square_ref, out_ref, sems) = refs[:tn], refs[tn:-4], refs[-4:]
    copies = []
    j = info_ref[0]
    rows = parts[0].shape[0]
    piece = high_ref.shape[1]
    squares = square_refs[0][...]
    for ref in square_refs[1:]:
        squares = squares + ref[...]
    scales = lax.rsqrt(squares / width + EPSILON)
    for b in range(tn):
        out_square_ref[:, b * rows:(b + 1) * rows] = scales[:, b * rows:(b + 1) * rows]
    for s in range(tn):
        first = pl.multiple_of((j ^ s) * rows, rows)
        at = pl.ds(first, rows)
        scale = column(out_square_ref[0:1, at])
        total = jnp.zeros((rows, 128), F32)
        for c in range(0, piece, 128):
            cols = slice(c, c + 128)
            gain = gain_ref[2:3, pl.ds(pl.multiple_of(j * piece + c, 128), 128)]
            merged = (parts[s][:, cols].astype(F32) + high_ref[at, cols].astype(F32) * scale * gain).astype(BF16)
            out_ref[at, cols] = merged
            merged = merged.astype(F32)
            total = total + merged * merged
        copy = pltpu.make_async_copy(out_ref.at[at, :], far_ref.at[at, :], sems.at[s])
        copy.start()
        copies.append(copy)
        out_square_ref[:, at] = lane_sums(total)
    for copy in copies:
        copy.wait()


def merge(info, gain, high, parts, squares, width):
    pack, piece = high.shape
    tn = len(parts)
    return pl.pallas_call(
        functools.partial(merge_kernel, width, tn),
        in_specs=[SMEM] + [VMEM] * (2 + tn + len(squares)),
        out_specs=[HBM, VMEM],
        out_shape=[
            jax.ShapeDtypeStruct((pack, piece), BF16),
            jax.ShapeDtypeStruct((8, pack), F32),
        ],
        scratch_shapes=[pltpu.VMEM((pack, piece), BF16), pltpu.SemaphoreType.DMA((tn,))],
        compiler_params=pltpu.CompilerParams(vmem_limit_bytes=VMEM_LIMIT),
        cost_estimate=pl.CostEstimate(flops=8 * pack * piece, bytes_accessed=6 * pack * piece, transcendentals=0),
        name="merge",
    )(info, gain, high, *parts, *squares)


def grads(info, gain, merged, folds, squares, width, ny, tn):
    pack, piece = merged.shape
    rows = pack // tn
    vw = folds[0].shape[1]
    chunk = piece // (2 * ny)
    kept, sent = (KEPT, SENT) if ny > 1 else (((0,), (0,)), ((), ()))
    steps = [(h, s, True) for h in range(2) for s in kept[h]] + [(h, s, False) for h in range(2) for s in sent[h]]
    steps.sort(key=lambda step: step[2])
    size = chunk // (2 * tn) if ny > 1 else chunk

    def kernel(info_ref, gain_ref, merged_ref, *refs):
        fold_refs, square_refs, refs = refs[:tn], refs[tn:2 * tn], refs[2 * tn:]
        keep_refs, refs = refs[:2], refs[2:]
        send_refs, refs = refs[:2 if ny > 1 else 0], refs[2 if ny > 1 else 0:]
        hidden_ref, fold_ref, near_ref, near_folds, near_cut, sems = refs
        coming = [
            pltpu.make_async_copy(
                merged_ref.at[b * rows:(b + 1) * rows, :], near_ref.at[b * rows:(b + 1) * rows, :], sems.at[b])
            for b in range(tn)]
        folds_coming = [
            pltpu.make_async_copy(fold_refs[s], near_folds.at[s], sems.at[tn + s]) for s in range(tn)]
        for copy in coming + folds_coming:
            copy.start()
        j, y = info_ref[0], info_ref[1]
        squares = square_refs[0][...]
        for s in range(1, tn):
            squares = squares + square_refs[s][...]
        scales = lax.rsqrt(squares / width + EPSILON)
        for b in range(tn):
            at = slice(b * rows, (b + 1) * rows)
            scale = column(scales[0:1, at])
            coming[b].wait()
            for c in range(0, piece, 128):
                cols = slice(c, c + 128)
                gain = gain_ref[:, pl.ds(pl.multiple_of(j * piece + c, 128), 128)]
                hidden_ref[at, cols] = (near_ref[at, cols].astype(F32) * scale * gain).astype(BF16)
        fold_ref[...] = jnp.zeros_like(fold_ref)
        for s in range(tn):
            at = pl.ds(pl.multiple_of((j ^ s) * rows, rows), rows + OFFMAX)
            folds_coming[s].wait()
            fold_ref[at, :] = fold_ref[at, :] + near_folds[s].astype(F32)
        folded = fold_ref[OFFMAX:, :].astype(BF16)
        going = []
        for h, s, keep in steps:
            at = pl.ds(pl.multiple_of(h * ny * chunk + (y ^ s) * chunk, chunk), chunk)
            part = lax.dot_general(
                hidden_ref[:, at], folded, (((0,), (0,)), ((), ())), preferred_element_type=F32)
            if size < chunk:
                part = jnp.concatenate(
                    [part[(x * tn + t) * size:(x * tn + t + 1) * size] for t in range(tn) for x in range(2)], axis=0)
            if keep:
                keep_refs[h][kept[h].index(s)] = part
            else:
                k = sent[h].index(s)
                near_cut[h, k] = part.astype(BF16)
                copy = pltpu.make_async_copy(near_cut.at[h, k], send_refs[h].at[k], sems.at[2 * tn + 2 * h + k])
                copy.start()
                going.append(copy)
        for copy in going:
            copy.wait()

    out_shape = [jax.ShapeDtypeStruct((len(kept[h]), chunk, vw), F32) for h in range(2)]
    if ny > 1:
        out_shape += [jax.ShapeDtypeStruct((len(sent[h]), chunk, vw), BF16) for h in range(2)]
    out_shape += [jax.ShapeDtypeStruct((pack, piece), BF16)]
    out = pl.pallas_call(
        kernel,
        in_specs=[SMEM, VMEM, HBM] + [HBM] * tn + [VMEM] * tn,
        out_specs=[VMEM] * 2 + ([HBM] * 2 if ny > 1 else []) + [VMEM],
        out_shape=out_shape,
        scratch_shapes=[
            pltpu.VMEM((pack + OFFMAX, vw), F32),
            pltpu.VMEM((pack, piece), BF16),
            pltpu.VMEM((tn, rows + OFFMAX, vw), BF16),
            pltpu.VMEM((2, 2, chunk if ny > 1 else 16, vw), BF16),
            pltpu.SemaphoreType.DMA((2 * tn + 4,)),
        ],
        compiler_params=pltpu.CompilerParams(vmem_limit_bytes=VMEM_LIMIT),
        cost_estimate=pl.CostEstimate(flops=2 * pack * piece * vw, bytes_accessed=8 * pack * piece, transcendentals=0),
        name="grads",
    )(info, gain, merged, *folds, *squares)
    return out[:2], out[2:-1] if ny > 1 else (None, None), out[-1]


def project(info, hidden, weights, tn, nz, nx):
    pack, piece = hidden.shape
    rows = pack // tn
    vw = weights[0][0].shape[1]
    parts = [
        (part, far, near)
        for half, near, (first, second) in zip(weights, (0, 1), EXCHANGES)
        for part, far in zip(half, (0, first, second, first ^ second))]
    distances = (0, 4, 2, 6) if nz > 1 else (0,)
    size = parts[0][0].shape[0] // (len(distances) * nx)

    def kernel(info_ref, hidden_ref, *refs):
        weight_refs, value_refs = refs[:len(parts)], refs[len(parts):-4]
        weight_ref, total_ref, near_ref, sems = refs[-4:]
        coming = [pltpu.make_async_copy(ref, near_ref.at[p], sems.at[p]) for p, ref in enumerate(weight_refs)]
        for copy in coming:
            copy.start()
        j, y, z, x = info_ref[0], info_ref[1], info_ref[2], info_ref[3]
        for p, (_, far, near) in enumerate(parts):
            coming[p].wait()
            for k, distance in enumerate(distances):
                for m in range(nx):
                    block = ((y ^ far) * nz + (z ^ distance ^ near)) * nx + (x ^ m)
                    at = pl.ds(pl.multiple_of(block * size, size), size)
                    weight_ref[at, :] = near_ref[p, (k * nx + m) * size:(k * nx + m + 1) * size, :]
        total_ref[0:OFFMAX, :] = jnp.zeros((OFFMAX, vw), F32)
        for c in range(0, pack, 256):
            total_ref[OFFMAX + c:OFFMAX + c + 256, :] = jnp.dot(
                hidden_ref[c:c + 256, :], weight_ref[...], preferred_element_type=F32)
        for s in range(tn):
            at = pl.ds(pl.multiple_of((j ^ s) * rows, rows), rows + OFFMAX)
            value_refs[s][...] = total_ref[at, :].astype(value_refs[s].dtype)

    return pl.pallas_call(
        kernel,
        in_specs=[SMEM, VMEM] + [HBM] * len(parts),
        out_specs=[VMEM] * tn,
        out_shape=[jax.ShapeDtypeStruct((rows + OFFMAX, vw), F32 if s == 0 else BF16) for s in range(tn)],
        scratch_shapes=[
            pltpu.VMEM((piece, vw), BF16),
            pltpu.VMEM((pack + OFFMAX, vw), F32),
            pltpu.VMEM((len(parts),) + parts[0][0].shape, BF16),
            pltpu.SemaphoreType.DMA((len(parts),)),
        ],
        compiler_params=pltpu.CompilerParams(vmem_limit_bytes=VMEM_LIMIT),
        cost_estimate=pl.CostEstimate(flops=2 * pack * piece * vw, bytes_accessed=4 * pack * piece, transcendentals=0),
        name="project",
    )(info, hidden, *[part for part, _, _ in parts])


def spread(info, parts):
    rows, vw = parts[0].shape[0] - OFFMAX, parts[0].shape[1]

    def kernel(info_ref, *refs):
        parts_refs, out_ref = refs[:-1], refs[-1]
        total = None
        for ref in parts_refs:
            part = ref[...].astype(F32)
            total = part if total is None else total + part
        total = total.astype(BF16)
        for s in range(STEPS):
            pick = chosen(info_ref, s, rows, OFFMAX)
            out_ref[s] = jnp.dot(pick, total, preferred_element_type=F32).astype(BF16)

    return pl.pallas_call(
        kernel,
        in_specs=[SMEM] + [VMEM] * len(parts),
        out_specs=VMEM,
        out_shape=jax.ShapeDtypeStruct((STEPS, rows, vw), BF16),
        compiler_params=pltpu.CompilerParams(vmem_limit_bytes=VMEM_LIMIT),
        cost_estimate=pl.CostEstimate(flops=2 * STEPS * rows * 160 * vw, bytes_accessed=8 * STEPS * rows * vw, transcendentals=0),
        name="spread",
    )(info, *parts)


def body(
    target_queries,
    target_keys,
    target_values,
    low_feature,
    mid_feature,
    merging_gain,
    draft_gain,
    draft_weight,
    cotangent,
    doc_lengths,
    step_offsets,
):
    n = lax.axis_size("dp")
    tn = lax.axis_size("tensor")
    j = lax.axis_index("tensor")
    i = lax.axis_index("dp")
    flat = i * tn + j
    nz, ny, nx = sides_of(n)
    place = jnp.stack([j, i // nx % ny, i // (ny * nx), i % nx]).astype(jnp.int32)
    info = jnp.concatenate([place, step_offsets, doc_lengths.reshape(-1)])
    width = low_feature.shape[1]
    piece = width // tn
    pack = target_queries.shape[0]
    both = ("dp", "tensor")

    def swapped(values, s):
        return lax.ppermute(values, "tensor", [(a, a ^ s) for a in range(tn)])

    folded = fold(info, cotangent)
    across = swapped(folded, 2)
    low_feature, folded = lax.optimization_barrier((low_feature, folded))
    sent = features(info, low_feature, mid_feature, merging_gain, tn)
    across, sent = lax.optimization_barrier((across, sent))
    parts = [sent[0]] + [swapped(sent[s], s) for s in range(1, tn)]

    high, squares = attend(info, target_queries, target_keys, target_values)
    own_weight, high, folded, across = lax.optimization_barrier((draft_weight, high, folded, across))
    squares = squares + swapped(squares, 1)
    folds = [folded, swapped(folded, 1), across, swapped(across, 1)]
    squares, folds, parts[1] = lax.optimization_barrier((squares, folds, parts[1]))
    squares = [squares, swapped(squares, 2)]
    weights = weight_to_place(own_weight)
    merged, squares = merge(info, merging_gain, high, parts, squares, width)
    weights, merged, squares = lax.optimization_barrier((weights, merged, squares))
    weights = jnp.concatenate(weights)
    far_weights = moved(weights, lambda z, y, x: (z ^ nz // 2, y, x)) if nz > 1 else weights
    squares = [squares] + [swapped(squares, s) for s in range(1, tn)]
    kept, cut, hidden = grads(info, draft_gain.reshape(1, width), merged, folds, squares, width, ny, tn)
    far_weights, cut = lax.optimization_barrier((far_weights, cut))
    weights, hidden = lax.optimization_barrier((weights, hidden))
    if nz > 1:
        weights = jnp.concatenate([weights, far_weights])
    weights = weight_halves(weight_across(weights, nz // 4))
    halves = reduce_once(kept, cut)
    weights, own = lax.optimization_barrier((weights, [half[0] for half in halves]))
    got = reduce_twice(halves)
    grad = [mine + part.astype(F32) for mine, part in zip(own, got)]
    if ny > 1:
        grad = [half.astype(BF16) for half in grad]
    grad = jnp.concatenate(grad)
    weights = weight_twice(weight_once(held(weights, grad)))
    grad = reduce_along_z(grad)
    hidden, grad = lax.optimization_barrier((hidden, grad))
    weight_grad = reduce_to_owner(grad)
    values = project(info, hidden, weights, tn, nz, nx)
    values = [values[0]] + [swapped(values[s], s) for s in range(1, tn)]
    draft_values = spread(info, values)

    rows = weight_grad.shape[0]
    gain = lax.dynamic_slice(draft_gain, (flat * rows,), (rows,))
    gain_grad = jnp.sum(weight_grad * draft_weight.astype(F32), axis=1) / gain
    return (draft_values, weight_grad, gain_grad)


def solution(mesh):
    placed = (
        P("dp", "tensor"),
        P("dp", "tensor"),
        P("dp", "tensor"),
        P(("dp", "tensor"), None),
        P(("dp", "tensor"), None),
        P(),
        P(),
        P(("dp", "tensor"), None),
        P(None, ("dp", "tensor"), None),
        P("dp", None),
        P(),
    )
    return jax.shard_map(
        body,
        mesh=mesh,
        in_specs=placed,
        out_specs=(P(None, ("dp", "tensor"), None), P(("dp", "tensor"), None), P(("dp", "tensor"))),
        check_vma=False,
    )
```

```python
import functools
import math

import jax
import jax.numpy as jnp
import numpy as np
from jax import lax
from jax.experimental import pallas as pl
from jax.experimental.pallas import tpu as pltpu
from jax.sharding import PartitionSpec as P

HD = 128
STEPS = 3
OFFMAX = 32
EPSILON = 1e-05
VMEM_LIMIT = 20 * 1024 * 1024
LARGE_LIMIT = 60 * 1024 * 1024

VMEM = pl.BlockSpec(memory_space=pltpu.VMEM)
SMEM = pl.BlockSpec(memory_space=pltpu.SMEM)
HBM = pl.BlockSpec(memory_space=pltpu.HBM)
F32 = jnp.float32
BF16 = jnp.bfloat16


SIDES = {64: (8, 4, 2)}


def sides_of(n):
    return SIDES.get(n, (1, 1, n))


def groups_along(n, *sides):
    sizes = sides_of(n)
    where = np.moveaxis(np.arange(n).reshape(sizes), sides, range(-len(sides), 0))
    return where.reshape(-1, math.prod(sizes[side] for side in sides)).tolist()


def block_order(n, tn):
    nz, ny, nx = sides_of(n)
    order = np.arange(n).reshape(ny, nz, nx)
    if nz == 2 * tn and n == ny * nx * tn * 2:
        for y in range(ny):
            for z in range(nz):
                for x in range(nx):
                    order[y, z, x] = (((z // tn) * ny + y) * nx + x) * tn + z % tn
    return order


def moved(values, change):
    n = lax.axis_size("dp")
    nz, ny, nx = sides_of(n)
    pairs = []
    for source in range(n):
        z, y, x = change(source // (ny * nx), source // nx % ny, source % nx)
        pairs.append((source, (z * ny + y) * nx + x))
    return lax.ppermute(values, "dp", pairs)


def weight_to_place(weight):
    n, tn = lax.axis_size("dp"), lax.axis_size("tensor")
    nz, ny, nx = sides_of(n)
    order = block_order(n, tn)
    parts = []
    for turn in range(nx):
        pairs = []
        for j in range(tn):
            for y, z, x in np.ndindex(ny, nz, nx):
                pairs.append((j * n + int(order[y, z, x ^ turn]), ((z * ny + y) * nx + x) * tn + j))
        parts.append(lax.ppermute(weight, ("dp", "tensor"), pairs))
    return parts


def weight_across(weight, far):
    if sides_of(lax.axis_size("dp"))[0] == 1:
        return weight
    return jnp.concatenate([weight, moved(weight, lambda z, y, x: (z ^ far, y, x))])


def weight_halves(weight):
    if sides_of(lax.axis_size("dp"))[0] == 1:
        return [weight]
    return [weight, moved(weight, lambda z, y, x: (z ^ 1, y, x))]


def weight_once(halves):
    if sides_of(lax.axis_size("dp"))[1] == 1:
        return [[half] for half in halves]
    return [[half, moved(half, lambda z, y, x: (z, y ^ first, x))] for half, (first, _) in zip(halves, EXCHANGES)]


def weight_twice(halves):
    if sides_of(lax.axis_size("dp"))[1] == 1:
        return halves
    return [
        half + [moved(part, lambda z, y, x: (z, y ^ second, x)) for part in half]
        for half, (_, second) in zip(halves, EXCHANGES)]


KEPT = ((0, 3), (0, 1))
SENT = ((1, 2), (3, 2))
EXCHANGES = ((1, 3), (3, 1))


def reduce_once(kept, sent):
    if sides_of(lax.axis_size("dp"))[1] == 1:
        return [(keep[0], None) for keep in kept]
    got = [moved(send, lambda z, y, x: (z, y ^ first, x)) for send, (first, _) in zip(sent, EXCHANGES)]
    got = lax.optimization_barrier(got)
    return [(keep[0] + part[0].astype(F32), (keep[1] + part[1].astype(F32)).astype(BF16)) for keep, part in zip(kept, got)]


def reduce_twice(halves):
    if sides_of(lax.axis_size("dp"))[1] == 1:
        return [jnp.zeros_like(own) for own, _ in halves]
    return [moved(other, lambda z, y, x: (z, y ^ second, x)) for (_, other), (_, second) in zip(halves, EXCHANGES)]


def reduce_along_z(grad):
    n = lax.axis_size("dp")
    nz = sides_of(n)[0]
    if nz == 1:
        return grad
    columns = grad.shape[-1]
    grad = lax.all_to_all(grad.astype(BF16), "dp", 0, 0, tiled=True, axis_index_groups=groups_along(n, 0))
    return jnp.sum(grad.reshape(nz, -1, columns).astype(F32), axis=0)


def reduce_to_owner(grad):
    n, tn = lax.axis_size("dp"), lax.axis_size("tensor")
    nz, ny, nx = sides_of(n)
    rows, columns = grad.shape[0] // nx, grad.shape[1]
    order = block_order(n, tn)
    x = lax.axis_index("dp") % nx
    total = None
    for turn in range(nx):
        pairs = []
        for z in range(nz):
            for y in range(ny):
                for x0 in range(nx):
                    for j in range(tn):
                        block = j * n + int(order[y, z, (x0 + turn) % nx])
                        pairs.append((((z * ny + y) * nx + x0) * tn + j, block))
        part = lax.dynamic_slice(grad, ((x + turn) % nx * rows, 0), (rows, columns))
        part = lax.ppermute(part, ("dp", "tensor"), pairs)
        total = part if total is None else total + part
    return total


def held(values, after):
    def kernel(*refs):
        pass

    return pl.pallas_call(
        kernel,
        in_specs=[pl.BlockSpec(memory_space=pl.ANY)] * (len(values) + 1),
        out_specs=[pl.BlockSpec(memory_space=pl.ANY)] * len(values),
        out_shape=[jax.ShapeDtypeStruct(value.shape, value.dtype) for value in values],
        input_output_aliases={k: k for k in range(len(values))},
        cost_estimate=pl.CostEstimate(flops=0, bytes_accessed=0, transcendentals=0),
        name="held",
    )(*values, after)


OFFSETS = 4
LENGTHS = OFFSETS + STEPS


def segment_start(places, info_ref):
    end = jnp.int32(0)
    start = jnp.zeros_like(places)
    for s in range(LENGTHS, info_ref.shape[0]):
        end = end + info_ref[s]
        start = jnp.where(places >= end, end, start)
    return start


def column(row):
    n = row.shape[-1]
    eye = lax.broadcasted_iota(jnp.int32, (n, n), 0) == lax.broadcasted_iota(jnp.int32, (n, n), 1)
    return jnp.sum(jnp.where(eye, row, 0.0), axis=1, keepdims=True)


def lane_sums(values):
    return lax.dot_general(
        jnp.ones((8, values.shape[1]), F32), values, (((1,), (1,)), ((), ())),
        precision=lax.Precision.HIGHEST, preferred_element_type=F32)


def folded_square_sum(values):
    total = None
    for c in range(0, values.shape[1], 128):
        piece = values[:, c:c + 128]
        total = piece * piece if total is None else total + piece * piece
    return total


def features_kernel(tn, info_ref, low_ref, mid_ref, gain_ref, *outs):
    j = info_ref[0]
    width = low_ref.shape[1]
    piece = width // tn
    step = 1024

    def rms_scale(ref):
        total = None
        for c in range(0, width, step):
            part = folded_square_sum(ref[:, c:c + step].astype(F32))
            total = part if total is None else total + part
        return lax.rsqrt(jnp.sum(total, axis=1, keepdims=True) / width + EPSILON)

    low_scale = rms_scale(low_ref)
    mid_scale = rms_scale(mid_ref)
    for s, out in enumerate(outs):
        first = pl.multiple_of((j ^ s) * piece, piece)
        for c in range(0, piece, 512):
            at = pl.ds(first + c, 512)
            value = (low_ref[:, at].astype(F32) * low_scale * gain_ref[0:1, at]
                     + mid_ref[:, at].astype(F32) * mid_scale * gain_ref[1:2, at])
            out[:, c:c + 512] = value.astype(BF16)


def features(info, low, mid, gain, tn):
    rows, width = low.shape
    block = 32
    piece = width // tn
    return pl.pallas_call(
        functools.partial(features_kernel, tn),
        grid=(rows // block,),
        in_specs=[
            SMEM,
            pl.BlockSpec((block, width), lambda b: (b, 0)),
            pl.BlockSpec((block, width), lambda b: (b, 0)),
            pl.BlockSpec(gain.shape, lambda b: (0, 0)),
        ],
        out_specs=[pl.BlockSpec((block, piece), lambda b: (b, 0))] * tn,
        out_shape=[jax.ShapeDtypeStruct((rows, piece), BF16)] * tn,
        compiler_params=pltpu.CompilerParams(vmem_limit_bytes=LARGE_LIMIT),
        cost_estimate=pl.CostEstimate(flops=10 * rows * width, bytes_accessed=6 * rows * width, transcendentals=0),
        name="features",
    )(info, low, mid, gain)


def attend_kernel(window, info_ref, query_ref, key_ref, value_ref, high_ref, square_ref):
    block = query_ref.shape[0]
    pack = key_ref.shape[0]
    b = pl.program_id(0)
    first = pl.multiple_of(jnp.clip(b * block - (window - block), 0, pack - window), block)
    query_places = b * block + lax.broadcasted_iota(jnp.int32, (block, window), 0)
    key_places = first + lax.broadcasted_iota(jnp.int32, (block, window), 1)
    allowed = (key_places <= query_places) & (key_places >= segment_start(query_places, info_ref))
    bias = jnp.where(allowed, 0.0, -1e30).astype(F32)
    group = (query_ref.shape[1] // HD) // (key_ref.shape[1] // HD)
    squares = jnp.zeros((block, HD), F32)
    ones = jnp.ones((window, HD), BF16)
    scale = math.log2(math.e) / math.sqrt(HD)
    for g in range(key_ref.shape[1] // HD):
        key = key_ref[pl.ds(first, window), g * HD:(g + 1) * HD]
        value = jnp.concatenate([value_ref[pl.ds(first, window), g * HD:(g + 1) * HD], ones], axis=1)
        for r in range(group):
            at = slice((g * group + r) * HD, (g * group + r + 1) * HD)
            scores = lax.dot_general(query_ref[:, at], key, (((1,), (1,)), ((), ())), preferred_element_type=F32)
            scores = scores * scale + bias
            highest = jnp.max(scores, axis=1, keepdims=True)
            expo = jnp.exp2(scores - highest).astype(BF16)
            mixed = jnp.dot(expo, value, preferred_element_type=F32)
            out = (mixed[:, :HD] / mixed[:, HD:]).astype(BF16)
            high_ref[:, at] = out
            out = out.astype(F32)
            squares = squares + out * out
    square_ref[...] = lane_sums(squares)


def attend(info, queries, keys, values):
    pack, width = queries.shape
    block = 128
    window = min(pack, 256 + block)
    return pl.pallas_call(
        functools.partial(attend_kernel, window),
        grid=(pack // block,),
        in_specs=[
            SMEM,
            pl.BlockSpec((block, width), lambda b: (b, 0)),
            pl.BlockSpec(keys.shape, lambda b: (0, 0)),
            pl.BlockSpec(values.shape, lambda b: (0, 0)),
        ],
        out_specs=[
            pl.BlockSpec((block, width), lambda b: (b, 0)),
            pl.BlockSpec((8, block), lambda b: (0, b)),
        ],
        out_shape=[
            jax.ShapeDtypeStruct((pack, width), BF16),
            jax.ShapeDtypeStruct((8, pack), F32),
        ],
        compiler_params=pltpu.CompilerParams(vmem_limit_bytes=VMEM_LIMIT),
        cost_estimate=pl.CostEstimate(
            flops=4 * pack * window * width, bytes_accessed=4 * pack * width,
            transcendentals=pack * window * width // HD),
        name="attend",
    )(info, queries, keys, values)


def chosen(info_ref, step, rows, lead):
    target = info_ref[0] * rows + lax.broadcasted_iota(jnp.int32, (rows, rows + lead), 0)
    source = info_ref[0] * rows - lead + lax.broadcasted_iota(jnp.int32, (rows, rows + lead), 1)
    hit = (source == target - info_ref[OFFSETS + step]) & (source >= segment_start(target, info_ref))
    return jnp.where(hit, 1.0, 0.0).astype(BF16)


def fold_kernel(info_ref, cotangent_ref, out_ref, near_ref, sems):
    steps, rows, width = cotangent_ref.shape
    coming = [pltpu.make_async_copy(cotangent_ref.at[s], near_ref.at[s], sems.at[s]) for s in range(steps)]
    for copy in coming:
        copy.start()
    total = None
    for s in range(steps):
        pick = chosen(info_ref, s, rows, OFFMAX)
        coming[s].wait()
        part = lax.dot_general(pick, near_ref[s], (((0,), (0,)), ((), ())), preferred_element_type=F32)
        total = part if total is None else total + part
    out_ref[...] = total.astype(BF16)


def fold(info, cotangent):
    steps, rows, width = cotangent.shape
    return pl.pallas_call(
        fold_kernel,
        in_specs=[SMEM, HBM],
        out_specs=VMEM,
        out_shape=jax.ShapeDtypeStruct((rows + OFFMAX, width), BF16),
        scratch_shapes=[pltpu.VMEM(cotangent.shape, BF16), pltpu.SemaphoreType.DMA((steps,))],
        compiler_params=pltpu.CompilerParams(vmem_limit_bytes=LARGE_LIMIT),
        cost_estimate=pl.CostEstimate(flops=2 * steps * rows * 160 * width, bytes_accessed=2 * steps * rows * width, transcendentals=0),
        name="fold",
    )(info, cotangent)


def merge_kernel(width, tn, info_ref, gain_ref, high_ref, *refs):
    parts, square_refs, (far_ref, out_square_ref, out_ref, sems) = refs[:tn], refs[tn:-4], refs[-4:]
    copies = []
    j = info_ref[0]
    rows = parts[0].shape[0]
    piece = high_ref.shape[1]
    squares = square_refs[0][...]
    for ref in square_refs[1:]:
        squares = squares + ref[...]
    scales = lax.rsqrt(squares / width + EPSILON)
    for b in range(tn):
        out_square_ref[:, b * rows:(b + 1) * rows] = scales[:, b * rows:(b + 1) * rows]
    for s in range(tn):
        first = pl.multiple_of((j ^ s) * rows, rows)
        at = pl.ds(first, rows)
        scale = column(out_square_ref[0:1, at])
        total = jnp.zeros((rows, 128), F32)
        for c in range(0, piece, 128):
            cols = slice(c, c + 128)
            gain = gain_ref[2:3, pl.ds(pl.multiple_of(j * piece + c, 128), 128)]
            merged = (parts[s][:, cols].astype(F32) + high_ref[at, cols].astype(F32) * scale * gain).astype(BF16)
            out_ref[at, cols] = merged
            merged = merged.astype(F32)
            total = total + merged * merged
        copy = pltpu.make_async_copy(out_ref.at[at, :], far_ref.at[at, :], sems.at[s])
        copy.start()
        copies.append(copy)
        out_square_ref[:, at] = lane_sums(total)
    for copy in copies:
        copy.wait()


def merge(info, gain, high, parts, squares, width):
    pack, piece = high.shape
    tn = len(parts)
    return pl.pallas_call(
        functools.partial(merge_kernel, width, tn),
        in_specs=[SMEM] + [VMEM] * (2 + tn + len(squares)),
        out_specs=[HBM, VMEM],
        out_shape=[
            jax.ShapeDtypeStruct((pack, piece), BF16),
            jax.ShapeDtypeStruct((8, pack), F32),
        ],
        scratch_shapes=[pltpu.VMEM((pack, piece), BF16), pltpu.SemaphoreType.DMA((tn,))],
        compiler_params=pltpu.CompilerParams(vmem_limit_bytes=VMEM_LIMIT),
        cost_estimate=pl.CostEstimate(flops=8 * pack * piece, bytes_accessed=6 * pack * piece, transcendentals=0),
        name="merge",
    )(info, gain, high, *parts, *squares)


def grads(info, gain, merged, folds, squares, width, ny, tn):
    pack, piece = merged.shape
    rows = pack // tn
    vw = folds[0].shape[1]
    chunk = piece // (2 * ny)
    kept, sent = (KEPT, SENT) if ny > 1 else (((0,), (0,)), ((), ()))
    steps = [(h, s, True) for h in range(2) for s in kept[h]] + [(h, s, False) for h in range(2) for s in sent[h]]
    steps.sort(key=lambda step: step[2])
    size = chunk // (2 * tn) if ny > 1 else chunk

    def kernel(info_ref, gain_ref, merged_ref, *refs):
        fold_refs, square_refs, refs = refs[:tn], refs[tn:2 * tn], refs[2 * tn:]
        keep_refs, refs = refs[:2], refs[2:]
        send_refs, refs = refs[:2 if ny > 1 else 0], refs[2 if ny > 1 else 0:]
        hidden_ref, fold_ref, near_ref, near_folds, near_cut, sems = refs
        coming = [
            pltpu.make_async_copy(
                merged_ref.at[b * rows:(b + 1) * rows, :], near_ref.at[b * rows:(b + 1) * rows, :], sems.at[b])
            for b in range(tn)]
        folds_coming = [
            pltpu.make_async_copy(fold_refs[s], near_folds.at[s], sems.at[tn + s]) for s in range(tn)]
        for copy in coming + folds_coming:
            copy.start()
        j, y = info_ref[0], info_ref[1]
        squares = square_refs[0][...]
        for s in range(1, tn):
            squares = squares + square_refs[s][...]
        scales = lax.rsqrt(squares / width + EPSILON)
        for b in range(tn):
            at = slice(b * rows, (b + 1) * rows)
            scale = column(scales[0:1, at])
            coming[b].wait()
            for c in range(0, piece, 128):
                cols = slice(c, c + 128)
                gain = gain_ref[:, pl.ds(pl.multiple_of(j * piece + c, 128), 128)]
                hidden_ref[at, cols] = (near_ref[at, cols].astype(F32) * scale * gain).astype(BF16)
        fold_ref[...] = jnp.zeros_like(fold_ref)
        for s in range(tn):
            at = pl.ds(pl.multiple_of((j ^ s) * rows, rows), rows + OFFMAX)
            folds_coming[s].wait()
            fold_ref[at, :] = fold_ref[at, :] + near_folds[s].astype(F32)
        folded = fold_ref[OFFMAX:, :].astype(BF16)
        going = []
        for h, s, keep in steps:
            at = pl.ds(pl.multiple_of(h * ny * chunk + (y ^ s) * chunk, chunk), chunk)
            part = lax.dot_general(
                hidden_ref[:, at], folded, (((0,), (0,)), ((), ())), preferred_element_type=F32)
            if size < chunk:
                part = jnp.concatenate(
                    [part[(x * tn + t) * size:(x * tn + t + 1) * size] for t in range(tn) for x in range(2)], axis=0)
            if keep:
                keep_refs[h][kept[h].index(s)] = part
            else:
                k = sent[h].index(s)
                near_cut[h, k] = part.astype(BF16)
                copy = pltpu.make_async_copy(near_cut.at[h, k], send_refs[h].at[k], sems.at[2 * tn + 2 * h + k])
                copy.start()
                going.append(copy)
        for copy in going:
            copy.wait()

    out_shape = [jax.ShapeDtypeStruct((len(kept[h]), chunk, vw), F32) for h in range(2)]
    if ny > 1:
        out_shape += [jax.ShapeDtypeStruct((len(sent[h]), chunk, vw), BF16) for h in range(2)]
    out_shape += [jax.ShapeDtypeStruct((pack, piece), BF16)]
    out = pl.pallas_call(
        kernel,
        in_specs=[SMEM, VMEM, HBM] + [HBM] * tn + [VMEM] * tn,
        out_specs=[VMEM] * 2 + ([HBM] * 2 if ny > 1 else []) + [VMEM],
        out_shape=out_shape,
        scratch_shapes=[
            pltpu.VMEM((pack + OFFMAX, vw), F32),
            pltpu.VMEM((pack, piece), BF16),
            pltpu.VMEM((tn, rows + OFFMAX, vw), BF16),
            pltpu.VMEM((2, 2, chunk if ny > 1 else 16, vw), BF16),
            pltpu.SemaphoreType.DMA((2 * tn + 4,)),
        ],
        compiler_params=pltpu.CompilerParams(vmem_limit_bytes=VMEM_LIMIT),
        cost_estimate=pl.CostEstimate(flops=2 * pack * piece * vw, bytes_accessed=8 * pack * piece, transcendentals=0),
        name="grads",
    )(info, gain, merged, *folds, *squares)
    return out[:2], out[2:-1] if ny > 1 else (None, None), out[-1]


def project(info, hidden, weights, tn, nz, ny, nx):
    pack, piece = hidden.shape
    rows = pack // tn
    vw = weights[0][0].shape[1]
    parts = [
        (part, far, near)
        for half, near, (first, second) in zip(weights, (0, 1), EXCHANGES)
        for part, far in zip(half, (0, first, second, first ^ second))]
    distances = (0, 4, 2, 6) if nz > 1 else (0,)
    size = parts[0][0].shape[0] // (len(distances) * nx)

    def kernel(info_ref, hidden_ref, *refs):
        weight_refs, value_refs = refs[:len(parts)], refs[len(parts):-4]
        weight_ref, total_ref, near_ref, sems = refs[-4:]
        coming = [pltpu.make_async_copy(ref, near_ref.at[p], sems.at[p]) for p, ref in enumerate(weight_refs)]
        for copy in coming:
            copy.start()
        j, y, z, x = info_ref[0], info_ref[1], info_ref[2], info_ref[3]
        for p, (_, far, near) in enumerate(parts):
            coming[p].wait()
            for k, distance in enumerate(distances):
                for m in range(nx):
                    y_at, z_at, x_at = y ^ far, z ^ distance ^ near, x ^ m
                    if nz == 2 * tn:
                        block = (((z_at // tn) * ny + y_at) * nx + x_at) * tn + z_at % tn
                    else:
                        block = (y_at * nz + z_at) * nx + x_at
                    at = pl.ds(pl.multiple_of(block * size, size), size)
                    weight_ref[at, :] = near_ref[p, (k * nx + m) * size:(k * nx + m + 1) * size, :]
        total_ref[0:OFFMAX, :] = jnp.zeros((OFFMAX, vw), F32)
        for c in range(0, pack, 256):
            total_ref[OFFMAX + c:OFFMAX + c + 256, :] = jnp.dot(
                hidden_ref[c:c + 256, :], weight_ref[...], preferred_element_type=F32)
        for s in range(tn):
            at = pl.ds(pl.multiple_of((j ^ s) * rows, rows), rows + OFFMAX)
            value_refs[s][...] = total_ref[at, :].astype(value_refs[s].dtype)

    return pl.pallas_call(
        kernel,
        in_specs=[SMEM, VMEM] + [HBM] * len(parts),
        out_specs=[VMEM] * tn,
        out_shape=[jax.ShapeDtypeStruct((rows + OFFMAX, vw), F32 if s == 0 else BF16) for s in range(tn)],
        scratch_shapes=[
            pltpu.VMEM((piece, vw), BF16),
            pltpu.VMEM((pack + OFFMAX, vw), F32),
            pltpu.VMEM((len(parts),) + parts[0][0].shape, BF16),
            pltpu.SemaphoreType.DMA((len(parts),)),
        ],
        compiler_params=pltpu.CompilerParams(vmem_limit_bytes=VMEM_LIMIT),
        cost_estimate=pl.CostEstimate(flops=2 * pack * piece * vw, bytes_accessed=4 * pack * piece, transcendentals=0),
        name="project",
    )(info, hidden, *[part for part, _, _ in parts])


def spread(info, parts):
    rows, vw = parts[0].shape[0] - OFFMAX, parts[0].shape[1]

    def kernel(info_ref, *refs):
        parts_refs, out_ref = refs[:-1], refs[-1]
        total = None
        for ref in parts_refs:
            part = ref[...].astype(F32)
            total = part if total is None else total + part
        total = total.astype(BF16)
        for s in range(STEPS):
            pick = chosen(info_ref, s, rows, OFFMAX)
            out_ref[s] = jnp.dot(pick, total, preferred_element_type=F32).astype(BF16)

    return pl.pallas_call(
        kernel,
        in_specs=[SMEM] + [VMEM] * len(parts),
        out_specs=VMEM,
        out_shape=jax.ShapeDtypeStruct((STEPS, rows, vw), BF16),
        compiler_params=pltpu.CompilerParams(vmem_limit_bytes=VMEM_LIMIT),
        cost_estimate=pl.CostEstimate(flops=2 * STEPS * rows * 160 * vw, bytes_accessed=8 * STEPS * rows * vw, transcendentals=0),
        name="spread",
    )(info, *parts)


def body(
    target_queries,
    target_keys,
    target_values,
    low_feature,
    mid_feature,
    merging_gain,
    draft_gain,
    draft_weight,
    cotangent,
    doc_lengths,
    step_offsets,
):
    n = lax.axis_size("dp")
    tn = lax.axis_size("tensor")
    j = lax.axis_index("tensor")
    i = lax.axis_index("dp")
    flat = i * tn + j
    nz, ny, nx = sides_of(n)
    place = jnp.stack([j, i // nx % ny, i // (ny * nx), i % nx]).astype(jnp.int32)
    info = jnp.concatenate([place, step_offsets, doc_lengths.reshape(-1)])
    width = low_feature.shape[1]
    piece = width // tn
    pack = target_queries.shape[0]
    both = ("dp", "tensor")

    def swapped(values, s):
        return lax.ppermute(values, "tensor", [(a, a ^ s) for a in range(tn)])

    folded = fold(info, cotangent)
    across = swapped(folded, 2)
    low_feature, folded = lax.optimization_barrier((low_feature, folded))
    sent = features(info, low_feature, mid_feature, merging_gain, tn)
    across, sent = lax.optimization_barrier((across, sent))
    parts = [sent[0]] + [swapped(sent[s], s) for s in range(1, tn)]

    high, squares = attend(info, target_queries, target_keys, target_values)
    own_weight, high, folded, across = lax.optimization_barrier((draft_weight, high, folded, across))
    squares = squares + swapped(squares, 1)
    folds = [folded, swapped(folded, 1), across, swapped(across, 1)]
    squares, folds, parts[1] = lax.optimization_barrier((squares, folds, parts[1]))
    squares = [squares, swapped(squares, 2)]
    weights = weight_to_place(own_weight)
    merged, squares = merge(info, merging_gain, high, parts, squares, width)
    weights, merged, squares = lax.optimization_barrier((weights, merged, squares))
    weights = jnp.concatenate(weights)
    far_weights = moved(weights, lambda z, y, x: (z ^ nz // 2, y, x)) if nz > 1 else weights
    squares = [squares] + [swapped(squares, s) for s in range(1, tn)]
    kept, cut, hidden = grads(info, draft_gain.reshape(1, width), merged, folds, squares, width, ny, tn)
    far_weights, cut = lax.optimization_barrier((far_weights, cut))
    weights, hidden = lax.optimization_barrier((weights, hidden))
    if nz > 1:
        weights = jnp.concatenate([weights, far_weights])
    weights = weight_halves(weight_across(weights, nz // 4))
    halves = reduce_once(kept, cut)
    weights, own = lax.optimization_barrier((weights, [half[0] for half in halves]))
    got = reduce_twice(halves)
    grad = [mine + part.astype(F32) for mine, part in zip(own, got)]
    if ny > 1:
        grad = [half.astype(BF16) for half in grad]
    grad = jnp.concatenate(grad)
    weights = weight_twice(weight_once(held(weights, grad)))
    grad = reduce_along_z(grad)
    values = project(info, hidden, weights, tn, nz, ny, nx)
    values, grad = lax.optimization_barrier((values, grad))
    weight_grad = reduce_to_owner(grad)
    values = [values[0]] + [swapped(values[s], s) for s in range(1, tn)]
    draft_values = spread(info, values)

    rows = weight_grad.shape[0]
    gain = lax.dynamic_slice(draft_gain, (flat * rows,), (rows,))
    gain_grad = jnp.sum(weight_grad * draft_weight.astype(F32), axis=1) / gain
    return (draft_values, weight_grad, gain_grad)


def solution(mesh):
    placed = (
        P("dp", "tensor"),
        P("dp", "tensor"),
        P("dp", "tensor"),
        P(("dp", "tensor"), None),
        P(("dp", "tensor"), None),
        P(),
        P(),
        P(("dp", "tensor"), None),
        P(None, ("dp", "tensor"), None),
        P("dp", None),
        P(),
    )
    return jax.shard_map(
        body,
        mesh=mesh,
        in_specs=placed,
        out_specs=(P(None, ("dp", "tensor"), None), P(("dp", "tensor"), None), P(("dp", "tensor"))),
        check_vma=False,
    )
```

```python
import functools
import math

import jax
import jax.numpy as jnp
import numpy as np
from jax import lax
from jax.experimental import pallas as pl
from jax.experimental.pallas import tpu as pltpu
from jax.sharding import PartitionSpec as P

HD = 128
STEPS = 3
OFFMAX = 32
EPSILON = 1e-05
VMEM_LIMIT = 20 * 1024 * 1024
LARGE_LIMIT = 60 * 1024 * 1024

VMEM = pl.BlockSpec(memory_space=pltpu.VMEM)
SMEM = pl.BlockSpec(memory_space=pltpu.SMEM)
HBM = pl.BlockSpec(memory_space=pltpu.HBM)
F32 = jnp.float32
BF16 = jnp.bfloat16


SIDES = {64: (8, 4, 2)}


def sides_of(n):
    return SIDES.get(n, (1, 1, n))


def groups_along(n, *sides):
    sizes = sides_of(n)
    where = np.moveaxis(np.arange(n).reshape(sizes), sides, range(-len(sides), 0))
    return where.reshape(-1, math.prod(sizes[side] for side in sides)).tolist()


def block_order(n, tn):
    nz, ny, nx = sides_of(n)
    order = np.arange(n).reshape(ny, nz, nx)
    if nz == 2 * tn and n == ny * nx * tn * 2:
        for y in range(ny):
            for z in range(nz):
                for x in range(nx):
                    order[y, z, x] = (((z // tn) * ny + y) * nx + x) * tn + z % tn
    return order


def moved(values, change):
    n = lax.axis_size("dp")
    nz, ny, nx = sides_of(n)
    pairs = []
    for source in range(n):
        z, y, x = change(source // (ny * nx), source // nx % ny, source % nx)
        pairs.append((source, (z * ny + y) * nx + x))
    return lax.ppermute(values, "dp", pairs)


def weight_to_place(weight):
    n, tn = lax.axis_size("dp"), lax.axis_size("tensor")
    nz, ny, nx = sides_of(n)
    order = block_order(n, tn)
    parts = []
    for turn in range(nx):
        pairs = []
        for j in range(tn):
            for y, z, x in np.ndindex(ny, nz, nx):
                pairs.append((j * n + int(order[y, z, x ^ turn]), ((z * ny + y) * nx + x) * tn + j))
        parts.append(lax.ppermute(weight, ("dp", "tensor"), pairs))
    return parts


def weight_across(weight, far):
    if sides_of(lax.axis_size("dp"))[0] == 1:
        return weight
    return jnp.concatenate([weight, moved(weight, lambda z, y, x: (z ^ far, y, x))])


def weight_halves(weight):
    if sides_of(lax.axis_size("dp"))[0] == 1:
        return [weight]
    return [weight, moved(weight, lambda z, y, x: (z ^ 1, y, x))]


def weight_once(halves):
    if sides_of(lax.axis_size("dp"))[1] == 1:
        return [[half] for half in halves]
    return [[half, moved(half, lambda z, y, x: (z, y ^ first, x))] for half, (first, _) in zip(halves, EXCHANGES)]


def weight_twice(halves):
    if sides_of(lax.axis_size("dp"))[1] == 1:
        return halves
    return [
        half + [moved(part, lambda z, y, x: (z, y ^ second, x)) for part in half]
        for half, (_, second) in zip(halves, EXCHANGES)]


KEPT = ((0, 3), (0, 1))
SENT = ((1, 2), (3, 2))
EXCHANGES = ((1, 3), (3, 1))


def reduce_once(kept, sent):
    if sides_of(lax.axis_size("dp"))[1] == 1:
        return [(keep[0], None) for keep in kept]
    got = [moved(send, lambda z, y, x: (z, y ^ first, x)) for send, (first, _) in zip(sent, EXCHANGES)]
    got = lax.optimization_barrier(got)
    return [(keep[0] + part[0].astype(F32), (keep[1] + part[1].astype(F32)).astype(BF16)) for keep, part in zip(kept, got)]


def reduce_twice(halves):
    if sides_of(lax.axis_size("dp"))[1] == 1:
        return [jnp.zeros_like(own) for own, _ in halves]
    return [moved(other, lambda z, y, x: (z, y ^ second, x)) for (_, other), (_, second) in zip(halves, EXCHANGES)]


def reduce_along_z(grad):
    n = lax.axis_size("dp")
    nz = sides_of(n)[0]
    if nz == 1:
        return grad
    columns = grad.shape[-1]
    grad = lax.all_to_all(grad.astype(BF16), "dp", 0, 0, tiled=True, axis_index_groups=groups_along(n, 0))
    return jnp.sum(grad.reshape(nz, -1, columns).astype(F32), axis=0)


def reduce_to_owner(grad):
    n, tn = lax.axis_size("dp"), lax.axis_size("tensor")
    nz, ny, nx = sides_of(n)
    rows, columns = grad.shape[0] // nx, grad.shape[1]
    order = block_order(n, tn)
    x = lax.axis_index("dp") % nx
    total = None
    for turn in range(nx):
        pairs = []
        for z in range(nz):
            for y in range(ny):
                for x0 in range(nx):
                    for j in range(tn):
                        block = j * n + int(order[y, z, (x0 + turn) % nx])
                        pairs.append((((z * ny + y) * nx + x0) * tn + j, block))
        part = lax.dynamic_slice(grad, ((x + turn) % nx * rows, 0), (rows, columns))
        part = lax.ppermute(part, ("dp", "tensor"), pairs)
        total = part if total is None else total + part
    return total


def held(values, after):
    def kernel(*refs):
        pass

    return pl.pallas_call(
        kernel,
        in_specs=[pl.BlockSpec(memory_space=pl.ANY)] * (len(values) + 1),
        out_specs=[pl.BlockSpec(memory_space=pl.ANY)] * len(values),
        out_shape=[jax.ShapeDtypeStruct(value.shape, value.dtype) for value in values],
        input_output_aliases={k: k for k in range(len(values))},
        cost_estimate=pl.CostEstimate(flops=0, bytes_accessed=0, transcendentals=0),
        name="held",
    )(*values, after)


OFFSETS = 4
LENGTHS = OFFSETS + STEPS


def segment_start(places, info_ref):
    end = jnp.int32(0)
    start = jnp.zeros_like(places)
    for s in range(LENGTHS, info_ref.shape[0]):
        end = end + info_ref[s]
        start = jnp.where(places >= end, end, start)
    return start


def column(row):
    n = row.shape[-1]
    eye = lax.broadcasted_iota(jnp.int32, (n, n), 0) == lax.broadcasted_iota(jnp.int32, (n, n), 1)
    return jnp.sum(jnp.where(eye, row, 0.0), axis=1, keepdims=True)


def lane_sums(values):
    return lax.dot_general(
        jnp.ones((8, values.shape[1]), F32), values, (((1,), (1,)), ((), ())),
        precision=lax.Precision.HIGHEST, preferred_element_type=F32)


def folded_square_sum(values):
    total = None
    for c in range(0, values.shape[1], 128):
        piece = values[:, c:c + 128]
        total = piece * piece if total is None else total + piece * piece
    return total


def features_kernel(tn, info_ref, low_ref, mid_ref, gain_ref, *outs):
    j = info_ref[0]
    width = low_ref.shape[1]
    piece = width // tn
    step = 1024

    def rms_scale(ref):
        total = None
        for c in range(0, width, step):
            part = folded_square_sum(ref[:, c:c + step].astype(F32))
            total = part if total is None else total + part
        return lax.rsqrt(jnp.sum(total, axis=1, keepdims=True) / width + EPSILON)

    low_scale = rms_scale(low_ref)
    mid_scale = rms_scale(mid_ref)
    for s, out in enumerate(outs):
        first = pl.multiple_of((j ^ s) * piece, piece)
        for c in range(0, piece, 512):
            at = pl.ds(first + c, 512)
            value = (low_ref[:, at].astype(F32) * low_scale * gain_ref[0:1, at]
                     + mid_ref[:, at].astype(F32) * mid_scale * gain_ref[1:2, at])
            out[:, c:c + 512] = value.astype(BF16)


def features(info, low, mid, gain, tn):
    rows, width = low.shape
    block = 32
    piece = width // tn
    return pl.pallas_call(
        functools.partial(features_kernel, tn),
        grid=(rows // block,),
        in_specs=[
            SMEM,
            pl.BlockSpec((block, width), lambda b: (b, 0)),
            pl.BlockSpec((block, width), lambda b: (b, 0)),
            pl.BlockSpec(gain.shape, lambda b: (0, 0)),
        ],
        out_specs=[pl.BlockSpec((block, piece), lambda b: (b, 0))] * tn,
        out_shape=[jax.ShapeDtypeStruct((rows, piece), BF16)] * tn,
        compiler_params=pltpu.CompilerParams(vmem_limit_bytes=LARGE_LIMIT),
        cost_estimate=pl.CostEstimate(flops=10 * rows * width, bytes_accessed=6 * rows * width, transcendentals=0),
        name="features",
    )(info, low, mid, gain)


def attend_kernel(window, info_ref, query_ref, key_ref, value_ref, high_ref, square_ref):
    block = query_ref.shape[0]
    pack = key_ref.shape[0]
    b = pl.program_id(0)
    first = pl.multiple_of(jnp.clip(b * block - (window - block), 0, pack - window), block)
    query_places = b * block + lax.broadcasted_iota(jnp.int32, (block, window), 0)
    key_places = first + lax.broadcasted_iota(jnp.int32, (block, window), 1)
    allowed = (key_places <= query_places) & (key_places >= segment_start(query_places, info_ref))
    bias = jnp.where(allowed, 0.0, -1e30).astype(F32)
    group = (query_ref.shape[1] // HD) // (key_ref.shape[1] // HD)
    squares = jnp.zeros((block, HD), F32)
    ones = jnp.ones((window, HD), BF16)
    scale = math.log2(math.e) / math.sqrt(HD)
    for g in range(key_ref.shape[1] // HD):
        key = key_ref[pl.ds(first, window), g * HD:(g + 1) * HD]
        value = jnp.concatenate([value_ref[pl.ds(first, window), g * HD:(g + 1) * HD], ones], axis=1)
        for r in range(group):
            at = slice((g * group + r) * HD, (g * group + r + 1) * HD)
            scores = lax.dot_general(query_ref[:, at], key, (((1,), (1,)), ((), ())), preferred_element_type=F32)
            scores = scores * scale + bias
            highest = jnp.max(scores, axis=1, keepdims=True)
            expo = jnp.exp2(scores - highest).astype(BF16)
            mixed = jnp.dot(expo, value, preferred_element_type=F32)
            out = (mixed[:, :HD] / mixed[:, HD:]).astype(BF16)
            high_ref[:, at] = out
            out = out.astype(F32)
            squares = squares + out * out
    square_ref[...] = lane_sums(squares)


def attend(info, queries, keys, values):
    pack, width = queries.shape
    block = 128
    window = min(pack, 256 + block)
    return pl.pallas_call(
        functools.partial(attend_kernel, window),
        grid=(pack // block,),
        in_specs=[
            SMEM,
            pl.BlockSpec((block, width), lambda b: (b, 0)),
            pl.BlockSpec(keys.shape, lambda b: (0, 0)),
            pl.BlockSpec(values.shape, lambda b: (0, 0)),
        ],
        out_specs=[
            pl.BlockSpec((block, width), lambda b: (b, 0)),
            pl.BlockSpec((8, block), lambda b: (0, b)),
        ],
        out_shape=[
            jax.ShapeDtypeStruct((pack, width), BF16),
            jax.ShapeDtypeStruct((8, pack), F32),
        ],
        compiler_params=pltpu.CompilerParams(vmem_limit_bytes=VMEM_LIMIT),
        cost_estimate=pl.CostEstimate(
            flops=4 * pack * window * width, bytes_accessed=4 * pack * width,
            transcendentals=pack * window * width // HD),
        name="attend",
    )(info, queries, keys, values)


def chosen(info_ref, step, rows, lead):
    target = info_ref[0] * rows + lax.broadcasted_iota(jnp.int32, (rows, rows + lead), 0)
    source = info_ref[0] * rows - lead + lax.broadcasted_iota(jnp.int32, (rows, rows + lead), 1)
    hit = (source == target - info_ref[OFFSETS + step]) & (source >= segment_start(target, info_ref))
    return jnp.where(hit, 1.0, 0.0).astype(BF16)


def fold_kernel(info_ref, cotangent_ref, out_ref, near_ref, sems):
    steps, rows, width = cotangent_ref.shape
    coming = [pltpu.make_async_copy(cotangent_ref.at[s], near_ref.at[s], sems.at[s]) for s in range(steps)]
    for copy in coming:
        copy.start()
    total = None
    for s in range(steps):
        pick = chosen(info_ref, s, rows, OFFMAX)
        coming[s].wait()
        part = lax.dot_general(pick, near_ref[s], (((0,), (0,)), ((), ())), preferred_element_type=F32)
        total = part if total is None else total + part
    out_ref[...] = total.astype(BF16)


def fold(info, cotangent):
    steps, rows, width = cotangent.shape
    return pl.pallas_call(
        fold_kernel,
        in_specs=[SMEM, HBM],
        out_specs=VMEM,
        out_shape=jax.ShapeDtypeStruct((rows + OFFMAX, width), BF16),
        scratch_shapes=[pltpu.VMEM(cotangent.shape, BF16), pltpu.SemaphoreType.DMA((steps,))],
        compiler_params=pltpu.CompilerParams(vmem_limit_bytes=LARGE_LIMIT),
        cost_estimate=pl.CostEstimate(flops=2 * steps * rows * 160 * width, bytes_accessed=2 * steps * rows * width, transcendentals=0),
        name="fold",
    )(info, cotangent)


def merge_kernel(width, tn, info_ref, gain_ref, high_ref, *refs):
    parts, square_refs, (far_ref, out_square_ref, out_ref, sems) = refs[:tn], refs[tn:-4], refs[-4:]
    copies = []
    j = info_ref[0]
    rows = parts[0].shape[0]
    piece = high_ref.shape[1]
    squares = square_refs[0][...]
    for ref in square_refs[1:]:
        squares = squares + ref[...]
    scales = lax.rsqrt(squares / width + EPSILON)
    for b in range(tn):
        out_square_ref[:, b * rows:(b + 1) * rows] = scales[:, b * rows:(b + 1) * rows]
    for s in range(tn):
        first = pl.multiple_of((j ^ s) * rows, rows)
        at = pl.ds(first, rows)
        scale = column(out_square_ref[0:1, at])
        total = jnp.zeros((rows, 128), F32)
        for c in range(0, piece, 128):
            cols = slice(c, c + 128)
            gain = gain_ref[2:3, pl.ds(pl.multiple_of(j * piece + c, 128), 128)]
            merged = (parts[s][:, cols].astype(F32) + high_ref[at, cols].astype(F32) * scale * gain).astype(BF16)
            out_ref[at, cols] = merged
            merged = merged.astype(F32)
            total = total + merged * merged
        copy = pltpu.make_async_copy(out_ref.at[at, :], far_ref.at[at, :], sems.at[s])
        copy.start()
        copies.append(copy)
        out_square_ref[:, at] = lane_sums(total)
    for copy in copies:
        copy.wait()


def merge(info, gain, high, parts, squares, width):
    pack, piece = high.shape
    tn = len(parts)
    return pl.pallas_call(
        functools.partial(merge_kernel, width, tn),
        in_specs=[SMEM] + [VMEM] * (2 + tn + len(squares)),
        out_specs=[HBM, VMEM],
        out_shape=[
            jax.ShapeDtypeStruct((pack, piece), BF16),
            jax.ShapeDtypeStruct((8, pack), F32),
        ],
        scratch_shapes=[pltpu.VMEM((pack, piece), BF16), pltpu.SemaphoreType.DMA((tn,))],
        compiler_params=pltpu.CompilerParams(vmem_limit_bytes=VMEM_LIMIT),
        cost_estimate=pl.CostEstimate(flops=8 * pack * piece, bytes_accessed=6 * pack * piece, transcendentals=0),
        name="merge",
    )(info, gain, high, *parts, *squares)


def grads(info, gain, merged, folds, squares, width, ny, tn):
    pack, piece = merged.shape
    rows = pack // tn
    vw = folds[0].shape[1]
    chunk = piece // (2 * ny)
    kept, sent = (KEPT, SENT) if ny > 1 else (((0,), (0,)), ((), ()))
    steps = [(h, s, True) for h in range(2) for s in kept[h]] + [(h, s, False) for h in range(2) for s in sent[h]]
    steps.sort(key=lambda step: step[2])
    size = chunk // (2 * tn) if ny > 1 else chunk

    def kernel(info_ref, gain_ref, merged_ref, *refs):
        fold_refs, square_refs, refs = refs[:tn], refs[tn:2 * tn], refs[2 * tn:]
        keep_refs, refs = refs[:2], refs[2:]
        send_refs, refs = refs[:2 if ny > 1 else 0], refs[2 if ny > 1 else 0:]
        hidden_ref, fold_ref, near_ref, near_folds, near_cut, sems = refs
        coming = [
            pltpu.make_async_copy(
                merged_ref.at[b * rows:(b + 1) * rows, :], near_ref.at[b * rows:(b + 1) * rows, :], sems.at[b])
            for b in range(tn)]
        folds_coming = [
            pltpu.make_async_copy(fold_refs[s], near_folds.at[s], sems.at[tn + s]) for s in range(tn)]
        for copy in coming + folds_coming:
            copy.start()
        j, y = info_ref[0], info_ref[1]
        squares = square_refs[0][...]
        for s in range(1, tn):
            squares = squares + square_refs[s][...]
        scales = lax.rsqrt(squares / width + EPSILON)
        for b in range(tn):
            at = slice(b * rows, (b + 1) * rows)
            scale = column(scales[0:1, at])
            coming[b].wait()
            for c in range(0, piece, 128):
                cols = slice(c, c + 128)
                gain = gain_ref[:, pl.ds(pl.multiple_of(j * piece + c, 128), 128)]
                hidden_ref[at, cols] = (near_ref[at, cols].astype(F32) * scale * gain).astype(BF16)
        fold_ref[...] = jnp.zeros_like(fold_ref)
        for s in range(tn):
            at = pl.ds(pl.multiple_of((j ^ s) * rows, rows), rows + OFFMAX)
            folds_coming[s].wait()
            fold_ref[at, :] = fold_ref[at, :] + near_folds[s].astype(F32)
        folded = fold_ref[OFFMAX:, :].astype(BF16)
        going = []
        for h, s, keep in steps:
            at = pl.ds(pl.multiple_of(h * ny * chunk + (y ^ s) * chunk, chunk), chunk)
            part = lax.dot_general(
                hidden_ref[:, at], folded, (((0,), (0,)), ((), ())), preferred_element_type=F32)
            if size < chunk:
                part = jnp.concatenate(
                    [part[(x * tn + t) * size:(x * tn + t + 1) * size] for t in range(tn) for x in range(2)], axis=0)
            if keep:
                keep_refs[h][kept[h].index(s)] = part
            else:
                k = sent[h].index(s)
                near_cut[h, k] = part.astype(BF16)
                copy = pltpu.make_async_copy(near_cut.at[h, k], send_refs[h].at[k], sems.at[2 * tn + 2 * h + k])
                copy.start()
                going.append(copy)
        for copy in going:
            copy.wait()

    out_shape = [jax.ShapeDtypeStruct((len(kept[h]), chunk, vw), F32) for h in range(2)]
    if ny > 1:
        out_shape += [jax.ShapeDtypeStruct((len(sent[h]), chunk, vw), BF16) for h in range(2)]
    out_shape += [jax.ShapeDtypeStruct((pack, piece), BF16)]
    out = pl.pallas_call(
        kernel,
        in_specs=[SMEM, VMEM, HBM] + [HBM] * tn + [VMEM] * tn,
        out_specs=[VMEM] * 2 + ([HBM] * 2 if ny > 1 else []) + [VMEM],
        out_shape=out_shape,
        scratch_shapes=[
            pltpu.VMEM((pack + OFFMAX, vw), F32),
            pltpu.VMEM((pack, piece), BF16),
            pltpu.VMEM((tn, rows + OFFMAX, vw), BF16),
            pltpu.VMEM((2, 2, chunk if ny > 1 else 16, vw), BF16),
            pltpu.SemaphoreType.DMA((2 * tn + 4,)),
        ],
        compiler_params=pltpu.CompilerParams(vmem_limit_bytes=VMEM_LIMIT),
        cost_estimate=pl.CostEstimate(flops=2 * pack * piece * vw, bytes_accessed=8 * pack * piece, transcendentals=0),
        name="grads",
    )(info, gain, merged, *folds, *squares)
    return out[:2], out[2:-1] if ny > 1 else (None, None), out[-1]


def project(info, hidden, weights, tn, nz, ny, nx):
    pack, piece = hidden.shape
    rows = pack // tn
    vw = weights[0][0].shape[1]
    parts = [
        (part, far, near)
        for half, near, (first, second) in zip(weights, (0, 1), EXCHANGES)
        for part, far in zip(half, (0, first, second, first ^ second))]
    distances = (0, 4, 2, 6) if nz > 1 else (0,)
    size = parts[0][0].shape[0] // (len(distances) * nx)

    def kernel(info_ref, hidden_ref, *refs):
        weight_refs, value_refs = refs[:len(parts)], refs[len(parts):-4]
        weight_ref, total_ref, near_ref, sems = refs[-4:]
        coming = [pltpu.make_async_copy(ref, near_ref.at[p], sems.at[p]) for p, ref in enumerate(weight_refs)]
        for copy in coming:
            copy.start()
        j, y, z, x = info_ref[0], info_ref[1], info_ref[2], info_ref[3]
        for p, (_, far, near) in enumerate(parts):
            coming[p].wait()
            for k, distance in enumerate(distances):
                for m in range(nx):
                    y_at, z_at, x_at = y ^ far, z ^ distance ^ near, x ^ m
                    if nz == 2 * tn:
                        block = (((z_at // tn) * ny + y_at) * nx + x_at) * tn + z_at % tn
                    else:
                        block = (y_at * nz + z_at) * nx + x_at
                    at = pl.ds(pl.multiple_of(block * size, size), size)
                    weight_ref[at, :] = near_ref[p, (k * nx + m) * size:(k * nx + m + 1) * size, :]
        total_ref[0:OFFMAX, :] = jnp.zeros((OFFMAX, vw), F32)
        for c in range(0, pack, 256):
            total_ref[OFFMAX + c:OFFMAX + c + 256, :] = jnp.dot(
                hidden_ref[c:c + 256, :], weight_ref[...], preferred_element_type=F32)
        for s in range(tn):
            at = pl.ds(pl.multiple_of((j ^ s) * rows, rows), rows + OFFMAX)
            value_refs[s][...] = total_ref[at, :].astype(value_refs[s].dtype)

    return pl.pallas_call(
        kernel,
        in_specs=[SMEM, VMEM] + [pl.BlockSpec(memory_space=pl.ANY)] * len(parts),
        out_specs=[VMEM] * tn,
        out_shape=[jax.ShapeDtypeStruct((rows + OFFMAX, vw), F32 if s == 0 else BF16) for s in range(tn)],
        scratch_shapes=[
            pltpu.VMEM((piece, vw), BF16),
            pltpu.VMEM((pack + OFFMAX, vw), F32),
            pltpu.VMEM((len(parts),) + parts[0][0].shape, BF16),
            pltpu.SemaphoreType.DMA((len(parts),)),
        ],
        compiler_params=pltpu.CompilerParams(vmem_limit_bytes=VMEM_LIMIT),
        cost_estimate=pl.CostEstimate(flops=2 * pack * piece * vw, bytes_accessed=4 * pack * piece, transcendentals=0),
        name="project",
    )(info, hidden, *[part for part, _, _ in parts])


def spread(info, parts):
    rows, vw = parts[0].shape[0] - OFFMAX, parts[0].shape[1]

    def kernel(info_ref, *refs):
        parts_refs, out_ref = refs[:-1], refs[-1]
        total = None
        for ref in parts_refs:
            part = ref[...].astype(F32)
            total = part if total is None else total + part
        total = total.astype(BF16)
        for s in range(STEPS):
            pick = chosen(info_ref, s, rows, OFFMAX)
            out_ref[s] = jnp.dot(pick, total, preferred_element_type=F32).astype(BF16)

    return pl.pallas_call(
        kernel,
        in_specs=[SMEM] + [VMEM] * len(parts),
        out_specs=VMEM,
        out_shape=jax.ShapeDtypeStruct((STEPS, rows, vw), BF16),
        compiler_params=pltpu.CompilerParams(vmem_limit_bytes=VMEM_LIMIT),
        cost_estimate=pl.CostEstimate(flops=2 * STEPS * rows * 160 * vw, bytes_accessed=8 * STEPS * rows * vw, transcendentals=0),
        name="spread",
    )(info, *parts)


def body(
    target_queries,
    target_keys,
    target_values,
    low_feature,
    mid_feature,
    merging_gain,
    draft_gain,
    draft_weight,
    cotangent,
    doc_lengths,
    step_offsets,
):
    n = lax.axis_size("dp")
    tn = lax.axis_size("tensor")
    j = lax.axis_index("tensor")
    i = lax.axis_index("dp")
    flat = i * tn + j
    nz, ny, nx = sides_of(n)
    lengths = doc_lengths.reshape(-1)
    count = LENGTHS + lengths.size
    info = jnp.pad(step_offsets, (OFFSETS, lengths.size)) + jnp.pad(lengths, (LENGTHS, 0))
    for at, value in enumerate((j, i // nx % ny, i // (ny * nx), i % nx)):
        info = jnp.where(lax.iota(jnp.int32, count) == at, value.astype(jnp.int32), info)
    width = low_feature.shape[1]
    piece = width // tn
    pack = target_queries.shape[0]
    both = ("dp", "tensor")

    def swapped(values, s):
        return lax.ppermute(values, "tensor", [(a, a ^ s) for a in range(tn)])

    folded = fold(info, cotangent)
    across = swapped(folded, 2)
    low_feature, folded = lax.optimization_barrier((low_feature, folded))
    sent = features(info, low_feature, mid_feature, merging_gain, tn)
    across, sent = lax.optimization_barrier((across, sent))
    parts = [sent[0]] + [swapped(sent[s], s) for s in range(1, tn)]

    high, squares = attend(info, target_queries, target_keys, target_values)
    own_weight, high, folded, across = lax.optimization_barrier((draft_weight, high, folded, across))
    squares = squares + swapped(squares, 1)
    folds = [folded, swapped(folded, 1), across, swapped(across, 1)]
    squares, folds, parts[1] = lax.optimization_barrier((squares, folds, parts[1]))
    squares = [squares, swapped(squares, 2)]
    weights = weight_to_place(own_weight)
    merged, squares = merge(info, merging_gain, high, parts, squares, width)
    weights, merged, squares = lax.optimization_barrier((weights, merged, squares))
    weights = jnp.concatenate(weights)
    far_weights = moved(weights, lambda z, y, x: (z ^ nz // 2, y, x)) if nz > 1 else weights
    squares = [squares] + [swapped(squares, s) for s in range(1, tn)]
    kept, cut, hidden = grads(info, draft_gain.reshape(1, width), merged, folds, squares, width, ny, tn)
    far_weights, cut = lax.optimization_barrier((far_weights, cut))
    weights, hidden = lax.optimization_barrier((weights, hidden))
    if nz > 1:
        weights = jnp.concatenate([weights, far_weights])
    weights = weight_halves(weight_across(weights, nz // 4))
    halves = reduce_once(kept, cut)
    weights, own = lax.optimization_barrier((weights, [half[0] for half in halves]))
    got = reduce_twice(halves)
    grad = [mine + part.astype(F32) for mine, part in zip(own, got)]
    if ny > 1:
        grad = [half.astype(BF16) for half in grad]
    grad = jnp.concatenate(grad)
    weights = weight_twice(weight_once(held(weights, grad)))
    grad = reduce_along_z(grad)
    hidden, grad = lax.optimization_barrier((hidden, grad))
    weight_grad = reduce_to_owner(grad)
    values = project(info, hidden, weights, tn, nz, ny, nx)
    values = [values[0]] + [swapped(values[s], s) for s in range(1, tn)]
    draft_values = spread(info, values)

    rows = weight_grad.shape[0]
    gain = lax.dynamic_slice(draft_gain, (flat * rows,), (rows,))
    gain_grad = jnp.sum(weight_grad * draft_weight.astype(F32), axis=1) / gain
    return (draft_values, weight_grad, gain_grad)


def solution(mesh):
    placed = (
        P("dp", "tensor"),
        P("dp", "tensor"),
        P("dp", "tensor"),
        P(("dp", "tensor"), None),
        P(("dp", "tensor"), None),
        P(),
        P(),
        P(("dp", "tensor"), None),
        P(None, ("dp", "tensor"), None),
        P("dp", None),
        P(),
    )
    return jax.shard_map(
        body,
        mesh=mesh,
        in_specs=placed,
        out_specs=(P(None, ("dp", "tensor"), None), P(("dp", "tensor"), None), P(("dp", "tensor"))),
        check_vma=False,
    )
```

```python
import functools
import math

import jax
import jax.numpy as jnp
import numpy as np
from jax import lax
from jax.experimental import pallas as pl
from jax.experimental.pallas import tpu as pltpu
from jax.sharding import PartitionSpec as P

HD = 128
STEPS = 3
OFFMAX = 32
EPSILON = 1e-05
VMEM_LIMIT = 20 * 1024 * 1024
LARGE_LIMIT = 60 * 1024 * 1024

VMEM = pl.BlockSpec(memory_space=pltpu.VMEM)
SMEM = pl.BlockSpec(memory_space=pltpu.SMEM)
HBM = pl.BlockSpec(memory_space=pltpu.HBM)
F32 = jnp.float32
BF16 = jnp.bfloat16


SIDES = {64: (8, 4, 2)}


def sides_of(n):
    return SIDES.get(n, (1, 1, n))


def groups_along(n, *sides):
    sizes = sides_of(n)
    where = np.moveaxis(np.arange(n).reshape(sizes), sides, range(-len(sides), 0))
    return where.reshape(-1, math.prod(sizes[side] for side in sides)).tolist()


def block_order(n, tn):
    nz, ny, nx = sides_of(n)
    order = np.arange(n).reshape(ny, nz, nx)
    if nz == 2 * tn and n == ny * nx * tn * 2:
        for y in range(ny):
            for z in range(nz):
                for x in range(nx):
                    order[y, z, x] = (((z // tn) * ny + y) * nx + x) * tn + z % tn
    return order


def moved(values, change):
    n = lax.axis_size("dp")
    nz, ny, nx = sides_of(n)
    pairs = []
    for source in range(n):
        z, y, x = change(source // (ny * nx), source // nx % ny, source % nx)
        pairs.append((source, (z * ny + y) * nx + x))
    return lax.ppermute(values, "dp", pairs)


def weight_to_place(weight):
    n, tn = lax.axis_size("dp"), lax.axis_size("tensor")
    nz, ny, nx = sides_of(n)
    order = block_order(n, tn)
    parts = []
    for turn in range(nx):
        pairs = []
        for j in range(tn):
            for y, z, x in np.ndindex(ny, nz, nx):
                pairs.append((j * n + int(order[y, z, x ^ turn]), ((z * ny + y) * nx + x) * tn + j))
        parts.append(lax.ppermute(weight, ("dp", "tensor"), pairs))
    return parts


def weight_across(weight, far):
    if sides_of(lax.axis_size("dp"))[0] == 1:
        return weight
    return jnp.concatenate([weight, moved(weight, lambda z, y, x: (z ^ far, y, x))])


def weight_halves(weight):
    if sides_of(lax.axis_size("dp"))[0] == 1:
        return [weight]
    return [weight, moved(weight, lambda z, y, x: (z ^ 1, y, x))]


def weight_once(halves):
    if sides_of(lax.axis_size("dp"))[1] == 1:
        return [[half] for half in halves]
    return [[half, moved(half, lambda z, y, x: (z, y ^ first, x))] for half, (first, _) in zip(halves, EXCHANGES)]


def weight_twice(halves):
    if sides_of(lax.axis_size("dp"))[1] == 1:
        return halves
    return [
        half + [moved(part, lambda z, y, x: (z, y ^ second, x)) for part in half]
        for half, (_, second) in zip(halves, EXCHANGES)]


KEPT = ((0, 3), (0, 1))
SENT = ((1, 2), (3, 2))
EXCHANGES = ((1, 3), (3, 1))


def reduce_once(kept, sent):
    if sides_of(lax.axis_size("dp"))[1] == 1:
        return [(keep[0], None) for keep in kept]
    got = [moved(send, lambda z, y, x: (z, y ^ first, x)) for send, (first, _) in zip(sent, EXCHANGES)]
    got = lax.optimization_barrier(got)
    return [(keep[0] + part[0].astype(F32), (keep[1] + part[1].astype(F32)).astype(BF16)) for keep, part in zip(kept, got)]


def reduce_twice(halves):
    if sides_of(lax.axis_size("dp"))[1] == 1:
        return [jnp.zeros_like(own) for own, _ in halves]
    return [moved(other, lambda z, y, x: (z, y ^ second, x)) for (_, other), (_, second) in zip(halves, EXCHANGES)]


def reduce_along_z(grad):
    n = lax.axis_size("dp")
    nz = sides_of(n)[0]
    if nz == 1:
        return grad
    columns = grad.shape[-1]
    grad = lax.all_to_all(grad.astype(BF16), "dp", 0, 0, tiled=True, axis_index_groups=groups_along(n, 0))
    return jnp.sum(grad.reshape(nz, -1, columns).astype(F32), axis=0)


def parts_by_turn(grad):
    nx = sides_of(lax.axis_size("dp"))[2]
    rows, columns = grad.shape[0] // nx, grad.shape[1]
    x = lax.axis_index("dp") % nx
    return [lax.dynamic_slice(grad, ((x + turn) % nx * rows, 0), (rows, columns)) for turn in range(nx)]


def reduce_to_owner(parts):
    n, tn = lax.axis_size("dp"), lax.axis_size("tensor")
    nz, ny, nx = sides_of(n)
    order = block_order(n, tn)
    total = None
    for turn, part in enumerate(parts):
        pairs = []
        for z in range(nz):
            for y in range(ny):
                for x0 in range(nx):
                    for j in range(tn):
                        block = j * n + int(order[y, z, (x0 + turn) % nx])
                        pairs.append((((z * ny + y) * nx + x0) * tn + j, block))
        part = lax.ppermute(part, ("dp", "tensor"), pairs)
        total = part if total is None else total + part
    return total


def held(values, after):
    def kernel(*refs):
        pass

    return pl.pallas_call(
        kernel,
        in_specs=[pl.BlockSpec(memory_space=pl.ANY)] * (len(values) + 1),
        out_specs=[pl.BlockSpec(memory_space=pl.ANY)] * len(values),
        out_shape=[jax.ShapeDtypeStruct(value.shape, value.dtype) for value in values],
        input_output_aliases={k: k for k in range(len(values))},
        cost_estimate=pl.CostEstimate(flops=0, bytes_accessed=0, transcendentals=0),
        name="held",
    )(*values, after)


OFFSETS = 4
LENGTHS = OFFSETS + STEPS


def segment_start(places, info_ref):
    end = jnp.int32(0)
    start = jnp.zeros_like(places)
    for s in range(LENGTHS, info_ref.shape[0]):
        end = end + info_ref[s]
        start = jnp.where(places >= end, end, start)
    return start


def column(row):
    n = row.shape[-1]
    eye = lax.broadcasted_iota(jnp.int32, (n, n), 0) == lax.broadcasted_iota(jnp.int32, (n, n), 1)
    return jnp.sum(jnp.where(eye, row, 0.0), axis=1, keepdims=True)


def lane_sums(values):
    return lax.dot_general(
        jnp.ones((8, values.shape[1]), F32), values, (((1,), (1,)), ((), ())),
        precision=lax.Precision.HIGHEST, preferred_element_type=F32)


def folded_square_sum(values):
    total = None
    for c in range(0, values.shape[1], 128):
        piece = values[:, c:c + 128]
        total = piece * piece if total is None else total + piece * piece
    return total


def features_kernel(tn, info_ref, low_ref, mid_ref, gain_ref, *outs):
    j = info_ref[0]
    width = low_ref.shape[1]
    piece = width // tn
    step = 1024

    def rms_scale(ref):
        total = None
        for c in range(0, width, step):
            part = folded_square_sum(ref[:, c:c + step].astype(F32))
            total = part if total is None else total + part
        return lax.rsqrt(jnp.sum(total, axis=1, keepdims=True) / width + EPSILON)

    low_scale = rms_scale(low_ref)
    mid_scale = rms_scale(mid_ref)
    for s, out in enumerate(outs):
        first = pl.multiple_of((j ^ s) * piece, piece)
        for c in range(0, piece, 512):
            at = pl.ds(first + c, 512)
            value = (low_ref[:, at].astype(F32) * low_scale * gain_ref[0:1, at]
                     + mid_ref[:, at].astype(F32) * mid_scale * gain_ref[1:2, at])
            out[:, c:c + 512] = value.astype(BF16)


def features(info, low, mid, gain, tn):
    rows, width = low.shape
    block = 32
    piece = width // tn
    return pl.pallas_call(
        functools.partial(features_kernel, tn),
        grid=(rows // block,),
        in_specs=[
            SMEM,
            pl.BlockSpec((block, width), lambda b: (b, 0)),
            pl.BlockSpec((block, width), lambda b: (b, 0)),
            pl.BlockSpec(gain.shape, lambda b: (0, 0)),
        ],
        out_specs=[pl.BlockSpec((block, piece), lambda b: (b, 0))] * tn,
        out_shape=[jax.ShapeDtypeStruct((rows, piece), BF16)] * tn,
        compiler_params=pltpu.CompilerParams(vmem_limit_bytes=LARGE_LIMIT),
        cost_estimate=pl.CostEstimate(flops=10 * rows * width, bytes_accessed=6 * rows * width, transcendentals=0),
        name="features",
    )(info, low, mid, gain)


def attend_kernel(window, info_ref, query_ref, key_ref, value_ref, high_ref, square_ref):
    block = query_ref.shape[0]
    pack = key_ref.shape[0]
    b = pl.program_id(0)
    first = pl.multiple_of(jnp.clip(b * block - (window - block), 0, pack - window), block)
    query_places = b * block + lax.broadcasted_iota(jnp.int32, (block, window), 0)
    key_places = first + lax.broadcasted_iota(jnp.int32, (block, window), 1)
    allowed = (key_places <= query_places) & (key_places >= segment_start(query_places, info_ref))
    bias = jnp.where(allowed, 0.0, -1e30).astype(F32)
    group = (query_ref.shape[1] // HD) // (key_ref.shape[1] // HD)
    squares = jnp.zeros((block, HD), F32)
    ones = jnp.ones((window, HD), BF16)
    scale = math.log2(math.e) / math.sqrt(HD)
    for g in range(key_ref.shape[1] // HD):
        key = key_ref[pl.ds(first, window), g * HD:(g + 1) * HD]
        value = jnp.concatenate([value_ref[pl.ds(first, window), g * HD:(g + 1) * HD], ones], axis=1)
        for r in range(group):
            at = slice((g * group + r) * HD, (g * group + r + 1) * HD)
            scores = lax.dot_general(query_ref[:, at], key, (((1,), (1,)), ((), ())), preferred_element_type=F32)
            scores = scores * scale + bias
            highest = jnp.max(scores, axis=1, keepdims=True)
            expo = jnp.exp2(scores - highest).astype(BF16)
            mixed = jnp.dot(expo, value, preferred_element_type=F32)
            out = (mixed[:, :HD] / mixed[:, HD:]).astype(BF16)
            high_ref[:, at] = out
            out = out.astype(F32)
            squares = squares + out * out
    square_ref[...] = lane_sums(squares)


def attend(info, queries, keys, values):
    pack, width = queries.shape
    block = 128
    window = min(pack, 256 + block)
    return pl.pallas_call(
        functools.partial(attend_kernel, window),
        grid=(pack // block,),
        in_specs=[
            SMEM,
            pl.BlockSpec((block, width), lambda b: (b, 0)),
            pl.BlockSpec(keys.shape, lambda b: (0, 0)),
            pl.BlockSpec(values.shape, lambda b: (0, 0)),
        ],
        out_specs=[
            pl.BlockSpec((block, width), lambda b: (b, 0)),
            pl.BlockSpec((8, block), lambda b: (0, b)),
        ],
        out_shape=[
            jax.ShapeDtypeStruct((pack, width), BF16),
            jax.ShapeDtypeStruct((8, pack), F32),
        ],
        compiler_params=pltpu.CompilerParams(vmem_limit_bytes=VMEM_LIMIT),
        cost_estimate=pl.CostEstimate(
            flops=4 * pack * window * width, bytes_accessed=4 * pack * width,
            transcendentals=pack * window * width // HD),
        name="attend",
    )(info, queries, keys, values)


def chosen(info_ref, step, rows, lead):
    target = info_ref[0] * rows + lax.broadcasted_iota(jnp.int32, (rows, rows + lead), 0)
    source = info_ref[0] * rows - lead + lax.broadcasted_iota(jnp.int32, (rows, rows + lead), 1)
    hit = (source == target - info_ref[OFFSETS + step]) & (source >= segment_start(target, info_ref))
    return jnp.where(hit, 1.0, 0.0).astype(BF16)


def fold_kernel(info_ref, cotangent_ref, out_ref, near_ref, sems):
    steps, rows, width = cotangent_ref.shape
    coming = [pltpu.make_async_copy(cotangent_ref.at[s], near_ref.at[s], sems.at[s]) for s in range(steps)]
    for copy in coming:
        copy.start()
    total = None
    for s in range(steps):
        pick = chosen(info_ref, s, rows, OFFMAX)
        coming[s].wait()
        part = lax.dot_general(pick, near_ref[s], (((0,), (0,)), ((), ())), preferred_element_type=F32)
        total = part if total is None else total + part
    out_ref[...] = total.astype(BF16)


def fold(info, cotangent):
    steps, rows, width = cotangent.shape
    return pl.pallas_call(
        fold_kernel,
        in_specs=[SMEM, HBM],
        out_specs=VMEM,
        out_shape=jax.ShapeDtypeStruct((rows + OFFMAX, width), BF16),
        scratch_shapes=[pltpu.VMEM(cotangent.shape, BF16), pltpu.SemaphoreType.DMA((steps,))],
        compiler_params=pltpu.CompilerParams(vmem_limit_bytes=LARGE_LIMIT),
        cost_estimate=pl.CostEstimate(flops=2 * steps * rows * 160 * width, bytes_accessed=2 * steps * rows * width, transcendentals=0),
        name="fold",
    )(info, cotangent)


def merge_kernel(width, tn, info_ref, gain_ref, high_ref, *refs):
    parts, square_refs, (far_ref, out_square_ref, out_ref, sems) = refs[:tn], refs[tn:-4], refs[-4:]
    copies = []
    j = info_ref[0]
    rows = parts[0].shape[0]
    piece = high_ref.shape[1]
    squares = square_refs[0][...]
    for ref in square_refs[1:]:
        squares = squares + ref[...]
    scales = lax.rsqrt(squares / width + EPSILON)
    for b in range(tn):
        out_square_ref[:, b * rows:(b + 1) * rows] = scales[:, b * rows:(b + 1) * rows]
    for s in range(tn):
        first = pl.multiple_of((j ^ s) * rows, rows)
        at = pl.ds(first, rows)
        scale = column(out_square_ref[0:1, at])
        total = jnp.zeros((rows, 128), F32)
        for c in range(0, piece, 128):
            cols = slice(c, c + 128)
            gain = gain_ref[2:3, pl.ds(pl.multiple_of(j * piece + c, 128), 128)]
            merged = (parts[s][:, cols].astype(F32) + high_ref[at, cols].astype(F32) * scale * gain).astype(BF16)
            out_ref[at, cols] = merged
            merged = merged.astype(F32)
            total = total + merged * merged
        copy = pltpu.make_async_copy(out_ref.at[at, :], far_ref.at[at, :], sems.at[s])
        copy.start()
        copies.append(copy)
        out_square_ref[:, at] = lane_sums(total)
    for copy in copies:
        copy.wait()


def merge(info, gain, high, parts, squares, width):
    pack, piece = high.shape
    tn = len(parts)
    return pl.pallas_call(
        functools.partial(merge_kernel, width, tn),
        in_specs=[SMEM] + [VMEM] * (2 + tn + len(squares)),
        out_specs=[HBM, VMEM],
        out_shape=[
            jax.ShapeDtypeStruct((pack, piece), BF16),
            jax.ShapeDtypeStruct((8, pack), F32),
        ],
        scratch_shapes=[pltpu.VMEM((pack, piece), BF16), pltpu.SemaphoreType.DMA((tn,))],
        compiler_params=pltpu.CompilerParams(vmem_limit_bytes=VMEM_LIMIT),
        cost_estimate=pl.CostEstimate(flops=8 * pack * piece, bytes_accessed=6 * pack * piece, transcendentals=0),
        name="merge",
    )(info, gain, high, *parts, *squares)


def grads(info, gain, merged, folds, squares, width, ny, tn):
    pack, piece = merged.shape
    rows = pack // tn
    vw = folds[0].shape[1]
    chunk = piece // (2 * ny)
    kept, sent = (KEPT, SENT) if ny > 1 else (((0,), (0,)), ((), ()))
    steps = [(h, s, True) for h in range(2) for s in kept[h]] + [(h, s, False) for h in range(2) for s in sent[h]]
    steps.sort(key=lambda step: step[2])
    size = chunk // (2 * tn) if ny > 1 else chunk

    def kernel(info_ref, gain_ref, merged_ref, *refs):
        fold_refs, square_refs, refs = refs[:tn], refs[tn:2 * tn], refs[2 * tn:]
        keep_refs, refs = refs[:2], refs[2:]
        send_refs, refs = refs[:2 if ny > 1 else 0], refs[2 if ny > 1 else 0:]
        hidden_ref, fold_ref, near_ref, near_folds, near_cut, sems = refs
        coming = [
            pltpu.make_async_copy(
                merged_ref.at[b * rows:(b + 1) * rows, :], near_ref.at[b * rows:(b + 1) * rows, :], sems.at[b])
            for b in range(tn)]
        folds_coming = [
            pltpu.make_async_copy(fold_refs[s], near_folds.at[s], sems.at[tn + s]) for s in range(tn)]
        for copy in coming + folds_coming:
            copy.start()
        j, y = info_ref[0], info_ref[1]
        squares = square_refs[0][...]
        for s in range(1, tn):
            squares = squares + square_refs[s][...]
        scales = lax.rsqrt(squares / width + EPSILON)
        for b in range(tn):
            at = slice(b * rows, (b + 1) * rows)
            scale = column(scales[0:1, at])
            coming[b].wait()
            for c in range(0, piece, 128):
                cols = slice(c, c + 128)
                gain = gain_ref[:, pl.ds(pl.multiple_of(j * piece + c, 128), 128)]
                hidden_ref[at, cols] = (near_ref[at, cols].astype(F32) * scale * gain).astype(BF16)
        fold_ref[...] = jnp.zeros_like(fold_ref)
        for s in range(tn):
            at = pl.ds(pl.multiple_of((j ^ s) * rows, rows), rows + OFFMAX)
            folds_coming[s].wait()
            fold_ref[at, :] = fold_ref[at, :] + near_folds[s].astype(F32)
        folded = fold_ref[OFFMAX:, :].astype(BF16)
        going = []
        for h, s, keep in steps:
            at = pl.ds(pl.multiple_of(h * ny * chunk + (y ^ s) * chunk, chunk), chunk)
            part = lax.dot_general(
                hidden_ref[:, at], folded, (((0,), (0,)), ((), ())), preferred_element_type=F32)
            if size < chunk:
                part = jnp.concatenate(
                    [part[(x * tn + t) * size:(x * tn + t + 1) * size] for t in range(tn) for x in range(2)], axis=0)
            if keep:
                keep_refs[h][kept[h].index(s)] = part
            else:
                k = sent[h].index(s)
                near_cut[h, k] = part.astype(BF16)
                copy = pltpu.make_async_copy(near_cut.at[h, k], send_refs[h].at[k], sems.at[2 * tn + 2 * h + k])
                copy.start()
                going.append(copy)
        for copy in going:
            copy.wait()

    out_shape = [jax.ShapeDtypeStruct((len(kept[h]), chunk, vw), F32) for h in range(2)]
    if ny > 1:
        out_shape += [jax.ShapeDtypeStruct((len(sent[h]), chunk, vw), BF16) for h in range(2)]
    out_shape += [jax.ShapeDtypeStruct((pack, piece), BF16)]
    out = pl.pallas_call(
        kernel,
        in_specs=[SMEM, VMEM, HBM] + [HBM] * tn + [VMEM] * tn,
        out_specs=[VMEM] * 2 + ([HBM] * 2 if ny > 1 else []) + [VMEM],
        out_shape=out_shape,
        scratch_shapes=[
            pltpu.VMEM((pack + OFFMAX, vw), F32),
            pltpu.VMEM((pack, piece), BF16),
            pltpu.VMEM((tn, rows + OFFMAX, vw), BF16),
            pltpu.VMEM((2, 2, chunk if ny > 1 else 16, vw), BF16),
            pltpu.SemaphoreType.DMA((2 * tn + 4,)),
        ],
        compiler_params=pltpu.CompilerParams(vmem_limit_bytes=VMEM_LIMIT),
        cost_estimate=pl.CostEstimate(flops=2 * pack * piece * vw, bytes_accessed=8 * pack * piece, transcendentals=0),
        name="grads",
    )(info, gain, merged, *folds, *squares)
    return out[:2], out[2:-1] if ny > 1 else (None, None), out[-1]


def project(info, hidden, weights, tn, nz, ny, nx):
    pack, piece = hidden.shape
    rows = pack // tn
    vw = weights[0][0].shape[1]
    parts = [
        (part, far, near)
        for half, near, (first, second) in zip(weights, (0, 1), EXCHANGES)
        for part, far in zip(half, (0, first, second, first ^ second))]
    distances = (0, 4, 2, 6) if nz > 1 else (0,)
    size = parts[0][0].shape[0] // (len(distances) * nx)

    def kernel(info_ref, hidden_ref, *refs):
        weight_refs, value_refs = refs[:len(parts)], refs[len(parts):-4]
        weight_ref, total_ref, near_ref, sems = refs[-4:]
        coming = [pltpu.make_async_copy(ref, near_ref.at[p], sems.at[p]) for p, ref in enumerate(weight_refs)]
        for copy in coming:
            copy.start()
        j, y, z, x = info_ref[0], info_ref[1], info_ref[2], info_ref[3]
        for p, (_, far, near) in enumerate(parts):
            coming[p].wait()
            for k, distance in enumerate(distances):
                for m in range(nx):
                    y_at, z_at, x_at = y ^ far, z ^ distance ^ near, x ^ m
                    if nz == 2 * tn:
                        block = (((z_at // tn) * ny + y_at) * nx + x_at) * tn + z_at % tn
                    else:
                        block = (y_at * nz + z_at) * nx + x_at
                    at = pl.ds(pl.multiple_of(block * size, size), size)
                    weight_ref[at, :] = near_ref[p, (k * nx + m) * size:(k * nx + m + 1) * size, :]
        total_ref[0:OFFMAX, :] = jnp.zeros((OFFMAX, vw), F32)
        for c in range(0, pack, 256):
            total_ref[OFFMAX + c:OFFMAX + c + 256, :] = jnp.dot(
                hidden_ref[c:c + 256, :], weight_ref[...], preferred_element_type=F32)
        for s in range(tn):
            at = pl.ds(pl.multiple_of((j ^ s) * rows, rows), rows + OFFMAX)
            value_refs[s][...] = total_ref[at, :].astype(value_refs[s].dtype)

    return pl.pallas_call(
        kernel,
        in_specs=[SMEM, VMEM] + [pl.BlockSpec(memory_space=pl.ANY)] * len(parts),
        out_specs=[VMEM] * tn,
        out_shape=[jax.ShapeDtypeStruct((rows + OFFMAX, vw), F32 if s == 0 else BF16) for s in range(tn)],
        scratch_shapes=[
            pltpu.VMEM((piece, vw), BF16),
            pltpu.VMEM((pack + OFFMAX, vw), F32),
            pltpu.VMEM((len(parts),) + parts[0][0].shape, BF16),
            pltpu.SemaphoreType.DMA((len(parts),)),
        ],
        compiler_params=pltpu.CompilerParams(vmem_limit_bytes=VMEM_LIMIT),
        cost_estimate=pl.CostEstimate(flops=2 * pack * piece * vw, bytes_accessed=4 * pack * piece, transcendentals=0),
        name="project",
    )(info, hidden, *[part for part, _, _ in parts])


def spread(info, parts):
    rows, vw = parts[0].shape[0] - OFFMAX, parts[0].shape[1]

    def kernel(info_ref, *refs):
        parts_refs, out_ref = refs[:-1], refs[-1]
        total = None
        for ref in parts_refs:
            part = ref[...].astype(F32)
            total = part if total is None else total + part
        total = total.astype(BF16)
        for s in range(STEPS):
            pick = chosen(info_ref, s, rows, OFFMAX)
            out_ref[s] = jnp.dot(pick, total, preferred_element_type=F32).astype(BF16)

    return pl.pallas_call(
        kernel,
        in_specs=[SMEM] + [VMEM] * len(parts),
        out_specs=VMEM,
        out_shape=jax.ShapeDtypeStruct((STEPS, rows, vw), BF16),
        compiler_params=pltpu.CompilerParams(vmem_limit_bytes=VMEM_LIMIT),
        cost_estimate=pl.CostEstimate(flops=2 * STEPS * rows * 160 * vw, bytes_accessed=8 * STEPS * rows * vw, transcendentals=0),
        name="spread",
    )(info, *parts)


def body(
    target_queries,
    target_keys,
    target_values,
    low_feature,
    mid_feature,
    merging_gain,
    draft_gain,
    draft_weight,
    cotangent,
    doc_lengths,
    step_offsets,
):
    n = lax.axis_size("dp")
    tn = lax.axis_size("tensor")
    j = lax.axis_index("tensor")
    i = lax.axis_index("dp")
    flat = i * tn + j
    nz, ny, nx = sides_of(n)
    lengths = doc_lengths.reshape(-1)
    count = LENGTHS + lengths.size
    info = jnp.pad(step_offsets, (OFFSETS, lengths.size)) + jnp.pad(lengths, (LENGTHS, 0))
    for at, value in enumerate((j, i // nx % ny, i // (ny * nx), i % nx)):
        info = jnp.where(lax.iota(jnp.int32, count) == at, value.astype(jnp.int32), info)
    width = low_feature.shape[1]
    piece = width // tn
    pack = target_queries.shape[0]
    both = ("dp", "tensor")

    def swapped(values, s):
        return lax.ppermute(values, "tensor", [(a, a ^ s) for a in range(tn)])

    folded = fold(info, cotangent)
    across = swapped(folded, 2)
    low_feature, folded = lax.optimization_barrier((low_feature, folded))
    sent = features(info, low_feature, mid_feature, merging_gain, tn)
    across, sent = lax.optimization_barrier((across, sent))
    parts = [sent[0]] + [swapped(sent[s], s) for s in range(1, tn)]

    high, squares = attend(info, target_queries, target_keys, target_values)
    own_weight, high, folded, across = lax.optimization_barrier((draft_weight, high, folded, across))
    squares = squares + swapped(squares, 1)
    folds = [folded, swapped(folded, 1), across, swapped(across, 1)]
    squares, folds, parts[1] = lax.optimization_barrier((squares, folds, parts[1]))
    squares = [squares, swapped(squares, 2)]
    weights = weight_to_place(own_weight)
    merged, squares = merge(info, merging_gain, high, parts, squares, width)
    weights, merged, squares = lax.optimization_barrier((weights, merged, squares))
    weights = jnp.concatenate(weights)
    far_weights = moved(weights, lambda z, y, x: (z ^ nz // 2, y, x)) if nz > 1 else weights
    squares = [squares] + [swapped(squares, s) for s in range(1, tn)]
    kept, cut, hidden = grads(info, draft_gain.reshape(1, width), merged, folds, squares, width, ny, tn)
    far_weights, cut = lax.optimization_barrier((far_weights, cut))
    weights, hidden = lax.optimization_barrier((weights, hidden))
    if nz > 1:
        weights = jnp.concatenate([weights, far_weights])
    weights = weight_halves(weight_across(weights, nz // 4))
    halves = reduce_once(kept, cut)
    weights, own = lax.optimization_barrier((weights, [half[0] for half in halves]))
    got = reduce_twice(halves)
    grad = [mine + part.astype(F32) for mine, part in zip(own, got)]
    if ny > 1:
        grad = [half.astype(BF16) for half in grad]
    grad = jnp.concatenate(grad)
    weights = weight_twice(weight_once(held(weights, grad)))
    grad = reduce_along_z(grad)
    hidden, grad = lax.optimization_barrier((hidden, grad))
    grad = parts_by_turn(grad)
    values = project(info, hidden, weights, tn, nz, ny, nx)
    values, grad[-1] = lax.optimization_barrier((values, grad[-1]))
    weight_grad = reduce_to_owner(grad)
    values = [values[0]] + [swapped(values[s], s) for s in range(1, tn)]
    draft_values = spread(info, values)

    rows = weight_grad.shape[0]
    gain = lax.dynamic_slice(draft_gain, (flat * rows,), (rows,))
    gain_grad = jnp.sum(weight_grad * draft_weight.astype(F32), axis=1) / gain
    return (draft_values, weight_grad, gain_grad)


def solution(mesh):
    placed = (
        P("dp", "tensor"),
        P("dp", "tensor"),
        P("dp", "tensor"),
        P(("dp", "tensor"), None),
        P(("dp", "tensor"), None),
        P(),
        P(),
        P(("dp", "tensor"), None),
        P(None, ("dp", "tensor"), None),
        P("dp", None),
        P(),
    )
    return jax.shard_map(
        body,
        mesh=mesh,
        in_specs=placed,
        out_specs=(P(None, ("dp", "tensor"), None), P(("dp", "tensor"), None), P(("dp", "tensor"))),
        check_vma=False,
    )
```

```python
import functools
import math

import jax
import jax.numpy as jnp
import numpy as np
from jax import lax
from jax.experimental import pallas as pl
from jax.experimental.pallas import tpu as pltpu
from jax.sharding import PartitionSpec as P

HD = 128
STEPS = 3
OFFMAX = 32
EPSILON = 1e-05
VMEM_LIMIT = 20 * 1024 * 1024
LARGE_LIMIT = 60 * 1024 * 1024

VMEM = pl.BlockSpec(memory_space=pltpu.VMEM)
SMEM = pl.BlockSpec(memory_space=pltpu.SMEM)
HBM = pl.BlockSpec(memory_space=pltpu.HBM)
F32 = jnp.float32
BF16 = jnp.bfloat16


SIDES = {64: (8, 4, 2)}


def sides_of(n):
    return SIDES.get(n, (1, 1, n))


def groups_along(n, *sides):
    sizes = sides_of(n)
    where = np.moveaxis(np.arange(n).reshape(sizes), sides, range(-len(sides), 0))
    return where.reshape(-1, math.prod(sizes[side] for side in sides)).tolist()


def block_order(n, tn):
    nz, ny, nx = sides_of(n)
    order = np.arange(n).reshape(ny, nz, nx)
    if nz == 2 * tn and n == ny * nx * tn * 2:
        for y in range(ny):
            for z in range(nz):
                for x in range(nx):
                    order[y, z, x] = (((z // tn) * ny + y) * nx + x) * tn + z % tn
    return order


def moved(values, change):
    n = lax.axis_size("dp")
    nz, ny, nx = sides_of(n)
    pairs = []
    for source in range(n):
        z, y, x = change(source // (ny * nx), source // nx % ny, source % nx)
        pairs.append((source, (z * ny + y) * nx + x))
    return lax.ppermute(values, "dp", pairs)


def weight_to_place(weight):
    n, tn = lax.axis_size("dp"), lax.axis_size("tensor")
    nz, ny, nx = sides_of(n)
    order = block_order(n, tn)
    parts = []
    for turn in range(nx):
        pairs = []
        for j in range(tn):
            for y, z, x in np.ndindex(ny, nz, nx):
                pairs.append((j * n + int(order[y, z, x ^ turn]), ((z * ny + y) * nx + x) * tn + j))
        parts.append(lax.ppermute(weight, ("dp", "tensor"), pairs))
    return parts


def weight_across(weight, far):
    if sides_of(lax.axis_size("dp"))[0] == 1:
        return weight
    return jnp.concatenate([weight, moved(weight, lambda z, y, x: (z ^ far, y, x))])


def weight_halves(weight):
    if sides_of(lax.axis_size("dp"))[0] == 1:
        return [weight]
    return [weight, moved(weight, lambda z, y, x: (z ^ 1, y, x))]


def weight_once(halves):
    if sides_of(lax.axis_size("dp"))[1] == 1:
        return [[half] for half in halves]
    return [[half, moved(half, lambda z, y, x: (z, y ^ first, x))] for half, (first, _) in zip(halves, EXCHANGES)]


def weight_twice(halves):
    if sides_of(lax.axis_size("dp"))[1] == 1:
        return halves
    return [
        half + [moved(part, lambda z, y, x: (z, y ^ second, x)) for part in half]
        for half, (_, second) in zip(halves, EXCHANGES)]


KEPT = ((0, 3), (0, 1))
SENT = ((1, 2), (3, 2))
EXCHANGES = ((1, 3), (3, 1))


def reduce_once(kept, sent):
    if sides_of(lax.axis_size("dp"))[1] == 1:
        return [(keep[0], None) for keep in kept]
    got = [moved(send, lambda z, y, x: (z, y ^ first, x)) for send, (first, _) in zip(sent, EXCHANGES)]
    got = lax.optimization_barrier(got)
    return [(keep[0] + part[0].astype(F32), (keep[1] + part[1].astype(F32)).astype(BF16)) for keep, part in zip(kept, got)]


def reduce_twice(halves):
    if sides_of(lax.axis_size("dp"))[1] == 1:
        return [jnp.zeros_like(own) for own, _ in halves]
    return [moved(other, lambda z, y, x: (z, y ^ second, x)) for (_, other), (_, second) in zip(halves, EXCHANGES)]


def reduce_along_z(grad):
    n = lax.axis_size("dp")
    nz = sides_of(n)[0]
    if nz == 1:
        return grad
    columns = grad.shape[-1]
    grad = lax.all_to_all(grad.astype(BF16), "dp", 0, 0, tiled=True, axis_index_groups=groups_along(n, 0))
    return jnp.sum(grad.reshape(nz, -1, columns).astype(F32), axis=0)


def reduce_to_owner(grad):
    n, tn = lax.axis_size("dp"), lax.axis_size("tensor")
    nz, ny, nx = sides_of(n)
    rows, columns = grad.shape[0] // nx, grad.shape[1]
    order = block_order(n, tn)
    x = lax.axis_index("dp") % nx
    total = None
    for turn in range(nx):
        pairs = []
        for z in range(nz):
            for y in range(ny):
                for x0 in range(nx):
                    for j in range(tn):
                        block = j * n + int(order[y, z, (x0 + turn) % nx])
                        pairs.append((((z * ny + y) * nx + x0) * tn + j, block))
        part = lax.dynamic_slice(grad, ((x + turn) % nx * rows, 0), (rows, columns))
        part = lax.ppermute(part, ("dp", "tensor"), pairs)
        total = part if total is None else total + part
    return total


def held(values, after):
    def kernel(*refs):
        pass

    return pl.pallas_call(
        kernel,
        in_specs=[pl.BlockSpec(memory_space=pl.ANY)] * (len(values) + 1),
        out_specs=[pl.BlockSpec(memory_space=pl.ANY)] * len(values),
        out_shape=[jax.ShapeDtypeStruct(value.shape, value.dtype) for value in values],
        input_output_aliases={k: k for k in range(len(values))},
        cost_estimate=pl.CostEstimate(flops=0, bytes_accessed=0, transcendentals=0),
        name="held",
    )(*values, after)


OFFSETS = 4
LENGTHS = OFFSETS + STEPS


def segment_start(places, info_ref):
    end = jnp.int32(0)
    start = jnp.zeros_like(places)
    for s in range(LENGTHS, info_ref.shape[0]):
        end = end + info_ref[s]
        start = jnp.where(places >= end, end, start)
    return start


def column(row):
    n = row.shape[-1]
    eye = lax.broadcasted_iota(jnp.int32, (n, n), 0) == lax.broadcasted_iota(jnp.int32, (n, n), 1)
    return jnp.sum(jnp.where(eye, row, 0.0), axis=1, keepdims=True)


def lane_sums(values):
    return lax.dot_general(
        jnp.ones((8, values.shape[1]), F32), values, (((1,), (1,)), ((), ())),
        precision=lax.Precision.HIGHEST, preferred_element_type=F32)


def folded_square_sum(values):
    total = None
    for c in range(0, values.shape[1], 128):
        piece = values[:, c:c + 128]
        total = piece * piece if total is None else total + piece * piece
    return total


def features_kernel(tn, info_ref, low_ref, mid_ref, gain_ref, *outs):
    j = info_ref[0]
    width = low_ref.shape[1]
    piece = width // tn
    step = 1024

    def rms_scale(ref):
        total = None
        for c in range(0, width, step):
            part = folded_square_sum(ref[:, c:c + step].astype(F32))
            total = part if total is None else total + part
        return lax.rsqrt(jnp.sum(total, axis=1, keepdims=True) / width + EPSILON)

    low_scale = rms_scale(low_ref)
    mid_scale = rms_scale(mid_ref)
    for s, out in enumerate(outs):
        first = pl.multiple_of((j ^ s) * piece, piece)
        for c in range(0, piece, 512):
            at = pl.ds(first + c, 512)
            value = (low_ref[:, at].astype(F32) * low_scale * gain_ref[0:1, at]
                     + mid_ref[:, at].astype(F32) * mid_scale * gain_ref[1:2, at])
            out[:, c:c + 512] = value.astype(BF16)


def features(info, low, mid, gain, tn):
    rows, width = low.shape
    block = 32
    piece = width // tn
    return pl.pallas_call(
        functools.partial(features_kernel, tn),
        grid=(rows // block,),
        in_specs=[
            SMEM,
            pl.BlockSpec((block, width), lambda b: (b, 0)),
            pl.BlockSpec((block, width), lambda b: (b, 0)),
            pl.BlockSpec(gain.shape, lambda b: (0, 0)),
        ],
        out_specs=[pl.BlockSpec((block, piece), lambda b: (b, 0))] * tn,
        out_shape=[jax.ShapeDtypeStruct((rows, piece), BF16)] * tn,
        compiler_params=pltpu.CompilerParams(vmem_limit_bytes=LARGE_LIMIT),
        cost_estimate=pl.CostEstimate(flops=10 * rows * width, bytes_accessed=6 * rows * width, transcendentals=0),
        name="features",
    )(info, low, mid, gain)


def attend_kernel(window, info_ref, query_ref, key_ref, value_ref, high_ref, square_ref):
    block = query_ref.shape[0]
    pack = key_ref.shape[0]
    b = pl.program_id(0)
    first = pl.multiple_of(jnp.clip(b * block - (window - block), 0, pack - window), block)
    query_places = b * block + lax.broadcasted_iota(jnp.int32, (block, window), 0)
    key_places = first + lax.broadcasted_iota(jnp.int32, (block, window), 1)
    allowed = (key_places <= query_places) & (key_places >= segment_start(query_places, info_ref))
    bias = jnp.where(allowed, 0.0, -1e30).astype(F32)
    group = (query_ref.shape[1] // HD) // (key_ref.shape[1] // HD)
    squares = jnp.zeros((block, HD), F32)
    ones = jnp.ones((window, HD), BF16)
    scale = math.log2(math.e) / math.sqrt(HD)
    for g in range(key_ref.shape[1] // HD):
        key = key_ref[pl.ds(first, window), g * HD:(g + 1) * HD]
        value = jnp.concatenate([value_ref[pl.ds(first, window), g * HD:(g + 1) * HD], ones], axis=1)
        for r in range(group):
            at = slice((g * group + r) * HD, (g * group + r + 1) * HD)
            scores = lax.dot_general(query_ref[:, at], key, (((1,), (1,)), ((), ())), preferred_element_type=F32)
            scores = scores * scale + bias
            highest = jnp.max(scores, axis=1, keepdims=True)
            expo = jnp.exp2(scores - highest).astype(BF16)
            mixed = jnp.dot(expo, value, preferred_element_type=F32)
            out = (mixed[:, :HD] / mixed[:, HD:]).astype(BF16)
            high_ref[:, at] = out
            out = out.astype(F32)
            squares = squares + out * out
    square_ref[...] = lane_sums(squares)


def attend(info, queries, keys, values):
    pack, width = queries.shape
    block = 128
    window = min(pack, 256 + block)
    return pl.pallas_call(
        functools.partial(attend_kernel, window),
        grid=(pack // block,),
        in_specs=[
            SMEM,
            pl.BlockSpec((block, width), lambda b: (b, 0)),
            pl.BlockSpec(keys.shape, lambda b: (0, 0)),
            pl.BlockSpec(values.shape, lambda b: (0, 0)),
        ],
        out_specs=[
            pl.BlockSpec((block, width), lambda b: (b, 0)),
            pl.BlockSpec((8, block), lambda b: (0, b)),
        ],
        out_shape=[
            jax.ShapeDtypeStruct((pack, width), BF16),
            jax.ShapeDtypeStruct((8, pack), F32),
        ],
        compiler_params=pltpu.CompilerParams(vmem_limit_bytes=VMEM_LIMIT),
        cost_estimate=pl.CostEstimate(
            flops=4 * pack * window * width, bytes_accessed=4 * pack * width,
            transcendentals=pack * window * width // HD),
        name="attend",
    )(info, queries, keys, values)


def chosen(info_ref, step, rows, lead):
    target = info_ref[0] * rows + lax.broadcasted_iota(jnp.int32, (rows, rows + lead), 0)
    source = info_ref[0] * rows - lead + lax.broadcasted_iota(jnp.int32, (rows, rows + lead), 1)
    hit = (source == target - info_ref[OFFSETS + step]) & (source >= segment_start(target, info_ref))
    return jnp.where(hit, 1.0, 0.0).astype(BF16)


def fold_kernel(info_ref, cotangent_ref, out_ref, near_ref, sems):
    steps, rows, width = cotangent_ref.shape
    coming = [pltpu.make_async_copy(cotangent_ref.at[s], near_ref.at[s], sems.at[s]) for s in range(steps)]
    for copy in coming:
        copy.start()
    total = None
    for s in range(steps):
        pick = chosen(info_ref, s, rows, OFFMAX)
        coming[s].wait()
        part = lax.dot_general(pick, near_ref[s], (((0,), (0,)), ((), ())), preferred_element_type=F32)
        total = part if total is None else total + part
    out_ref[...] = total.astype(BF16)


def fold(info, cotangent):
    steps, rows, width = cotangent.shape
    return pl.pallas_call(
        fold_kernel,
        in_specs=[SMEM, HBM],
        out_specs=VMEM,
        out_shape=jax.ShapeDtypeStruct((rows + OFFMAX, width), BF16),
        scratch_shapes=[pltpu.VMEM(cotangent.shape, BF16), pltpu.SemaphoreType.DMA((steps,))],
        compiler_params=pltpu.CompilerParams(vmem_limit_bytes=LARGE_LIMIT),
        cost_estimate=pl.CostEstimate(flops=2 * steps * rows * 160 * width, bytes_accessed=2 * steps * rows * width, transcendentals=0),
        name="fold",
    )(info, cotangent)


def merge_kernel(width, tn, info_ref, gain_ref, high_ref, *refs):
    parts, square_refs, (far_ref, out_square_ref, out_ref, sems) = refs[:tn], refs[tn:-4], refs[-4:]
    copies = []
    j = info_ref[0]
    rows = parts[0].shape[0]
    piece = high_ref.shape[1]
    squares = square_refs[0][...]
    for ref in square_refs[1:]:
        squares = squares + ref[...]
    scales = lax.rsqrt(squares / width + EPSILON)
    for b in range(tn):
        out_square_ref[:, b * rows:(b + 1) * rows] = scales[:, b * rows:(b + 1) * rows]
    for s in range(tn):
        first = pl.multiple_of((j ^ s) * rows, rows)
        at = pl.ds(first, rows)
        scale = column(out_square_ref[0:1, at])
        total = jnp.zeros((rows, 128), F32)
        for c in range(0, piece, 128):
            cols = slice(c, c + 128)
            gain = gain_ref[2:3, pl.ds(pl.multiple_of(j * piece + c, 128), 128)]
            merged = (parts[s][:, cols].astype(F32) + high_ref[at, cols].astype(F32) * scale * gain).astype(BF16)
            out_ref[at, cols] = merged
            merged = merged.astype(F32)
            total = total + merged * merged
        copy = pltpu.make_async_copy(out_ref.at[at, :], far_ref.at[at, :], sems.at[s])
        copy.start()
        copies.append(copy)
        out_square_ref[:, at] = lane_sums(total)
    for copy in copies:
        copy.wait()


def merge(info, gain, high, parts, squares, width):
    pack, piece = high.shape
    tn = len(parts)
    return pl.pallas_call(
        functools.partial(merge_kernel, width, tn),
        in_specs=[SMEM] + [VMEM] * (2 + tn + len(squares)),
        out_specs=[HBM, VMEM],
        out_shape=[
            jax.ShapeDtypeStruct((pack, piece), BF16),
            jax.ShapeDtypeStruct((8, pack), F32),
        ],
        scratch_shapes=[pltpu.VMEM((pack, piece), BF16), pltpu.SemaphoreType.DMA((tn,))],
        compiler_params=pltpu.CompilerParams(vmem_limit_bytes=VMEM_LIMIT),
        cost_estimate=pl.CostEstimate(flops=8 * pack * piece, bytes_accessed=6 * pack * piece, transcendentals=0),
        name="merge",
    )(info, gain, high, *parts, *squares)


def grads(info, gain, merged, folds, squares, width, ny, tn):
    pack, piece = merged.shape
    rows = pack // tn
    vw = folds[0].shape[1]
    chunk = piece // (2 * ny)
    kept, sent = (KEPT, SENT) if ny > 1 else (((0,), (0,)), ((), ()))
    steps = [(h, s, True) for h in range(2) for s in kept[h]] + [(h, s, False) for h in range(2) for s in sent[h]]
    steps.sort(key=lambda step: step[2])
    size = chunk // (2 * tn) if ny > 1 else chunk

    def kernel(info_ref, gain_ref, merged_ref, *refs):
        fold_refs, square_refs, refs = refs[:tn], refs[tn:2 * tn], refs[2 * tn:]
        keep_refs, refs = refs[:2], refs[2:]
        send_refs, refs = refs[:2 if ny > 1 else 0], refs[2 if ny > 1 else 0:]
        hidden_ref, fold_ref, near_ref, near_folds, near_cut, sems = refs
        coming = [
            pltpu.make_async_copy(
                merged_ref.at[b * rows:(b + 1) * rows, :], near_ref.at[b * rows:(b + 1) * rows, :], sems.at[b])
            for b in range(tn)]
        folds_coming = [
            pltpu.make_async_copy(fold_refs[s], near_folds.at[s], sems.at[tn + s]) for s in range(tn)]
        for copy in coming + folds_coming:
            copy.start()
        j, y = info_ref[0], info_ref[1]
        squares = square_refs[0][...]
        for s in range(1, tn):
            squares = squares + square_refs[s][...]
        scales = lax.rsqrt(squares / width + EPSILON)
        for b in range(tn):
            at = slice(b * rows, (b + 1) * rows)
            scale = column(scales[0:1, at])
            coming[b].wait()
            for c in range(0, piece, 128):
                cols = slice(c, c + 128)
                gain = gain_ref[:, pl.ds(pl.multiple_of(j * piece + c, 128), 128)]
                hidden_ref[at, cols] = (near_ref[at, cols].astype(F32) * scale * gain).astype(BF16)
        fold_ref[...] = jnp.zeros_like(fold_ref)
        for s in range(tn):
            at = pl.ds(pl.multiple_of((j ^ s) * rows, rows), rows + OFFMAX)
            folds_coming[s].wait()
            fold_ref[at, :] = fold_ref[at, :] + near_folds[s].astype(F32)
        folded = fold_ref[OFFMAX:, :].astype(BF16)
        going = []
        for h, s, keep in steps:
            at = pl.ds(pl.multiple_of(h * ny * chunk + (y ^ s) * chunk, chunk), chunk)
            part = lax.dot_general(
                hidden_ref[:, at], folded, (((0,), (0,)), ((), ())), preferred_element_type=F32)
            if size < chunk:
                part = jnp.concatenate(
                    [part[(x * tn + t) * size:(x * tn + t + 1) * size] for t in range(tn) for x in range(2)], axis=0)
            if keep:
                keep_refs[h][kept[h].index(s)] = part
            else:
                k = sent[h].index(s)
                near_cut[h, k] = part.astype(BF16)
                copy = pltpu.make_async_copy(near_cut.at[h, k], send_refs[h].at[k], sems.at[2 * tn + 2 * h + k])
                copy.start()
                going.append(copy)
        for copy in going:
            copy.wait()

    out_shape = [jax.ShapeDtypeStruct((len(kept[h]), chunk, vw), F32) for h in range(2)]
    if ny > 1:
        out_shape += [jax.ShapeDtypeStruct((len(sent[h]), chunk, vw), BF16) for h in range(2)]
    out_shape += [jax.ShapeDtypeStruct((pack, piece), BF16)]
    out = pl.pallas_call(
        kernel,
        in_specs=[SMEM, VMEM, HBM] + [HBM] * tn + [VMEM] * tn,
        out_specs=[VMEM] * 2 + ([HBM] * 2 if ny > 1 else []) + [VMEM],
        out_shape=out_shape,
        scratch_shapes=[
            pltpu.VMEM((pack + OFFMAX, vw), F32),
            pltpu.VMEM((pack, piece), BF16),
            pltpu.VMEM((tn, rows + OFFMAX, vw), BF16),
            pltpu.VMEM((2, 2, chunk if ny > 1 else 16, vw), BF16),
            pltpu.SemaphoreType.DMA((2 * tn + 4,)),
        ],
        compiler_params=pltpu.CompilerParams(vmem_limit_bytes=VMEM_LIMIT),
        cost_estimate=pl.CostEstimate(flops=2 * pack * piece * vw, bytes_accessed=8 * pack * piece, transcendentals=0),
        name="grads",
    )(info, gain, merged, *folds, *squares)
    return out[:2], out[2:-1] if ny > 1 else (None, None), out[-1]


def project(info, hidden, weights, tn, nz, ny, nx):
    pack, piece = hidden.shape
    rows = pack // tn
    vw = weights[0][0].shape[1]
    parts = [
        (part, far, near)
        for half, near, (first, second) in zip(weights, (0, 1), EXCHANGES)
        for part, far in zip(half, (0, first, second, first ^ second))]
    distances = (0, 4, 2, 6) if nz > 1 else (0,)
    size = parts[0][0].shape[0] // (len(distances) * nx)

    def kernel(info_ref, hidden_ref, *refs):
        weight_refs, value_refs = refs[:len(parts)], refs[len(parts):-4]
        weight_ref, total_ref, near_ref, sems = refs[-4:]
        coming = [pltpu.make_async_copy(ref, near_ref.at[p], sems.at[p]) for p, ref in enumerate(weight_refs)]
        for copy in coming:
            copy.start()
        j, y, z, x = info_ref[0], info_ref[1], info_ref[2], info_ref[3]
        for p, (_, far, near) in enumerate(parts):
            coming[p].wait()
            for k, distance in enumerate(distances):
                for m in range(nx):
                    y_at, z_at, x_at = y ^ far, z ^ distance ^ near, x ^ m
                    if nz == 2 * tn:
                        block = (((z_at // tn) * ny + y_at) * nx + x_at) * tn + z_at % tn
                    else:
                        block = (y_at * nz + z_at) * nx + x_at
                    at = pl.ds(pl.multiple_of(block * size, size), size)
                    weight_ref[at, :] = near_ref[p, (k * nx + m) * size:(k * nx + m + 1) * size, :]
        total_ref[0:OFFMAX, :] = jnp.zeros((OFFMAX, vw), F32)
        for c in range(0, pack, 256):
            total_ref[OFFMAX + c:OFFMAX + c + 256, :] = jnp.dot(
                hidden_ref[c:c + 256, :], weight_ref[...], preferred_element_type=F32)
        for s in range(tn):
            at = pl.ds(pl.multiple_of((j ^ s) * rows, rows), rows + OFFMAX)
            value_refs[s][...] = total_ref[at, :].astype(value_refs[s].dtype)

    return pl.pallas_call(
        kernel,
        in_specs=[SMEM, VMEM] + [pl.BlockSpec(memory_space=pl.ANY)] * len(parts),
        out_specs=[VMEM] * tn,
        out_shape=[jax.ShapeDtypeStruct((rows + OFFMAX, vw), F32 if s == 0 else BF16) for s in range(tn)],
        scratch_shapes=[
            pltpu.VMEM((piece, vw), BF16),
            pltpu.VMEM((pack + OFFMAX, vw), F32),
            pltpu.VMEM((len(parts),) + parts[0][0].shape, BF16),
            pltpu.SemaphoreType.DMA((len(parts),)),
        ],
        compiler_params=pltpu.CompilerParams(vmem_limit_bytes=VMEM_LIMIT),
        cost_estimate=pl.CostEstimate(flops=2 * pack * piece * vw, bytes_accessed=4 * pack * piece, transcendentals=0),
        name="project",
    )(info, hidden, *[part for part, _, _ in parts])


def spread(info, parts):
    rows, vw = parts[0].shape[0] - OFFMAX, parts[0].shape[1]

    def kernel(info_ref, *refs):
        parts_refs, out_ref = refs[:-1], refs[-1]
        total = None
        for ref in parts_refs:
            part = ref[...].astype(F32)
            total = part if total is None else total + part
        total = total.astype(BF16)
        for s in range(STEPS):
            pick = chosen(info_ref, s, rows, OFFMAX)
            out_ref[s] = jnp.dot(pick, total, preferred_element_type=F32).astype(BF16)

    return pl.pallas_call(
        kernel,
        in_specs=[SMEM] + [VMEM] * len(parts),
        out_specs=VMEM,
        out_shape=jax.ShapeDtypeStruct((STEPS, rows, vw), BF16),
        compiler_params=pltpu.CompilerParams(vmem_limit_bytes=VMEM_LIMIT),
        cost_estimate=pl.CostEstimate(flops=2 * STEPS * rows * 160 * vw, bytes_accessed=8 * STEPS * rows * vw, transcendentals=0),
        name="spread",
    )(info, *parts)


def body(
    target_queries,
    target_keys,
    target_values,
    low_feature,
    mid_feature,
    merging_gain,
    draft_gain,
    draft_weight,
    cotangent,
    doc_lengths,
    step_offsets,
):
    n = lax.axis_size("dp")
    tn = lax.axis_size("tensor")
    j = lax.axis_index("tensor")
    i = lax.axis_index("dp")
    flat = i * tn + j
    nz, ny, nx = sides_of(n)
    lengths = doc_lengths.reshape(-1)
    count = LENGTHS + lengths.size
    info = jnp.pad(step_offsets, (OFFSETS, lengths.size)) + jnp.pad(lengths, (LENGTHS, 0))
    for at, value in enumerate((j, i // nx % ny, i // (ny * nx), i % nx)):
        info = jnp.where(lax.iota(jnp.int32, count) == at, value.astype(jnp.int32), info)
    width = low_feature.shape[1]
    piece = width // tn
    pack = target_queries.shape[0]
    both = ("dp", "tensor")

    def swapped(values, s):
        return lax.ppermute(values, "tensor", [(a, a ^ s) for a in range(tn)])

    folded = fold(info, cotangent)
    across = swapped(folded, 2)
    low_feature, folded = lax.optimization_barrier((low_feature, folded))
    sent = features(info, low_feature, mid_feature, merging_gain, tn)
    across, sent = lax.optimization_barrier((across, sent))
    parts = [sent[0]] + [swapped(sent[s], s) for s in range(1, tn)]

    high, squares = attend(info, target_queries, target_keys, target_values)
    own_weight, high, folded, across = lax.optimization_barrier((draft_weight, high, folded, across))
    squares = squares + swapped(squares, 1)
    folds = [folded, swapped(folded, 1), across, swapped(across, 1)]
    squares, folds, parts[1] = lax.optimization_barrier((squares, folds, parts[1]))
    squares = [squares, swapped(squares, 2)]
    weights = weight_to_place(own_weight)
    merged, squares = merge(info, merging_gain, high, parts, squares, width)
    weights, merged, squares = lax.optimization_barrier((weights, merged, squares))
    weights = jnp.concatenate(weights)
    far_weights = moved(weights, lambda z, y, x: (z ^ nz // 2, y, x)) if nz > 1 else weights
    squares = [squares] + [swapped(squares, s) for s in range(1, tn)]
    kept, cut, hidden = grads(info, draft_gain.reshape(1, width), merged, folds, squares, width, ny, tn)
    far_weights, cut = lax.optimization_barrier((far_weights, cut))
    weights, hidden = lax.optimization_barrier((weights, hidden))
    if nz > 1:
        weights = jnp.concatenate([weights, far_weights])
    weights = weight_halves(weight_across(weights, nz // 4))
    halves = reduce_once(kept, cut)
    weights, own = lax.optimization_barrier((weights, [half[0] for half in halves]))
    got = reduce_twice(halves)
    grad = [mine + part.astype(F32) for mine, part in zip(own, got)]
    if ny > 1:
        grad = [half.astype(BF16) for half in grad]
    grad = jnp.concatenate(grad)
    weights = weight_twice(weight_once(held(weights, grad)))
    grad = reduce_along_z(grad)
    weight_grad = reduce_to_owner(grad)
    values = project(info, hidden, weights, tn, nz, ny, nx)
    values = [values[0]] + [swapped(values[s], s) for s in range(1, tn)]
    draft_values = spread(info, values)

    rows = weight_grad.shape[0]
    gain = lax.dynamic_slice(draft_gain, (flat * rows,), (rows,))
    gain_grad = jnp.sum(weight_grad * draft_weight.astype(F32), axis=1) / gain
    return (draft_values, weight_grad, gain_grad)


def solution(mesh):
    placed = (
        P("dp", "tensor"),
        P("dp", "tensor"),
        P("dp", "tensor"),
        P(("dp", "tensor"), None),
        P(("dp", "tensor"), None),
        P(),
        P(),
        P(("dp", "tensor"), None),
        P(None, ("dp", "tensor"), None),
        P("dp", None),
        P(),
    )
    return jax.shard_map(
        body,
        mesh=mesh,
        in_specs=placed,
        out_specs=(P(None, ("dp", "tensor"), None), P(("dp", "tensor"), None), P(("dp", "tensor"))),
        check_vma=False,
    )
```
